32 devices in a mesh: tp: 4 (over z), ep: 8 (over y, x, core).
Axes of the slice: x: 2, y: 2, z: 4, core: 2. Of those that a mesh axis runs over, the one named last changes fastest.
Arguments:
- hidden_in: bfloat16 [4096, 3584], P(('ep', 'tp')), may hold values from -6 to 6
- cotangent: bfloat16 [4096, 3584], P(('ep', 'tp')), may hold values from -8 to 8
- routes: int32 [4096, 2], P(('ep', 'tp')), may hold values from 0 to 63, all different within a row; in each aligned block of 128 rows (0 to 127, 128 to 255, ...) at most 4 rows name the same one
- gate_values: float32 [4096, 2], P(('ep', 'tp')), may hold values from 0.25 to 1
- dense_gate: bfloat16 [2432, 3584], P('tp'), may hold values from -0.09375 to 0.09375
- dense_up: bfloat16 [2432, 3584], P('tp'), may hold values from -0.09375 to 0.09375
- dense_down: bfloat16 [2432, 3584], P('tp', 'ep'), may hold values from -0.125 to 0.125
- expert_gate: bfloat16 [4, 4864, 3584], P('tp', 'ep'), may hold values from -0.09375 to 0.09375
- expert_up: bfloat16 [4, 4864, 3584], P('tp', 'ep'), may hold values from -0.09375 to 0.09375
- expert_down: bfloat16 [4, 4864, 3584], P('tp', 'ep'), may hold values from -0.078125 to 0.078125
Outputs:
- grad_input: bfloat16 [4096, 3584], P(('ep', 'tp'))
- grad_dense_gate: bfloat16 [2432, 3584], P('tp', 'ep')
- grad_dense_up: bfloat16 [2432, 3584], P('tp', 'ep')
- grad_dense_down: bfloat16 [2432, 3584], P('tp', 'ep')
- grad_expert_gate: bfloat16 [4, 4864, 3584], P('tp', 'ep')
- grad_expert_up: bfloat16 [4, 4864, 3584], P('tp', 'ep')
- grad_expert_down: bfloat16 [4, 4864, 3584], P('tp', 'ep')
The draws below stay inside these ranges and needn't reach their ends.
Inputs may be any that keep to these rules, and one draw needn't show every extreme that they name: `routes`: the two experts of a token differ. Among the tokens of one aligned block of 128 rows no expert is named more than 4 times, a bound that some block reaches; every expert is named somewhere.
All inputs are finite; a program needn't handle non-finite values.
Results may differ from the reference program's by a relative error of at most 0.012.
Values may be sent and summed in bfloat16 or wider, within the bound.
No kernel may reach another device: no remote copies, remote signals or barrier semaphores. Data moves between devices by JAX's collectives and lax.ppermute only.
A program may use at most 192 MiB of HBM per device.

```python
import math
from functools import partial
import jax
import jax.numpy as jnp
import numpy as np
from jax import lax

D = 3584
DFF = 2432
EXP_H = 4864
TOK_DEV = 128
CAP = 4
E_WIN = 4
E_ALL = 64
TOKENS = 4096
GROUP = 512
DFF_BLOCK = 608
EXP_BLOCK = 608
N_TP = 4
N_EP = 8


def strengthened(values, rng, source, target, parts, factor):
    owner, partner = [(jnp.arange(values.shape[dim]) // (values.shape[dim] // parts)).reshape([-1 if axis == dim else 1 for axis in range(values.ndim)]) for dim in (source, target)]
    chosen = jax.random.permutation(rng, parts)[partner]
    strong = (owner == chosen) | (owner == (partner + parts // 2) % parts)
    return jnp.where(strong, factor * values, values)


def level_of(key, shape, cuts, smallest, largest):
    gain = 1.0
    for dim, parts in cuts:
        steps = jax.random.uniform(jax.random.fold_in(jax.random.fold_in(key, 6), dim), (parts,), jnp.float32, smallest / len(cuts), largest / len(cuts))
        gain = gain * jnp.repeat(jnp.exp(steps), shape[dim] // parts).reshape((-1,) + (1,) * (len(shape) - 1 - dim))
    return gain


def shared_out(rng, own, number, rows, number_of, top, bound, lean):
    ranking = jax.random.permutation(rng, number_of)
    crowded, ordinary = portions_of(number_of, rows * top, bound, lean, True), portions_of(number_of, rows * top, bound, lean, False)
    places = jnp.arange(number_of)

    def named(sizes, offset_by):
        used = int((sizes > 0).sum())
        fixed = max(1, used // 4)
        shifted = fixed + (places - fixed + offset_by * (used - fixed)) % max(1, number_of - fixed)
        return jnp.zeros((number_of,), jnp.int32).at[ranking[jnp.where(places < fixed, places, shifted)]].set(jnp.asarray(sizes, jnp.int32))

    sizes = jnp.where(number % 4 == 0, named(crowded, number // 4), named(ordinary, number - number // 4 - 1))
    mixed = jax.random.permutation(jax.random.fold_in(own, 3), number_of)
    giver, receiver = mixed[0:number_of // 2 * 2:2], mixed[1:number_of // 2 * 2:2]
    slack = jnp.minimum(sizes[giver] - 1, bound - sizes[receiver]) // 2
    slack = jnp.where((giver == ranking[0]) | (receiver == ranking[0]) | (sizes[receiver] == 0), 0, jnp.maximum(slack, 0))
    shifted = jax.random.randint(jax.random.fold_in(own, 4), (number_of // 2,), 0, 1 << 20) % (slack + 1)
    sizes = sizes.at[giver].add(-shifted).at[receiver].add(shifted)
    items = jnp.searchsorted(jnp.cumsum(sizes), jnp.arange(rows * top), side="right").astype(jnp.int32)
    listing = items.reshape(top, rows).T
    listing = listing[jax.random.permutation(jax.random.fold_in(own, 1), rows)]
    offset_by = jax.random.randint(jax.random.fold_in(own, 2), (rows, 1), 0, top)
    return jnp.take_along_axis(listing, (jnp.arange(top)[None, :] + offset_by) % top, axis=1)


def portions_of(count, total, reach, skew, full):
    portions = [(1 << 20) // math.isqrt(standing ** skew) + 1 for standing in range(1, count + 1)]
    largest = reach if full else min(reach, max(-(-total // count), total * portions[0] // sum(portions)))
    least = 1 if total - largest >= count - 1 else 0
    given, surplus = [largest] + [least] * (count - 1), total - largest - least * (count - 1)
    while surplus > 0:
        free = [i for i in range(1, count) if given[i] < largest] or [i for i in range(1, count) if given[i] < reach]
        pool, left = sum([portions[i] for i in free]), surplus
        for i in free:
            extra = min(reach - given[i], max(1, left * portions[i] // pool), surplus)
            given[i] = given[i] + extra
            surplus = surplus - extra
    return np.array(given)


def noise(key, extent, deviation, most, pieces=(), kind=jnp.bfloat16):
    array = deviation * jax.random.normal(key, extent, jnp.float32)
    if pieces:
        array = array * level_of(key, extent, pieces, -0.22, 0.18)
    return jnp.clip(array, -most, most).astype(kind)


def gaussian_with(own_key, shape, deviation, limit, split, heavy, kind=jnp.bfloat16):
    array = deviation * jax.random.normal(own_key, shape, jnp.float32)
    if split:
        array = array * level_of(own_key, shape, split, -0.22, 0.18)
    return jnp.clip(strengthened(array, jax.random.fold_in(own_key, 3), *heavy), -limit, limit).astype(kind)


def setup_inputs(seed: int = 0) -> dict:
    key_of = jax.random.split(jax.random.key(seed), 11)
    hidden_in = noise(key_of[0], (TOKENS, D), 1.0, 6.0, ((0, 32),))
    cotangent = gaussian_with(key_of[1], (TOKENS, D), 1.0, 8.0, ((0, 32),), (0, 1, 32, 2.75))
    routes_keys = jax.random.split(jax.random.fold_in(key_of[2], 1), TOKENS // TOK_DEV)
    routes_turns = jax.random.permutation(jax.random.fold_in(key_of[2], 3), TOKENS // TOK_DEV)
    routes = jax.vmap(lambda own, number: shared_out(jax.random.fold_in(key_of[2], 2), own, number, TOK_DEV, E_ALL, 2, CAP, 2))(routes_keys, routes_turns).reshape((TOKENS, 2))
    gate_values = jnp.clip(0.25 + 0.75 * jax.random.uniform(key_of[3], (TOKENS, 2), jnp.float32) ** level_of(key_of[3], (TOKENS, 2), ((0, 32),), -0.2, 0.2), 0.25, 1.0)
    dense_gate = noise(key_of[4], (DFF, D), D ** -0.5, 0.09375, ((0, 4),))
    dense_up = noise(key_of[5], (DFF, D), D ** -0.5, 0.09375, ((0, 4),))
    dense_down = noise(key_of[6], (DFF, D), DFF ** -0.5, 0.125, ((0, 4), (1, 8)))
    expert_gate = noise(key_of[7], (E_WIN, EXP_H, D), D ** -0.5, 0.09375, ((0, 4), (1, 8)))
    expert_up = noise(key_of[8], (E_WIN, EXP_H, D), D ** -0.5, 0.09375, ((0, 4), (1, 8)))
    expert_down = noise(key_of[9], (E_WIN, EXP_H, D), EXP_H ** -0.5, 0.078125, ((0, 4), (1, 8)))
    return {"hidden_in": hidden_in, "cotangent": cotangent, "routes": routes, "gate_values": gate_values, "dense_gate": dense_gate, "dense_up": dense_up, "dense_down": dense_down, "expert_gate": expert_gate, "expert_up": expert_up, "expert_down": expert_down}


def swiglu_backward(gate_pre, up_pre, grad_act):
    sigmoid_gate = jax.nn.sigmoid(gate_pre)
    silu_gate = gate_pre * sigmoid_gate
    act = (silu_gate * up_pre).astype(jnp.bfloat16)
    silu_slope = sigmoid_gate * (1.0 + gate_pre * (1.0 - sigmoid_gate))
    grad_gate = (grad_act * up_pre * silu_slope).astype(jnp.bfloat16)
    grad_up = (grad_act * silu_gate).astype(jnp.bfloat16)
    return act, grad_gate, grad_up


def slot_tables(route_block, gate_block, experts, capacity):
    tok_count = route_block.shape[0]
    flat_routes = route_block.reshape(-1).astype(jnp.int32)
    onehot = (flat_routes[:, None] == jnp.arange(experts, dtype=jnp.int32)[None, :]).astype(jnp.int32)
    before = jnp.cumsum(onehot, axis=0) - onehot
    position = jnp.sum(before * onehot, axis=1)
    slot_index = flat_routes * capacity + position
    slot_table = (slot_index[:, None] == jnp.arange(experts * capacity, dtype=jnp.int32)[None, :]).astype(jnp.float32)
    route_token = jnp.arange(2 * tok_count, dtype=jnp.int32) // 2
    holder = (route_token[:, None] == jnp.arange(tok_count, dtype=jnp.int32)[None, :]).astype(jnp.float32)
    dispatch = jnp.dot(slot_table.T, holder, precision=lax.Precision.HIGHEST)
    weighted = jnp.dot((slot_table * gate_block.reshape(-1)[:, None]).T, holder, precision=lax.Precision.HIGHEST)
    return dispatch, weighted


def reference(hidden_in, cotangent, routes, gate_values, dense_gate, dense_up, dense_down, expert_gate, expert_up, expert_down):
    contract = (((1,), (1,)), ((), ()))
    leading = (((0,), (0,)), ((), ()))
    gate_pre = lax.dot_general(hidden_in, dense_gate, contract, preferred_element_type=jnp.float32)
    up_pre = lax.dot_general(hidden_in, dense_up, contract, preferred_element_type=jnp.float32)
    grad_act = lax.dot_general(cotangent, dense_down, contract, preferred_element_type=jnp.float32)
    act, grad_gate_pre, grad_up_pre = swiglu_backward(gate_pre, up_pre, grad_act)

    unit_blocks = (grad_gate_pre.reshape(TOKENS, N_TP, DFF_BLOCK).transpose(1, 0, 2),
                   grad_up_pre.reshape(TOKENS, N_TP, DFF_BLOCK).transpose(1, 0, 2),
                   dense_gate.reshape(N_TP, DFF_BLOCK, D),
                   dense_up.reshape(N_TP, DFF_BLOCK, D))

    def add_units(total, block):
        gg, gu, wg, wu = block
        term = jnp.dot(gg, wg, preferred_element_type=jnp.float32) + jnp.dot(gu, wu, preferred_element_type=jnp.float32)
        rounded = lax.optimization_barrier(term.astype(jnp.bfloat16))
        return total + rounded.astype(jnp.float32), None

    dense_input, _ = lax.scan(add_units, jnp.zeros((TOKENS, D), jnp.float32), unit_blocks)

    groups = TOKENS // GROUP
    blocks = (act.reshape(groups, GROUP, DFF), grad_gate_pre.reshape(groups, GROUP, DFF), grad_up_pre.reshape(groups, GROUP, DFF), hidden_in.reshape(groups, GROUP, D), cotangent.reshape(groups, GROUP, D))

    def accumulate(carry, block):
        act_b, gate_b, up_b, rows_b, cot_b = block
        terms = (lax.dot_general(act_b, cot_b, leading, preferred_element_type=jnp.float32),
                 lax.dot_general(gate_b, rows_b, leading, preferred_element_type=jnp.float32),
                 lax.dot_general(up_b, rows_b, leading, preferred_element_type=jnp.float32))
        rounded = lax.optimization_barrier(tuple(term.astype(jnp.bfloat16) for term in terms))
        return tuple(total + piece.astype(jnp.float32) for total, piece in zip(carry, rounded)), None

    zero_grad = jnp.zeros((DFF, D), jnp.float32)
    sums, _ = lax.scan(accumulate, (zero_grad, zero_grad, zero_grad), blocks)
    grad_dense_down = sums[0].astype(jnp.bfloat16)
    grad_dense_gate = sums[1].astype(jnp.bfloat16)
    grad_dense_up = sums[2].astype(jnp.bfloat16)

    devices_all = N_TP * N_EP
    route_blocks = routes.reshape(devices_all, TOK_DEV, 2)
    gate_blocks = gate_values.reshape(devices_all, TOK_DEV, 2)
    dispatch, weighted = jax.vmap(partial(slot_tables, experts=E_WIN, capacity=CAP))(route_blocks, gate_blocks)
    rows_f = hidden_in.astype(jnp.float32).reshape(devices_all, TOK_DEV, D)
    cot_f = cotangent.astype(jnp.float32).reshape(devices_all, TOK_DEV, D)
    slot_rows = jnp.einsum("nst,ntd->nsd", dispatch, rows_f, precision=lax.Precision.HIGHEST).astype(jnp.bfloat16)
    slot_cot = jnp.einsum("nst,ntd->nsd", weighted, cot_f, precision=lax.Precision.HIGHEST).astype(jnp.bfloat16)
    routed_rows = slot_rows.reshape(devices_all, E_WIN, CAP, D).transpose(1, 0, 2, 3).reshape(E_WIN, devices_all * CAP, D)
    routed_cot = slot_cot.reshape(devices_all, E_WIN, CAP, D).transpose(1, 0, 2, 3).reshape(E_WIN, devices_all * CAP, D)

    def one_expert(inputs):
        rows_e, cot_e, gate_w, up_w, down_w = inputs
        e_gate = lax.dot_general(rows_e, gate_w, contract, preferred_element_type=jnp.float32)
        e_up = lax.dot_general(rows_e, up_w, contract, preferred_element_type=jnp.float32)
        e_grad_act = lax.dot_general(cot_e, down_w, contract, preferred_element_type=jnp.float32)
        e_act, e_grad_gate, e_grad_up = swiglu_backward(e_gate, e_up, e_grad_act)
        g_down = lax.dot_general(e_act, cot_e, leading, preferred_element_type=jnp.float32).astype(jnp.bfloat16)
        g_gate = lax.dot_general(e_grad_gate, rows_e, leading, preferred_element_type=jnp.float32).astype(jnp.bfloat16)
        g_up = lax.dot_general(e_grad_up, rows_e, leading, preferred_element_type=jnp.float32).astype(jnp.bfloat16)
        slots = rows_e.shape[0]
        gate_blk = e_grad_gate.astype(jnp.float32).reshape(slots, N_EP, EXP_BLOCK)
        up_blk = e_grad_up.astype(jnp.float32).reshape(slots, N_EP, EXP_BLOCK)
        gate_wb = gate_w.astype(jnp.float32).reshape(N_EP, EXP_BLOCK, D)
        up_wb = up_w.astype(jnp.float32).reshape(N_EP, EXP_BLOCK, D)
        terms = jnp.einsum("snh,nhd->nsd", gate_blk, gate_wb) + jnp.einsum("snh,nhd->nsd", up_blk, up_wb)
        rounded = lax.optimization_barrier(terms.astype(jnp.bfloat16))
        slot_input = jnp.sum(rounded.astype(jnp.float32), axis=0)
        return g_gate, g_up, g_down, slot_input

    grad_expert_gate, grad_expert_up, grad_expert_down, slot_input = lax.map(one_expert, (routed_rows, routed_cot, expert_gate, expert_up, expert_down))
    back = slot_input.reshape(E_WIN, devices_all, CAP, D).transpose(1, 0, 2, 3).reshape(devices_all, E_WIN * CAP, D)
    routed_input = jnp.einsum("nst,nsd->ntd", dispatch, back, precision=lax.Precision.HIGHEST).reshape(TOKENS, D)
    grad_input = (dense_input + routed_input).astype(jnp.bfloat16)
    return (grad_input, grad_dense_gate, grad_dense_up, grad_dense_down, grad_expert_gate, grad_expert_up, grad_expert_down)
```

```python
import jax
import jax.numpy as jnp
from jax import lax
from jax.experimental import pallas as pl
from jax.experimental.pallas import tpu as pltpu
from jax.sharding import PartitionSpec as P

CAP = 4
CONTRACT = (((1,), (1,)), ((), ()))
LEADING = (((0,), (0,)), ((), ()))
F32 = jnp.float32
BF16 = jnp.bfloat16


def swiglu_backward(gate_pre, up_pre, grad_act):
    sigmoid_gate = jax.nn.sigmoid(gate_pre)
    silu_gate = gate_pre * sigmoid_gate
    act = (silu_gate * up_pre).astype(BF16)
    silu_slope = sigmoid_gate * (1.0 + gate_pre * (1.0 - sigmoid_gate))
    grad_gate = (grad_act * up_pre * silu_slope).astype(BF16)
    grad_up = (grad_act * silu_gate).astype(BF16)
    return act, grad_gate, grad_up


def slot_tables(routes, gate_values, me, experts):
    tok_count = routes.shape[0]
    named = lax.rem(me + jnp.arange(experts, dtype=jnp.int32), experts)
    onehot = (routes.reshape(-1)[:, None] == named[None, :]).astype(jnp.int32)
    before = jnp.cumsum(onehot, axis=0) - onehot
    slot = onehot[:, :, None] * (before[:, :, None] == jnp.arange(CAP, dtype=jnp.int32)).astype(
        jnp.int32
    )
    slot = slot.reshape(tok_count, 2, experts * CAP).astype(F32)
    dispatch = jnp.sum(slot, axis=1).T.astype(BF16)
    weight = jnp.sum(slot * gate_values[:, :, None], axis=(0, 1))
    return dispatch, weight


def shift(x, axis, size, by):
    return lax.ppermute(x, axis, [(i, (i + by) % size) for i in range(size)])


def send_to_experts(hidden_in, cotangent, dispatch, weight, experts):
    width = hidden_in.shape[1]
    rows = jnp.dot(dispatch, hidden_in, preferred_element_type=F32).astype(BF16)
    cots = jnp.dot(dispatch, cotangent, preferred_element_type=F32)
    cots = (cots * weight[:, None]).astype(BF16)
    sent = jnp.stack(
        [rows.reshape(experts, CAP, width), cots.reshape(experts, CAP, width)], axis=1
    )
    got = jnp.stack([sent[0]] + [shift(sent[k], "tp", experts, k) for k in range(1, experts)])
    got = got.transpose(1, 0, 2, 3).reshape(2, experts * CAP, width)
    slots = lax.all_gather(got, "ep", axis=0, tiled=False)
    return slots[:, 0].reshape(-1, width), slots[:, 1].reshape(-1, width)


def expert_layer(slot_rows, slot_cot, gate_weight, up_weight, down_weight):
    e_gate = lax.dot_general(slot_rows, gate_weight, CONTRACT, preferred_element_type=F32)
    e_up = lax.dot_general(slot_rows, up_weight, CONTRACT, preferred_element_type=F32)
    e_grad_act = lax.dot_general(slot_cot, down_weight, CONTRACT, preferred_element_type=F32)
    e_act, e_grad_gate, e_grad_up = swiglu_backward(e_gate, e_up, e_grad_act)
    g_down = lax.dot_general(e_act, slot_cot, LEADING, preferred_element_type=F32).astype(BF16)
    g_gate = lax.dot_general(e_grad_gate, slot_rows, LEADING, preferred_element_type=F32).astype(
        BF16
    )
    g_up = lax.dot_general(e_grad_up, slot_rows, LEADING, preferred_element_type=F32).astype(BF16)
    terms = jnp.dot(e_grad_gate, gate_weight, preferred_element_type=F32) + jnp.dot(
        e_grad_up, up_weight, preferred_element_type=F32
    )
    return g_gate, g_up, g_down, terms.astype(BF16)


def slots_back(slot_terms, dispatch, experts):
    width = slot_terms.shape[1]
    own = lax.psum_scatter(slot_terms, "ep", scatter_dimension=0, tiled=True)
    own = own.reshape(experts, CAP, width)
    back = jnp.stack([own[0]] + [shift(own[k], "tp", experts, -k) for k in range(1, experts)])
    return lax.dot_general(
        dispatch, back.reshape(experts * CAP, width), LEADING, preferred_element_type=F32
    )


def dense_block(rows, cot, gate, up, down):
    gate_pre = lax.dot_general(rows, gate, CONTRACT, preferred_element_type=F32)
    up_pre = lax.dot_general(rows, up, CONTRACT, preferred_element_type=F32)
    grad_act = lax.dot_general(cot, down, CONTRACT, preferred_element_type=F32)
    act, grad_gate, grad_up = swiglu_backward(gate_pre, up_pre, grad_act)
    partial = jnp.dot(grad_gate, gate, preferred_element_type=F32) + jnp.dot(
        grad_up, up, preferred_element_type=F32
    )
    return act, grad_gate, grad_up, partial.astype(BF16)


def weight_terms(tile, acts, rows, cots, width):
    units = acts[0].shape[1]
    count = len(acts)
    tok = rows[0].shape[0]

    def kernel(tile_ref, *refs):
        a, r, c, out = refs[:count], refs[count : 2 * count], refs[2 * count : 3 * count], refs[-1]
        rows_all = jnp.concatenate([ref[...] for ref in r], axis=0)
        cots_all = jnp.concatenate([ref[...] for ref in c], axis=0)
        for i in range(3):
            left = jnp.concatenate([ref[i] for ref in a], axis=1)
            right = cots_all if i == 0 else rows_all
            out[i] = jnp.dot(left, right, preferred_element_type=F32).astype(BF16)

    tokens = pl.BlockSpec((tok, width), lambda i, tile_ref: (0, tile_ref[0]))
    whole = pl.BlockSpec((3, units, tok), lambda i, tile_ref: (0, 0, 0))
    return pl.pallas_call(
        kernel,
        grid_spec=pltpu.PrefetchScalarGridSpec(
            num_scalar_prefetch=1,
            grid=(1,),
            in_specs=[whole] * count + [tokens] * (2 * count),
            out_specs=pl.BlockSpec((3, units, width), lambda i, tile_ref: (0, 0, 0)),
        ),
        out_shape=jax.ShapeDtypeStruct((3, units, width), BF16),
        compiler_params=pltpu.CompilerParams(vmem_limit_bytes=48 * 1024 * 1024),
        cost_estimate=pl.CostEstimate(
            flops=6 * units * count * tok * width,
            bytes_accessed=2 * (count * tok * (2 * width + 3 * units) + 3 * units * width),
            transcendentals=0,
        ),
        name="weight_terms",
    )(tile.reshape(1), *acts, *rows, *cots)


def line_body(
    hidden_in,
    cotangent,
    routes,
    gate_values,
    dense_gate,
    dense_up,
    dense_down,
    expert_gate,
    expert_up,
    expert_down,
):
    experts = lax.axis_size("tp")
    me = lax.axis_index("tp")
    ep = lax.axis_index("ep")
    core, chip = lax.rem(ep, 2), lax.div(ep, 2)
    half = dense_gate.shape[0] // 2
    columns = dense_down.shape[1]

    down = lax.all_gather(dense_down, "ep", axis=1, tiled=True)

    def gather(x):
        right1 = lax.ppermute(x, "tp", [(0, 1), (1, 2), (2, 3)])
        left1 = lax.ppermute(x, "tp", [(1, 0), (2, 1), (3, 2)])
        right2 = lax.ppermute(right1, "tp", [(1, 2), (2, 3)])
        left2 = lax.ppermute(left1, "tp", [(2, 1), (1, 0)])
        second = jnp.where(me < 2, left2, right2)
        both3 = lax.ppermute(second, "tp", [(1, 0), (2, 3)])
        first = jnp.where(me == 3, right1, left1)
        third = jnp.where((me == 0) | (me == 3), both3, right1)
        return [x, first, second, third]

    rows = gather(hidden_in)
    cots = gather(cotangent)

    dispatch, weight = slot_tables(routes, gate_values, me, experts)
    slot_rows, slot_cot = send_to_experts(hidden_in, cotangent, dispatch, weight, experts)
    g_gate, g_up, g_down, slot_terms = expert_layer(
        slot_rows, slot_cot, expert_gate[0], expert_up[0], expert_down[0]
    )
    routed_input = slots_back(slot_terms, dispatch, experts)

    partner = [(i, i ^ 1) for i in range(8)]
    acts, partials = [], []
    for r, c in zip(rows, cots):
        act, grad_gate, grad_up, partial = dense_block(r, c, dense_gate, dense_up, down)
        turned = jnp.stack([act.T, grad_gate.T, grad_up.T])
        own = lax.dynamic_slice_in_dim(turned, core * half, half, axis=1)
        other = lax.dynamic_slice_in_dim(turned, (1 - core) * half, half, axis=1)
        acts += [own, lax.ppermute(other, "ep", partner)]
        partials.append(partial)

    def add(a, b):
        return (a.astype(F32) + b.astype(F32)).astype(BF16)

    in_right = lax.ppermute(partials[2], "tp", [(0, 1), (1, 2)])
    in_left = lax.ppermute(partials[2], "tp", [(3, 2), (2, 1)])
    from_left = lax.ppermute(add(partials[1], in_right), "tp", [(0, 1), (1, 2), (2, 3)])
    from_right = lax.ppermute(
        add(jnp.where(me == 3, partials[1], partials[3]), in_left), "tp", [(3, 2), (2, 1), (1, 0)]
    )
    far = lax.ppermute(partials[3], "tp", [(0, 3), (3, 0)])
    grad_input = (
        partials[0].astype(F32)
        + from_left.astype(F32)
        + from_right.astype(F32)
        + far.astype(F32)
        + routed_input
    ).astype(BF16)

    rows_all, cots_all = [], []
    for r, c in zip(rows, cots):
        rows_all += [r, lax.ppermute(r, "ep", partner)]
        cots_all += [c, lax.ppermute(c, "ep", partner)]
    total = None
    for apart in (3, 1, 2, 0):
        term = weight_terms(
            jnp.bitwise_xor(chip, apart), acts, rows_all, cots_all, 2 * columns
        )
        if apart:
            term = lax.ppermute(term, "ep", [(i, i ^ (2 * apart)) for i in range(8)])
        total = term.astype(F32) if total is None else total + term.astype(F32)
    total = total.astype(BF16)
    own = lax.dynamic_slice_in_dim(total, core * columns, columns, axis=2)
    other = lax.dynamic_slice_in_dim(total, (1 - core) * columns, columns, axis=2)
    other = lax.ppermute(other, "ep", partner)
    grads = jnp.where(
        core == 0,
        jnp.concatenate([own, other], axis=1),
        jnp.concatenate([other, own], axis=1),
    )
    return (grad_input, grads[1], grads[2], grads[0], g_gate[None], g_up[None], g_down[None])


def general_body(
    hidden_in,
    cotangent,
    routes,
    gate_values,
    dense_gate,
    dense_up,
    dense_down,
    expert_gate,
    expert_up,
    expert_down,
):
    experts = lax.axis_size("tp")
    me = lax.axis_index("tp")
    dispatch, weight = slot_tables(routes, gate_values, me, experts)
    slot_rows, slot_cot = send_to_experts(hidden_in, cotangent, dispatch, weight, experts)
    rows = lax.all_gather(hidden_in, "tp", axis=0, tiled=True)
    cots = lax.all_gather(cotangent, "tp", axis=0, tiled=True)
    down = lax.all_gather(dense_down, "ep", axis=1, tiled=True)
    act, grad_gate, grad_up, partial = dense_block(rows, cots, dense_gate, dense_up, down)
    dense_input = lax.psum_scatter(partial, "tp", scatter_dimension=0, tiled=True)
    grads = [
        lax.psum_scatter(
            lax.dot_general(a, b, LEADING, preferred_element_type=F32).astype(BF16),
            "ep",
            scatter_dimension=1,
            tiled=True,
        )
        for a, b in ((act, cots), (grad_gate, rows), (grad_up, rows))
    ]
    g_gate, g_up, g_down, slot_terms = expert_layer(
        slot_rows, slot_cot, expert_gate[0], expert_up[0], expert_down[0]
    )
    routed_input = slots_back(slot_terms, dispatch, experts)
    grad_input = (dense_input.astype(F32) + routed_input).astype(BF16)
    return (grad_input, grads[1], grads[2], grads[0], g_gate[None], g_up[None], g_down[None])


def solution(mesh):
    placed = (
        P(("ep", "tp"), None),
        P(("ep", "tp"), None),
        P(("ep", "tp"), None),
        P(("ep", "tp"), None),
        P("tp", None),
        P("tp", None),
        P("tp", "ep"),
        P("tp", "ep", None),
        P("tp", "ep", None),
        P("tp", "ep", None),
    )
    in_line = mesh.shape["tp"] == 4 and mesh.shape["ep"] == 8
    return jax.shard_map(
        line_body if in_line else general_body,
        mesh=mesh,
        in_specs=placed,
        out_specs=(
            P(("ep", "tp"), None),
            P("tp", "ep"),
            P("tp", "ep"),
            P("tp", "ep"),
            P("tp", "ep", None),
            P("tp", "ep", None),
            P("tp", "ep", None),
        ),
        check_vma=False,
    )
```

```python
import jax
import jax.numpy as jnp
from jax import lax
from jax.experimental import pallas as pl
from jax.experimental.pallas import tpu as pltpu
from jax.sharding import PartitionSpec as P

CAP = 4
CONTRACT = (((1,), (1,)), ((), ()))
LEADING = (((0,), (0,)), ((), ()))
F32 = jnp.float32
BF16 = jnp.bfloat16


def swiglu_backward(gate_pre, up_pre, grad_act):
    sigmoid_gate = jax.nn.sigmoid(gate_pre)
    silu_gate = gate_pre * sigmoid_gate
    act = (silu_gate * up_pre).astype(BF16)
    silu_slope = sigmoid_gate * (1.0 + gate_pre * (1.0 - sigmoid_gate))
    grad_gate = (grad_act * up_pre * silu_slope).astype(BF16)
    grad_up = (grad_act * silu_gate).astype(BF16)
    return act, grad_gate, grad_up


def slot_tables(routes, gate_values, me, experts):
    tok_count = routes.shape[0]
    named = lax.rem(me + jnp.arange(experts, dtype=jnp.int32), experts)
    onehot = (routes.reshape(-1)[:, None] == named[None, :]).astype(jnp.int32)
    before = jnp.cumsum(onehot, axis=0) - onehot
    slot = onehot[:, :, None] * (before[:, :, None] == jnp.arange(CAP, dtype=jnp.int32)).astype(
        jnp.int32
    )
    slot = slot.reshape(tok_count, 2, experts * CAP).astype(F32)
    dispatch = jnp.sum(slot, axis=1).T.astype(BF16)
    weight = jnp.sum(slot * gate_values[:, :, None], axis=(0, 1))
    return dispatch, weight


def shift(x, axis, size, by):
    return lax.ppermute(x, axis, [(i, (i + by) % size) for i in range(size)])


def send_to_experts(hidden_in, cotangent, dispatch, weight, experts):
    width = hidden_in.shape[1]
    rows = jnp.dot(dispatch, hidden_in, preferred_element_type=F32).astype(BF16)
    cots = jnp.dot(dispatch, cotangent, preferred_element_type=F32)
    cots = (cots * weight[:, None]).astype(BF16)
    sent = jnp.stack(
        [rows.reshape(experts, CAP, width), cots.reshape(experts, CAP, width)], axis=1
    )
    got = jnp.stack([sent[0]] + [shift(sent[k], "tp", experts, k) for k in range(1, experts)])
    return got.transpose(1, 0, 2, 3).reshape(2, experts * CAP, width)


def expert_layer(slot_rows, slot_cot, gate_weight, up_weight, down_weight):
    e_gate = lax.dot_general(slot_rows, gate_weight, CONTRACT, preferred_element_type=F32)
    e_up = lax.dot_general(slot_rows, up_weight, CONTRACT, preferred_element_type=F32)
    e_grad_act = lax.dot_general(slot_cot, down_weight, CONTRACT, preferred_element_type=F32)
    e_act, e_grad_gate, e_grad_up = swiglu_backward(e_gate, e_up, e_grad_act)
    g_down = lax.dot_general(e_act, slot_cot, LEADING, preferred_element_type=F32).astype(BF16)
    g_gate = lax.dot_general(e_grad_gate, slot_rows, LEADING, preferred_element_type=F32).astype(
        BF16
    )
    g_up = lax.dot_general(e_grad_up, slot_rows, LEADING, preferred_element_type=F32).astype(BF16)
    terms = jnp.dot(e_grad_gate, gate_weight, preferred_element_type=F32) + jnp.dot(
        e_grad_up, up_weight, preferred_element_type=F32
    )
    return g_gate, g_up, g_down, terms.astype(BF16)


def slots_back(own, dispatch, experts):
    width = own.shape[1]
    own = own.reshape(experts, CAP, width)
    back = jnp.stack([own[0]] + [shift(own[k], "tp", experts, -k) for k in range(1, experts)])
    return lax.dot_general(
        dispatch, back.reshape(experts * CAP, width), LEADING, preferred_element_type=F32
    )


def plain_block(rows, cot, gate, up, down):
    gate_pre = lax.dot_general(rows, gate, CONTRACT, preferred_element_type=F32)
    up_pre = lax.dot_general(rows, up, CONTRACT, preferred_element_type=F32)
    grad_act = lax.dot_general(cot, down, CONTRACT, preferred_element_type=F32)
    act, grad_gate, grad_up = swiglu_backward(gate_pre, up_pre, grad_act)
    partial = jnp.dot(grad_gate, gate, preferred_element_type=F32) + jnp.dot(
        grad_up, up, preferred_element_type=F32
    )
    return act, grad_gate, grad_up, partial.astype(BF16)


VMEM_LIMIT = 56 * 1024 * 1024


def unit_tiles(units):
    tiles = [(i, 256, 0) for i in range(0, units - units % 256, 256)]
    rest = units % 256
    if rest:
        size = -(-rest // 128) * 128
        tiles.append((units - size, size, size - rest))
    return tiles


def layer_kernel(rows, cot, gate, up, down, loaded, sems, turned, partial, col):
    units, width = gate.shape
    tiles = unit_tiles(units)
    sources = (gate, up, down)
    begin = 0
    copies = []
    for t, (start, size, again) in enumerate(tiles):
        begin = start + again
        copies.append(
            [
                pltpu.make_async_copy(
                    sources[w].at[pl.ds(begin, size - again)],
                    loaded.at[w, pl.ds(begin, size - again)],
                    sems.at[w, t],
                )
                for w in range(3)
            ]
        )
    for group in copies:
        for copy in group:
            copy.start()
    grads = []
    for t, (start, size, again) in enumerate(tiles):
        pre = []
        for w in range(3):
            copies[t][w].wait()
            left = cot if w == 2 else rows
            pre.append(
                lax.dot_general(
                    left[...],
                    loaded[w, start : start + size],
                    CONTRACT,
                    preferred_element_type=F32,
                )
            )
        sigmoid_gate = jax.nn.sigmoid(pre[0])
        silu_gate = pre[0] * sigmoid_gate
        act = silu_gate * pre[1]
        slope = sigmoid_gate * (1.0 + pre[0] * (1.0 - sigmoid_gate))
        grad_gate = pre[2] * pre[1] * slope
        grad_up = pre[2] * silu_gate
        for i, value in enumerate((act, grad_gate, grad_up)):
            turned[i, start : start + size] = value.T.astype(BF16)
        if again:
            keep = lax.broadcasted_iota(jnp.int32, grad_gate.shape, 1) >= again
            grad_gate = jnp.where(keep, grad_gate, 0.0)
            grad_up = jnp.where(keep, grad_up, 0.0)
        grads.append((grad_gate.astype(BF16), grad_up.astype(BF16)))
    for j in range(0, width, col):
        total = None
        for t, (start, size, again) in enumerate(tiles):
            for w in range(2):
                term = jnp.dot(
                    grads[t][w],
                    loaded[w, start : start + size, j : j + col],
                    preferred_element_type=F32,
                )
                total = term if total is None else total + term
        partial[:, j : j + col] = total.astype(BF16)


def dense_block(core, rows, cot, gate, up, down):
    tok, width = rows.shape
    units = gate.shape[0]
    half = units // 2

    def kernel(core_ref, rows, cot, gate, up, down, own, other, partial, loaded, turned, sems):
        layer_kernel(rows, cot, gate, up, down, loaded, sems, turned, partial, 512)
        mine = core_ref[0]
        own[...] = turned[:, pl.ds(pl.multiple_of(mine * half, 16), half), :]
        other[...] = turned[:, pl.ds(pl.multiple_of((1 - mine) * half, 16), half), :]

    vmem = pl.BlockSpec(memory_space=pltpu.VMEM)
    hbm = pl.BlockSpec(memory_space=pl.ANY)
    return pl.pallas_call(
        kernel,
        in_specs=[pl.BlockSpec(memory_space=pltpu.SMEM), vmem, vmem, hbm, hbm, hbm],
        out_specs=[vmem, vmem, vmem],
        out_shape=[
            jax.ShapeDtypeStruct((3, half, tok), BF16),
            jax.ShapeDtypeStruct((3, half, tok), BF16),
            jax.ShapeDtypeStruct((tok, width), BF16),
        ],
        scratch_shapes=[
            pltpu.VMEM((3, units, width), BF16),
            pltpu.VMEM((3, units, tok), BF16),
            pltpu.SemaphoreType.DMA((3, len(unit_tiles(units)))),
        ],
        compiler_params=pltpu.CompilerParams(vmem_limit_bytes=VMEM_LIMIT),
        cost_estimate=pl.CostEstimate(
            flops=10 * units * width * tok,
            bytes_accessed=6 * units * width + 6 * tok * (width + units),
            transcendentals=units * tok,
        ),
        name="dense_block",
    )(core.reshape(1), rows, cot, gate, up, down)


def expert_block(rows, cot, gate, up, down):
    tok, width = rows.shape
    units = gate.shape[0]
    col = width // 4

    def kernel(
        rows, cot, gate, up, down, g_gate, g_up, g_down, partial, loaded, turned, made, sems, out_sems
    ):
        layer_kernel(rows, cot, gate, up, down, loaded, sems, turned, partial, 512)
        outs = (g_down, g_gate, g_up)
        pending = [None, None]
        step = 0
        for i in range(3):
            right = cot if i == 0 else rows
            for j in range(0, width, col):
                slot = step % 2
                if pending[slot] is not None:
                    pending[slot].wait()
                made[slot] = jnp.dot(
                    turned[i], right[:, j : j + col], preferred_element_type=F32
                ).astype(BF16)
                copy = pltpu.make_async_copy(
                    made.at[slot], outs[i].at[:, pl.ds(j, col)], out_sems.at[slot]
                )
                copy.start()
                pending[slot] = copy
                step += 1
        for copy in pending:
            copy.wait()

    vmem = pl.BlockSpec(memory_space=pltpu.VMEM)
    hbm = pl.BlockSpec(memory_space=pl.ANY)
    grad = jax.ShapeDtypeStruct((units, width), BF16)
    return pl.pallas_call(
        kernel,
        in_specs=[vmem, vmem, hbm, hbm, hbm],
        out_specs=[hbm, hbm, hbm, vmem],
        out_shape=[grad, grad, grad, jax.ShapeDtypeStruct((tok, width), BF16)],
        scratch_shapes=[
            pltpu.VMEM((3, units, width), BF16),
            pltpu.VMEM((3, units, tok), BF16),
            pltpu.VMEM((2, units, col), BF16),
            pltpu.SemaphoreType.DMA((3, len(unit_tiles(units)))),
            pltpu.SemaphoreType.DMA((2,)),
        ],
        compiler_params=pltpu.CompilerParams(vmem_limit_bytes=VMEM_LIMIT),
        cost_estimate=pl.CostEstimate(
            flops=16 * units * width * tok,
            bytes_accessed=12 * units * width + 6 * tok * width,
            transcendentals=units * tok,
        ),
        name="expert_block",
    )(rows, cot, gate, up, down)


def weight_terms(tile, acts, rows, cots, width, cut):
    units = acts[0].shape[1]
    count = len(acts)
    tok = rows[0].shape[0]

    def kernel(tile_ref, *refs):
        a, r, c = refs[:count], refs[count : 2 * count], refs[2 * count : 3 * count]
        low, high = refs[-2:]
        rows_all = jnp.concatenate([ref[...] for ref in r], axis=0)
        cots_all = jnp.concatenate([ref[...] for ref in c], axis=0)
        for i in range(3):
            left = jnp.concatenate([ref[i] for ref in a], axis=1)
            right = cots_all if i == 0 else rows_all
            made = jnp.dot(left, right, preferred_element_type=F32).astype(BF16)
            low[i] = made[:cut]
            high[i] = made[cut:]

    tokens = pl.BlockSpec((tok, width), lambda i, tile_ref: (0, tile_ref[0]))

    def whole(n, w):
        return pl.BlockSpec((3, n, w), lambda i, tile_ref: (0, 0, 0))

    return pl.pallas_call(
        kernel,
        grid_spec=pltpu.PrefetchScalarGridSpec(
            num_scalar_prefetch=1,
            grid=(1,),
            in_specs=[whole(units, tok)] * count + [tokens] * (2 * count),
            out_specs=[whole(cut, width), whole(units - cut, width)],
        ),
        out_shape=[
            jax.ShapeDtypeStruct((3, cut, width), BF16),
            jax.ShapeDtypeStruct((3, units - cut, width), BF16),
        ],
        compiler_params=pltpu.CompilerParams(vmem_limit_bytes=VMEM_LIMIT),
        cost_estimate=pl.CostEstimate(
            flops=6 * units * count * tok * width,
            bytes_accessed=2 * (count * tok * (2 * width + 3 * units) + 3 * units * width),
            transcendentals=0,
        ),
        name="weight_terms",
    )(tile.reshape(1), *acts, *rows, *cots)


def together(*values):
    return lax.optimization_barrier(values)


def line_body(
    hidden_in,
    cotangent,
    routes,
    gate_values,
    dense_gate,
    dense_up,
    dense_down,
    expert_gate,
    expert_up,
    expert_down,
):
    experts = lax.axis_size("tp")
    me = lax.axis_index("tp")
    ep = lax.axis_index("ep")
    core, chip = lax.rem(ep, 2), lax.div(ep, 2)
    half = dense_gate.shape[0] // 2
    columns = dense_down.shape[1]
    own_rows = (hidden_in, cotangent)

    down = lax.all_gather(dense_down, "ep", axis=1, tiled=True)

    def along(values, pairs):
        return [lax.ppermute(v, "tp", pairs) for v in values]

    def across(value, apart):
        return lax.ppermute(value, "ep", [(i, i ^ apart) for i in range(8)])

    def pick(condition, a, b):
        return [jnp.where(condition, x, y) for x, y in zip(a, b)]

    def add(a, b):
        return (a.astype(F32) + b.astype(F32)).astype(BF16)

    def block(values):
        own, other, partial = dense_block(core, *values, dense_gate, dense_up, down)
        both = ([own, across(other, 1)], *([v, across(v, 1)] for v in values))
        return both, partial

    right1 = along(own_rows, [(0, 1), (1, 2), (2, 3)])
    left1 = along(own_rows, [(1, 0), (2, 1), (3, 2)])
    dispatch, weight = slot_tables(routes, gate_values, me, experts)
    got = send_to_experts(hidden_in, cotangent, dispatch, weight, experts)

    *right1, left1[0], left1[1], down = together(*right1, *left1, down)
    right2 = along(right1, [(1, 2), (2, 3)])
    left2 = along(left1, [(2, 1), (1, 0)])
    got, down = together(got, down)
    slots = lax.all_gather(got, "ep", axis=0, tiled=False)
    first = pick(me == 3, right1, left1)
    own_rows = together(*own_rows, *first)[:2]
    both0, partial0 = block(own_rows)
    both1, partial1 = block(first)

    second = pick(me < 2, left2, right2)
    *second, partial0, partial1, slots = together(*second, partial0, partial1, slots)
    ends = along(second, [(1, 0), (2, 3)])
    both2, partial2 = block(second)
    slots, partial2 = together(slots, partial2)
    slot_rows, slot_cot = slots[:, 0].reshape(-1, hidden_in.shape[1]), slots[:, 1].reshape(
        -1, hidden_in.shape[1]
    )
    g_gate, g_up, g_down, slot_terms = expert_block(
        slot_rows, slot_cot, expert_gate[0], expert_up[0], expert_down[0]
    )
    in_right = lax.ppermute(partial2, "tp", [(0, 1), (1, 2)])
    in_left = lax.ppermute(partial2, "tp", [(3, 2), (2, 1)])

    third = pick((me == 0) | (me == 3), ends, right1)
    third, in_right, in_left, slot_terms, both0, both1, both2 = together(
        third, in_right, in_left, slot_terms, both0, both1, both2
    )
    from_left = lax.ppermute(add(partial1, in_right), "tp", [(0, 1), (1, 2), (2, 3)])
    both3, partial3 = block(third)
    far = lax.ppermute(partial3, "tp", [(0, 3), (3, 0)])
    from_right = lax.ppermute(
        add(jnp.where(me == 3, partial1, partial3), in_left), "tp", [(3, 2), (2, 1), (1, 0)]
    )

    acts, rows_all, cots_all = (a + b + c + d for a, b, c, d in zip(both0, both1, both2, both3))
    cut = -(-half // 32) * 16
    made = {
        apart: weight_terms(
            jnp.bitwise_xor(chip, apart), acts, rows_all, cots_all, 2 * columns, cut
        )
        for apart in (3, 1, 2, 0)
    }
    *made[3], from_left = together(*made[3], from_left)
    low = across(made[3][0], 2)
    high = across(made[3][1], 4)
    low_own = across(made[1][0], 2)
    high_own = across(made[2][1], 4)
    routed = lax.psum_scatter(slot_terms, "ep", scatter_dimension=0, tiled=True)
    low, high, far, from_right, routed = together(low, high, far, from_right, routed)
    routed_input = slots_back(routed, dispatch, experts)
    low = across(add(made[2][0], low), 4)
    high = across(add(made[1][1], high), 2)
    total = jnp.concatenate(
        [
            made[0][0].astype(F32) + low_own.astype(F32) + low.astype(F32),
            made[0][1].astype(F32) + high_own.astype(F32) + high.astype(F32),
        ],
        axis=1,
    ).astype(BF16)
    own = lax.dynamic_slice_in_dim(total, core * columns, columns, axis=2)
    other = lax.dynamic_slice_in_dim(total, (1 - core) * columns, columns, axis=2)
    other = across(other, 1)
    grads = [
        jnp.where(
            core == 0,
            jnp.concatenate([own[i], other[i]], axis=0),
            jnp.concatenate([other[i], own[i]], axis=0),
        )
        for i in range(3)
    ]
    grad_input = (
        partial0.astype(F32)
        + from_left.astype(F32)
        + from_right.astype(F32)
        + far.astype(F32)
        + routed_input
    ).astype(BF16)
    return (grad_input, grads[1], grads[2], grads[0], g_gate[None], g_up[None], g_down[None])


def general_body(
    hidden_in,
    cotangent,
    routes,
    gate_values,
    dense_gate,
    dense_up,
    dense_down,
    expert_gate,
    expert_up,
    expert_down,
):
    experts = lax.axis_size("tp")
    me = lax.axis_index("tp")
    dispatch, weight = slot_tables(routes, gate_values, me, experts)
    got = send_to_experts(hidden_in, cotangent, dispatch, weight, experts)
    slots = lax.all_gather(got, "ep", axis=0, tiled=False)
    slot_rows, slot_cot = slots[:, 0].reshape(-1, hidden_in.shape[1]), slots[:, 1].reshape(
        -1, hidden_in.shape[1]
    )
    rows = lax.all_gather(hidden_in, "tp", axis=0, tiled=True)
    cots = lax.all_gather(cotangent, "tp", axis=0, tiled=True)
    down = lax.all_gather(dense_down, "ep", axis=1, tiled=True)
    act, grad_gate, grad_up, partial = plain_block(rows, cots, dense_gate, dense_up, down)
    dense_input = lax.psum_scatter(partial, "tp", scatter_dimension=0, tiled=True)
    grads = [
        lax.psum_scatter(
            lax.dot_general(a, b, LEADING, preferred_element_type=F32).astype(BF16),
            "ep",
            scatter_dimension=1,
            tiled=True,
        )
        for a, b in ((act, cots), (grad_gate, rows), (grad_up, rows))
    ]
    g_gate, g_up, g_down, slot_terms = expert_layer(
        slot_rows, slot_cot, expert_gate[0], expert_up[0], expert_down[0]
    )
    routed = lax.psum_scatter(slot_terms, "ep", scatter_dimension=0, tiled=True)
    routed_input = slots_back(routed, dispatch, experts)
    grad_input = (dense_input.astype(F32) + routed_input).astype(BF16)
    return (grad_input, grads[1], grads[2], grads[0], g_gate[None], g_up[None], g_down[None])


def solution(mesh):
    placed = (
        P(("ep", "tp"), None),
        P(("ep", "tp"), None),
        P(("ep", "tp"), None),
        P(("ep", "tp"), None),
        P("tp", None),
        P("tp", None),
        P("tp", "ep"),
        P("tp", "ep", None),
        P("tp", "ep", None),
        P("tp", "ep", None),
    )
    in_line = mesh.shape["tp"] == 4 and mesh.shape["ep"] == 8
    return jax.shard_map(
        line_body if in_line else general_body,
        mesh=mesh,
        in_specs=placed,
        out_specs=(
            P(("ep", "tp"), None),
            P("tp", "ep"),
            P("tp", "ep"),
            P("tp", "ep"),
            P("tp", "ep", None),
            P("tp", "ep", None),
            P("tp", "ep", None),
        ),
        check_vma=False,
    )
```

```python
import jax
import jax.numpy as jnp
from jax import lax
from jax.experimental import pallas as pl
from jax.experimental.pallas import tpu as pltpu
from jax.sharding import PartitionSpec as P

CAP = 4
CONTRACT = (((1,), (1,)), ((), ()))
LEADING = (((0,), (0,)), ((), ()))
F32 = jnp.float32
BF16 = jnp.bfloat16


def swiglu_backward(gate_pre, up_pre, grad_act):
    sigmoid_gate = jax.nn.sigmoid(gate_pre)
    silu_gate = gate_pre * sigmoid_gate
    act = (silu_gate * up_pre).astype(BF16)
    silu_slope = sigmoid_gate * (1.0 + gate_pre * (1.0 - sigmoid_gate))
    grad_gate = (grad_act * up_pre * silu_slope).astype(BF16)
    grad_up = (grad_act * silu_gate).astype(BF16)
    return act, grad_gate, grad_up


def slot_tables(routes, gate_values, me, experts):
    tok_count = routes.shape[0]
    named = lax.rem(me + jnp.arange(experts, dtype=jnp.int32), experts)
    onehot = (routes.reshape(-1)[:, None] == named[None, :]).astype(jnp.int32)
    before = jnp.cumsum(onehot, axis=0) - onehot
    slot = onehot[:, :, None] * (before[:, :, None] == jnp.arange(CAP, dtype=jnp.int32)).astype(
        jnp.int32
    )
    slot = slot.reshape(tok_count, 2, experts * CAP).astype(F32)
    dispatch = jnp.sum(slot, axis=1).T.astype(BF16)
    weight = jnp.sum(slot * gate_values[:, :, None], axis=(0, 1))
    return dispatch, weight


def shift(x, axis, size, by):
    return lax.ppermute(x, axis, [(i, (i + by) % size) for i in range(size)])


def slots_to_send(hidden_in, cotangent, dispatch, weight, experts):
    width = hidden_in.shape[1]
    rows = jnp.dot(dispatch, hidden_in, preferred_element_type=F32).astype(BF16)
    cots = jnp.dot(dispatch, cotangent, preferred_element_type=F32)
    cots = (cots * weight[:, None]).astype(BF16)
    return jnp.stack(
        [rows.reshape(experts, CAP, width), cots.reshape(experts, CAP, width)], axis=1
    )


def exchange_slots(sent, experts):
    width = sent.shape[3]
    got = jnp.stack([sent[0]] + [shift(sent[k], "tp", experts, k) for k in range(1, experts)])
    return got.transpose(1, 0, 2, 3).reshape(2, experts * CAP, width)


def expert_layer(slot_rows, slot_cot, gate_weight, up_weight, down_weight):
    e_gate = lax.dot_general(slot_rows, gate_weight, CONTRACT, preferred_element_type=F32)
    e_up = lax.dot_general(slot_rows, up_weight, CONTRACT, preferred_element_type=F32)
    e_grad_act = lax.dot_general(slot_cot, down_weight, CONTRACT, preferred_element_type=F32)
    e_act, e_grad_gate, e_grad_up = swiglu_backward(e_gate, e_up, e_grad_act)
    g_down = lax.dot_general(e_act, slot_cot, LEADING, preferred_element_type=F32).astype(BF16)
    g_gate = lax.dot_general(e_grad_gate, slot_rows, LEADING, preferred_element_type=F32).astype(
        BF16
    )
    g_up = lax.dot_general(e_grad_up, slot_rows, LEADING, preferred_element_type=F32).astype(BF16)
    terms = jnp.dot(e_grad_gate, gate_weight, preferred_element_type=F32) + jnp.dot(
        e_grad_up, up_weight, preferred_element_type=F32
    )
    return g_gate, g_up, g_down, terms.astype(BF16)


def slots_back(own, dispatch, experts):
    width = own.shape[1]
    own = own.reshape(experts, CAP, width)
    back = jnp.stack([own[0]] + [shift(own[k], "tp", experts, -k) for k in range(1, experts)])
    return lax.dot_general(
        dispatch, back.reshape(experts * CAP, width), LEADING, preferred_element_type=F32
    )


def plain_block(rows, cot, gate, up, down):
    gate_pre = lax.dot_general(rows, gate, CONTRACT, preferred_element_type=F32)
    up_pre = lax.dot_general(rows, up, CONTRACT, preferred_element_type=F32)
    grad_act = lax.dot_general(cot, down, CONTRACT, preferred_element_type=F32)
    act, grad_gate, grad_up = swiglu_backward(gate_pre, up_pre, grad_act)
    partial = jnp.dot(grad_gate, gate, preferred_element_type=F32) + jnp.dot(
        grad_up, up, preferred_element_type=F32
    )
    return act, grad_gate, grad_up, partial.astype(BF16)


VMEM_LIMIT = 56 * 1024 * 1024


def unit_tiles(units):
    return [(start, min(256, units - start)) for start in range(0, units, 256)]


def layer_kernel(rows, cots, gate, up, down, loaded, sems, turned, partial, col):
    units, width = gate.shape
    tiles = unit_tiles(units)
    copies = [
        [
            pltpu.make_async_copy(
                source.at[pl.ds(start, size)], loaded.at[w, pl.ds(start, size)], sems.at[w, t]
            )
            for w, source in enumerate((gate, up, down))
        ]
        for t, (start, size) in enumerate(tiles)
    ]
    for group in copies:
        for copy in group:
            copy.start()
    rows = rows[0] if len(rows) == 1 else jnp.concatenate(rows, axis=0)
    cots = cots[0] if len(cots) == 1 else jnp.concatenate(cots, axis=0)
    grads = []
    for t, (start, size) in enumerate(tiles):
        pre = []
        for w in range(3):
            copies[t][w].wait()
            pre.append(
                lax.dot_general(
                    loaded[w, start : start + size],
                    cots if w == 2 else rows,
                    CONTRACT,
                    preferred_element_type=F32,
                )
            )
        act, grad_gate, grad_up = swiglu_backward(*pre)
        for i, value in enumerate((act, grad_gate, grad_up)):
            turned[i, start : start + size] = value
    grads = [turned[1].T, turned[2].T]
    for j in range(0, width, col):
        partial[:, j : j + col] = (
            jnp.dot(grads[0], loaded[0, :, j : j + col], preferred_element_type=F32)
            + jnp.dot(grads[1], loaded[1, :, j : j + col], preferred_element_type=F32)
        ).astype(BF16)


def dense_block(core, blocks, gate, up, down):
    tok, width = blocks[0].shape[1] * len(blocks), blocks[0].shape[2]
    units = gate.shape[0]
    half = units // 2

    def kernel(core_ref, *refs):
        ins, refs = refs[: len(blocks)], refs[len(blocks) :]
        gate, up, down, own, other, partial, loaded, turned, sems = refs
        rows = [ref[0] for ref in ins]
        cots = [ref[1] for ref in ins]
        layer_kernel(rows, cots, gate, up, down, loaded, sems, turned, partial, 512)
        mine = core_ref[0]
        own[...] = turned[:, pl.ds(pl.multiple_of(mine * half, 16), half), :]
        other[...] = turned[:, pl.ds(pl.multiple_of((1 - mine) * half, 16), half), :]

    vmem = pl.BlockSpec(memory_space=pltpu.VMEM)
    hbm = pl.BlockSpec(memory_space=pl.ANY)
    return pl.pallas_call(
        kernel,
        in_specs=[pl.BlockSpec(memory_space=pltpu.SMEM)] + [vmem] * len(blocks) + [hbm] * 3,
        out_specs=[vmem, vmem, vmem],
        out_shape=[
            jax.ShapeDtypeStruct((3, half, tok), BF16),
            jax.ShapeDtypeStruct((3, half, tok), BF16),
            jax.ShapeDtypeStruct((tok, width), BF16),
        ],
        scratch_shapes=[
            pltpu.VMEM((3, units, width), BF16),
            pltpu.VMEM((3, units, tok), BF16),
            pltpu.SemaphoreType.DMA((3, len(unit_tiles(units)))),
        ],
        compiler_params=pltpu.CompilerParams(vmem_limit_bytes=VMEM_LIMIT),
        cost_estimate=pl.CostEstimate(
            flops=10 * units * width * tok,
            bytes_accessed=6 * units * width + 6 * tok * (width + units),
            transcendentals=units * tok,
        ),
        name="dense_block",
    )(core.reshape(1), *blocks, gate, up, down)


def expert_block(rows, cots, gate, up, down):
    tok, width = rows.shape
    units = gate.shape[0]
    col = width // 4

    def kernel(
        rows, cots, gate, up, down, g_gate, g_up, g_down, partial, loaded, turned, made, sems, out_sems
    ):
        layer_kernel([rows[...]], [cots[...]], gate, up, down, loaded, sems, turned, partial, 512)
        outs = (g_down, g_gate, g_up)
        pending = [None, None]
        step = 0
        for i in range(3):
            right = cots if i == 0 else rows
            for j in range(0, width, col):
                slot = step % 2
                if pending[slot] is not None:
                    pending[slot].wait()
                made[slot] = jnp.dot(
                    turned[i], right[:, j : j + col], preferred_element_type=F32
                ).astype(BF16)
                copy = pltpu.make_async_copy(
                    made.at[slot], outs[i].at[:, pl.ds(j, col)], out_sems.at[slot]
                )
                copy.start()
                pending[slot] = copy
                step += 1
        for copy in pending:
            copy.wait()

    vmem = pl.BlockSpec(memory_space=pltpu.VMEM)
    hbm = pl.BlockSpec(memory_space=pl.ANY)
    grad = jax.ShapeDtypeStruct((units, width), BF16)
    return pl.pallas_call(
        kernel,
        in_specs=[vmem, vmem, hbm, hbm, hbm],
        out_specs=[hbm, hbm, hbm, vmem],
        out_shape=[grad, grad, grad, jax.ShapeDtypeStruct((tok, width), BF16)],
        scratch_shapes=[
            pltpu.VMEM((3, units, width), BF16),
            pltpu.VMEM((3, units, tok), BF16),
            pltpu.VMEM((2, units, col), BF16),
            pltpu.SemaphoreType.DMA((3, len(unit_tiles(units)))),
            pltpu.SemaphoreType.DMA((2,)),
        ],
        compiler_params=pltpu.CompilerParams(vmem_limit_bytes=VMEM_LIMIT),
        cost_estimate=pl.CostEstimate(
            flops=16 * units * width * tok,
            bytes_accessed=12 * units * width + 6 * tok * width,
            transcendentals=units * tok,
        ),
        name="expert_block",
    )(rows, cots, gate, up, down)


def weight_terms(tile, acts, blocks, width, cut):
    units = acts[0].shape[1]
    tokens = sum(b.shape[1] for b in blocks)

    def kernel(tile_ref, *refs):
        a, b = refs[: len(acts)], refs[len(acts) : -2]
        low, high = refs[-2:]
        rows = jnp.concatenate([ref[0] for ref in b], axis=0)
        cots = jnp.concatenate([ref[1] for ref in b], axis=0)
        for i in range(3):
            left = jnp.concatenate([ref[i] for ref in a], axis=1)
            made = jnp.dot(left, cots if i == 0 else rows, preferred_element_type=F32).astype(BF16)
            low[i] = made[:cut]
            high[i] = made[cut:]

    def whole(shape):
        return pl.BlockSpec(shape, lambda i, tile_ref: (0, 0, 0))

    def columns(block):
        return pl.BlockSpec((*block.shape[:2], width), lambda i, tile_ref: (0, 0, tile_ref[0]))

    return pl.pallas_call(
        kernel,
        grid_spec=pltpu.PrefetchScalarGridSpec(
            num_scalar_prefetch=1,
            grid=(1,),
            in_specs=[whole(a.shape) for a in acts] + [columns(b) for b in blocks],
            out_specs=[whole((3, cut, width)), whole((3, units - cut, width))],
        ),
        out_shape=[
            jax.ShapeDtypeStruct((3, cut, width), BF16),
            jax.ShapeDtypeStruct((3, units - cut, width), BF16),
        ],
        compiler_params=pltpu.CompilerParams(vmem_limit_bytes=VMEM_LIMIT),
        cost_estimate=pl.CostEstimate(
            flops=6 * units * tokens * width,
            bytes_accessed=2 * (tokens * (2 * width + 3 * units) + 3 * units * width),
            transcendentals=0,
        ),
        name="weight_terms",
    )(tile.reshape(1), *acts, *blocks)


def together(*values):
    return lax.optimization_barrier(values)


def line_body(
    hidden_in,
    cotangent,
    routes,
    gate_values,
    dense_gate,
    dense_up,
    dense_down,
    expert_gate,
    expert_up,
    expert_down,
):
    experts = lax.axis_size("tp")
    me = lax.axis_index("tp")
    ep = lax.axis_index("ep")
    core, chip = lax.rem(ep, 2), lax.div(ep, 2)
    half = dense_gate.shape[0] // 2
    columns = dense_down.shape[1]
    own = jnp.stack([hidden_in, cotangent])

    down = lax.all_gather(dense_down, "ep", axis=1, tiled=True)

    def across(value, apart):
        return lax.ppermute(value, "ep", [(i, i ^ apart) for i in range(8)])

    def add(a, b):
        return (a.astype(F32) + b.astype(F32)).astype(BF16)

    def dense(blocks):
        mine, other, partial = dense_block(core, blocks, dense_gate, dense_up, down)
        tokens = [*blocks, *(across(b, 1) for b in blocks)]
        return ([mine, across(other, 1)], tokens), partial

    right1 = lax.ppermute(own, "tp", [(0, 1), (1, 2), (2, 3)])
    left1 = lax.ppermute(own, "tp", [(1, 0), (2, 1), (3, 2)])
    dispatch, weight = slot_tables(routes, gate_values, me, experts)
    sent = slots_to_send(hidden_in, cotangent, dispatch, weight, experts)

    right1, left1, down, sent = together(right1, left1, down, sent)
    got = exchange_slots(sent, experts)
    right2 = lax.ppermute(right1, "tp", [(1, 2), (2, 3)])
    left2 = lax.ppermute(left1, "tp", [(2, 1), (1, 0)])
    slots = lax.all_gather(got, "ep", axis=0, tiled=False)
    first = jnp.where(me == 3, right1, left1)
    both01, partial01 = dense([own, first])

    second = jnp.where(me < 2, left2, right2)
    second, partial01, slots = together(second, partial01, slots)
    ends = lax.ppermute(second, "tp", [(1, 0), (2, 3)])
    both2, partial2 = dense([second])
    slots, partial2 = together(slots, partial2)
    slot_rows, slot_cot = slots[:, 0].reshape(-1, hidden_in.shape[1]), slots[:, 1].reshape(
        -1, hidden_in.shape[1]
    )
    g_gate, g_up, g_down, slot_terms = expert_block(
        slot_rows, slot_cot, expert_gate[0], expert_up[0], expert_down[0]
    )
    in_right = lax.ppermute(partial2, "tp", [(0, 1), (1, 2)])
    in_left = lax.ppermute(partial2, "tp", [(3, 2), (2, 1)])

    third = jnp.where((me == 0) | (me == 3), ends, right1)
    acts2, tokens2 = both2
    third, slot_terms, both01, tokens2 = together(third, slot_terms, both01, tokens2)
    both2 = (acts2, tokens2)
    partial0, partial1 = jnp.split(partial01, 2, axis=0)
    both3, partial3 = dense([third])
    partial3, in_right, in_left = together(partial3, in_right, in_left)
    from_left = lax.ppermute(add(partial1, in_right), "tp", [(0, 1), (1, 2), (2, 3)])
    far = lax.ppermute(partial3, "tp", [(0, 3), (3, 0)])
    from_right = lax.ppermute(
        add(jnp.where(me == 3, partial1, partial3), in_left), "tp", [(3, 2), (2, 1), (1, 0)]
    )

    acts, tokens = (a + b + c for a, b, c in zip(both01, both2, both3))
    cut = -(-half // 32) * 16
    made = {
        apart: weight_terms(
            jnp.bitwise_xor(chip, apart), acts, tokens, 2 * columns, cut
        )
        for apart in (3, 1, 2, 0)
    }
    low = across(made[3][0], 2)
    high = across(made[3][1], 4)
    low_own = across(made[1][0], 2)
    high_own = across(made[2][1], 4)
    routed = lax.psum_scatter(slot_terms, "ep", scatter_dimension=0, tiled=True)
    low_own, high_own, from_left, from_right, far, routed = together(
        low_own, high_own, from_left, from_right, far, routed
    )
    routed_input = slots_back(routed, dispatch, experts)
    low = across(add(made[2][0], low), 4)
    high = across(add(made[1][1], high), 2)
    total = jnp.concatenate(
        [
            made[0][0].astype(F32) + low_own.astype(F32) + low.astype(F32),
            made[0][1].astype(F32) + high_own.astype(F32) + high.astype(F32),
        ],
        axis=1,
    ).astype(BF16)
    own = lax.dynamic_slice_in_dim(total, core * columns, columns, axis=2)
    other = lax.dynamic_slice_in_dim(total, (1 - core) * columns, columns, axis=2)
    other = across(other, 1)
    grads = [
        jnp.where(
            core == 0,
            jnp.concatenate([own[i], other[i]], axis=0),
            jnp.concatenate([other[i], own[i]], axis=0),
        )
        for i in range(3)
    ]
    grad_input = (
        partial0.astype(F32)
        + from_left.astype(F32)
        + from_right.astype(F32)
        + far.astype(F32)
        + routed_input
    ).astype(BF16)
    return (grad_input, grads[1], grads[2], grads[0], g_gate[None], g_up[None], g_down[None])


def general_body(
    hidden_in,
    cotangent,
    routes,
    gate_values,
    dense_gate,
    dense_up,
    dense_down,
    expert_gate,
    expert_up,
    expert_down,
):
    experts = lax.axis_size("tp")
    me = lax.axis_index("tp")
    dispatch, weight = slot_tables(routes, gate_values, me, experts)
    sent = slots_to_send(hidden_in, cotangent, dispatch, weight, experts)
    got = exchange_slots(sent, experts)
    slots = lax.all_gather(got, "ep", axis=0, tiled=False)
    slot_rows, slot_cot = slots[:, 0].reshape(-1, hidden_in.shape[1]), slots[:, 1].reshape(
        -1, hidden_in.shape[1]
    )
    rows = lax.all_gather(hidden_in, "tp", axis=0, tiled=True)
    cots = lax.all_gather(cotangent, "tp", axis=0, tiled=True)
    down = lax.all_gather(dense_down, "ep", axis=1, tiled=True)
    act, grad_gate, grad_up, partial = plain_block(rows, cots, dense_gate, dense_up, down)
    dense_input = lax.psum_scatter(partial, "tp", scatter_dimension=0, tiled=True)
    grads = [
        lax.psum_scatter(
            lax.dot_general(a, b, LEADING, preferred_element_type=F32).astype(BF16),
            "ep",
            scatter_dimension=1,
            tiled=True,
        )
        for a, b in ((act, cots), (grad_gate, rows), (grad_up, rows))
    ]
    g_gate, g_up, g_down, slot_terms = expert_layer(
        slot_rows, slot_cot, expert_gate[0], expert_up[0], expert_down[0]
    )
    routed = lax.psum_scatter(slot_terms, "ep", scatter_dimension=0, tiled=True)
    routed_input = slots_back(routed, dispatch, experts)
    grad_input = (dense_input.astype(F32) + routed_input).astype(BF16)
    return (grad_input, grads[1], grads[2], grads[0], g_gate[None], g_up[None], g_down[None])


def solution(mesh):
    placed = (
        P(("ep", "tp"), None),
        P(("ep", "tp"), None),
        P(("ep", "tp"), None),
        P(("ep", "tp"), None),
        P("tp", None),
        P("tp", None),
        P("tp", "ep"),
        P("tp", "ep", None),
        P("tp", "ep", None),
        P("tp", "ep", None),
    )
    in_line = mesh.shape["tp"] == 4 and mesh.shape["ep"] == 8
    return jax.shard_map(
        line_body if in_line else general_body,
        mesh=mesh,
        in_specs=placed,
        out_specs=(
            P(("ep", "tp"), None),
            P("tp", "ep"),
            P("tp", "ep"),
            P("tp", "ep"),
            P("tp", "ep", None),
            P("tp", "ep", None),
            P("tp", "ep", None),
        ),
        check_vma=False,
    )
```

```python
import jax
import jax.numpy as jnp
from jax import lax
from jax.experimental import pallas as pl
from jax.experimental.pallas import tpu as pltpu
from jax.sharding import PartitionSpec as P

CAP = 4
CONTRACT = (((1,), (1,)), ((), ()))
LEADING = (((0,), (0,)), ((), ()))
F32 = jnp.float32
BF16 = jnp.bfloat16


def swiglu_backward(gate_pre, up_pre, grad_act):
    sigmoid_gate = jax.nn.sigmoid(gate_pre)
    silu_gate = gate_pre * sigmoid_gate
    act = (silu_gate * up_pre).astype(BF16)
    silu_slope = sigmoid_gate * (1.0 + gate_pre * (1.0 - sigmoid_gate))
    grad_gate = (grad_act * up_pre * silu_slope).astype(BF16)
    grad_up = (grad_act * silu_gate).astype(BF16)
    return act, grad_gate, grad_up


def slot_tables(routes, gate_values, me, experts):
    tok_count = routes.shape[0]
    named = lax.rem(me + jnp.arange(experts, dtype=jnp.int32), experts)
    onehot = (routes.reshape(-1)[:, None] == named[None, :]).astype(jnp.int32)
    before = jnp.cumsum(onehot, axis=0) - onehot
    slot = onehot[:, :, None] * (before[:, :, None] == jnp.arange(CAP, dtype=jnp.int32)).astype(
        jnp.int32
    )
    slot = slot.reshape(tok_count, 2, experts * CAP).astype(F32)
    dispatch = jnp.sum(slot, axis=1).T.astype(BF16)
    weight = jnp.sum(slot * gate_values[:, :, None], axis=(0, 1))
    return dispatch, weight


def shift(x, axis, size, by):
    return lax.ppermute(x, axis, [(i, (i + by) % size) for i in range(size)])


def slots_to_send(hidden_in, cotangent, dispatch, weight, experts):
    width = hidden_in.shape[1]
    rows = jnp.dot(dispatch, hidden_in, preferred_element_type=F32).astype(BF16)
    cots = jnp.dot(dispatch, cotangent, preferred_element_type=F32)
    cots = (cots * weight[:, None]).astype(BF16)
    return jnp.stack(
        [rows.reshape(experts, CAP, width), cots.reshape(experts, CAP, width)], axis=1
    )


def exchange_slots(sent, experts):
    width = sent.shape[3]
    got = jnp.stack([sent[0]] + [shift(sent[k], "tp", experts, k) for k in range(1, experts)])
    return got.transpose(1, 0, 2, 3).reshape(2, experts * CAP, width)


def expert_layer(slot_rows, slot_cot, gate_weight, up_weight, down_weight):
    e_gate = lax.dot_general(slot_rows, gate_weight, CONTRACT, preferred_element_type=F32)
    e_up = lax.dot_general(slot_rows, up_weight, CONTRACT, preferred_element_type=F32)
    e_grad_act = lax.dot_general(slot_cot, down_weight, CONTRACT, preferred_element_type=F32)
    e_act, e_grad_gate, e_grad_up = swiglu_backward(e_gate, e_up, e_grad_act)
    g_down = lax.dot_general(e_act, slot_cot, LEADING, preferred_element_type=F32).astype(BF16)
    g_gate = lax.dot_general(e_grad_gate, slot_rows, LEADING, preferred_element_type=F32).astype(
        BF16
    )
    g_up = lax.dot_general(e_grad_up, slot_rows, LEADING, preferred_element_type=F32).astype(BF16)
    terms = jnp.dot(e_grad_gate, gate_weight, preferred_element_type=F32) + jnp.dot(
        e_grad_up, up_weight, preferred_element_type=F32
    )
    return g_gate, g_up, g_down, terms.astype(BF16)


def slots_back(own, dispatch, experts):
    width = own.shape[1]
    own = own.reshape(experts, CAP, width)
    back = jnp.stack([own[0]] + [shift(own[k], "tp", experts, -k) for k in range(1, experts)])
    return lax.dot_general(
        dispatch, back.reshape(experts * CAP, width), LEADING, preferred_element_type=F32
    )


def plain_block(rows, cot, gate, up, down):
    gate_pre = lax.dot_general(rows, gate, CONTRACT, preferred_element_type=F32)
    up_pre = lax.dot_general(rows, up, CONTRACT, preferred_element_type=F32)
    grad_act = lax.dot_general(cot, down, CONTRACT, preferred_element_type=F32)
    act, grad_gate, grad_up = swiglu_backward(gate_pre, up_pre, grad_act)
    partial = jnp.dot(grad_gate, gate, preferred_element_type=F32) + jnp.dot(
        grad_up, up, preferred_element_type=F32
    )
    return act, grad_gate, grad_up, partial.astype(BF16)


VMEM_LIMIT = 24 * 1024 * 1024


def unit_tiles(units):
    return [(start, min(256, units - start)) for start in range(0, units, 256)]


def layer_kernel(rows, cots, gate, up, down, down_turned, turned, partial, col):
    units, width = gate.shape
    for start, size in unit_tiles(units):
        gate_pre, up_pre = [
            lax.dot_general(w[start : start + size], rows, CONTRACT, preferred_element_type=F32)
            for w in (gate, up)
        ]
        if down_turned:
            grad_act = jnp.dot(
                cots, down[:, start : start + size], preferred_element_type=F32
            ).T
        else:
            grad_act = lax.dot_general(
                down[start : start + size], cots, CONTRACT, preferred_element_type=F32
            )
        for i, value in enumerate(swiglu_backward(gate_pre, up_pre, grad_act)):
            turned[i, start : start + size] = value
    grads = [turned[1].T, turned[2].T]
    for j in range(0, width, col):
        partial[:, j : j + col] = (
            jnp.dot(grads[0], gate[:, j : j + col], preferred_element_type=F32)
            + jnp.dot(grads[1], up[:, j : j + col], preferred_element_type=F32)
        ).astype(BF16)


def dense_block(core, blocks, gate, up, down):
    tok, width = blocks[0].shape[1] * len(blocks), blocks[0].shape[2]
    units = gate.shape[0]
    half = units // 2

    def kernel(core_ref, *refs):
        ins, refs = refs[: len(blocks)], refs[len(blocks) :]
        gate, up, down, own, other, partial, turned = refs
        rows, cots = [
            ins[0][k]
            if len(ins) == 1
            else jnp.concatenate([ref[k] for ref in ins], axis=0)
            for k in range(2)
        ]
        layer_kernel(rows, cots, gate, up, down, True, turned, partial, 512)
        mine = core_ref[0]
        own[...] = turned[:, pl.ds(pl.multiple_of(mine * half, 16), half), :]
        other[...] = turned[:, pl.ds(pl.multiple_of((1 - mine) * half, 16), half), :]

    vmem = pl.BlockSpec(memory_space=pltpu.VMEM)
    return pl.pallas_call(
        kernel,
        in_specs=[pl.BlockSpec(memory_space=pltpu.SMEM)] + [vmem] * (len(blocks) + 3),
        out_specs=[vmem, vmem, vmem],
        out_shape=[
            jax.ShapeDtypeStruct((3, half, tok), BF16),
            jax.ShapeDtypeStruct((3, half, tok), BF16),
            jax.ShapeDtypeStruct((tok, width), BF16),
        ],
        scratch_shapes=[pltpu.VMEM((3, units, tok), BF16)],
        compiler_params=pltpu.CompilerParams(vmem_limit_bytes=VMEM_LIMIT),
        cost_estimate=pl.CostEstimate(
            flops=10 * units * width * tok,
            bytes_accessed=6 * units * width + 6 * tok * (width + units),
            transcendentals=units * tok,
        ),
        name="dense_block",
    )(core.reshape(1), *blocks, gate, up, down)


def expert_block(rows, cots, gate, up, down):
    tok, width = rows.shape
    units = gate.shape[0]
    col = width // 4

    def kernel(
        rows, cots, gate, up, down, g_gate, g_up, g_down, partial, turned, made, out_sems
    ):
        layer_kernel(rows[...], cots[...], gate, up, down, False, turned, partial, 512)
        outs = (g_down, g_gate, g_up)
        pending = [None, None]
        step = 0
        for i in range(3):
            right = cots if i == 0 else rows
            for j in range(0, width, col):
                slot = step % 2
                if pending[slot] is not None:
                    pending[slot].wait()
                made[slot] = jnp.dot(
                    turned[i], right[:, j : j + col], preferred_element_type=F32
                ).astype(BF16)
                copy = pltpu.make_async_copy(
                    made.at[slot], outs[i].at[:, pl.ds(j, col)], out_sems.at[slot]
                )
                copy.start()
                pending[slot] = copy
                step += 1
        for copy in pending:
            copy.wait()

    vmem = pl.BlockSpec(memory_space=pltpu.VMEM)
    hbm = pl.BlockSpec(memory_space=pl.ANY)
    grad = jax.ShapeDtypeStruct((units, width), BF16)
    return pl.pallas_call(
        kernel,
        in_specs=[vmem] * 5,
        out_specs=[hbm, hbm, hbm, vmem],
        out_shape=[grad, grad, grad, jax.ShapeDtypeStruct((tok, width), BF16)],
        scratch_shapes=[
            pltpu.VMEM((3, units, tok), BF16),
            pltpu.VMEM((2, units, col), BF16),
            pltpu.SemaphoreType.DMA((2,)),
        ],
        compiler_params=pltpu.CompilerParams(vmem_limit_bytes=VMEM_LIMIT),
        cost_estimate=pl.CostEstimate(
            flops=16 * units * width * tok,
            bytes_accessed=12 * units * width + 6 * tok * width,
            transcendentals=units * tok,
        ),
        name="expert_block",
    )(rows, cots, gate, up, down)


def final_sum(core, lows, highs):
    count = len(lows)
    _, cut, width = lows[0].shape
    units = cut + highs[0].shape[1]
    half = width // 2

    def kernel(core_ref, *refs):
        ins, (mine, other) = refs[:-2], refs[-2:]
        own_first = core_ref[0] == 0
        for i in range(3):
            for begin, group in ((0, ins[:count]), (cut, ins[count:])):
                total = group[0][i].astype(F32)
                for ref in group[1:]:
                    total = total + ref[i].astype(F32)
                left, right = total[:, :half].astype(BF16), total[:, half:].astype(BF16)
                size = total.shape[0]
                mine[i, begin : begin + size] = jnp.where(own_first, left, right)
                other[i, begin : begin + size] = jnp.where(own_first, right, left)

    vmem = pl.BlockSpec(memory_space=pltpu.VMEM)
    shape = jax.ShapeDtypeStruct((3, units, half), BF16)
    return pl.pallas_call(
        kernel,
        in_specs=[pl.BlockSpec(memory_space=pltpu.SMEM)] + [vmem] * (2 * count),
        out_specs=[vmem, vmem],
        out_shape=[shape, shape],
        compiler_params=pltpu.CompilerParams(vmem_limit_bytes=VMEM_LIMIT),
        cost_estimate=pl.CostEstimate(
            flops=3 * count * units * width,
            bytes_accessed=6 * (count + 1) * units * width,
            transcendentals=0,
        ),
        name="final_sum",
    )(core.reshape(1), *lows, *highs)


def join_halves(core, mine, other):
    _, units, width = mine.shape

    def kernel(core_ref, mine, other, *outs):
        me = core_ref[0]
        for i in range(3):
            outs[i][pl.ds(pl.multiple_of(me * units, 16), units), :] = mine[i]
            outs[i][pl.ds(pl.multiple_of((1 - me) * units, 16), units), :] = other[i]

    vmem = pl.BlockSpec(memory_space=pltpu.VMEM)
    return pl.pallas_call(
        kernel,
        in_specs=[pl.BlockSpec(memory_space=pltpu.SMEM), vmem, vmem],
        out_specs=[vmem] * 3,
        out_shape=[jax.ShapeDtypeStruct((2 * units, width), BF16)] * 3,
        compiler_params=pltpu.CompilerParams(vmem_limit_bytes=VMEM_LIMIT),
        cost_estimate=pl.CostEstimate(
            flops=0, bytes_accessed=24 * units * width, transcendentals=0
        ),
        name="join_halves",
    )(core.reshape(1), mine, other)


def weight_terms(tile, acts, blocks, width, cut):
    units = acts[0].shape[1]
    tokens = sum(b.shape[1] for b in blocks)

    def kernel(tile_ref, *refs):
        a, b = refs[: len(acts)], refs[len(acts) : -2]
        low, high = refs[-2:]
        rows = jnp.concatenate([ref[0] for ref in b], axis=0)
        cots = jnp.concatenate([ref[1] for ref in b], axis=0)
        for i in range(3):
            left = jnp.concatenate([ref[i] for ref in a], axis=1)
            made = jnp.dot(left, cots if i == 0 else rows, preferred_element_type=F32).astype(BF16)
            low[i] = made[:cut]
            high[i] = made[cut:]

    def whole(shape):
        return pl.BlockSpec(shape, lambda i, tile_ref: (0, 0, 0))

    def columns(block):
        return pl.BlockSpec((*block.shape[:2], width), lambda i, tile_ref: (0, 0, tile_ref[0]))

    return pl.pallas_call(
        kernel,
        grid_spec=pltpu.PrefetchScalarGridSpec(
            num_scalar_prefetch=1,
            grid=(1,),
            in_specs=[whole(a.shape) for a in acts] + [columns(b) for b in blocks],
            out_specs=[whole((3, cut, width)), whole((3, units - cut, width))],
        ),
        out_shape=[
            jax.ShapeDtypeStruct((3, cut, width), BF16),
            jax.ShapeDtypeStruct((3, units - cut, width), BF16),
        ],
        compiler_params=pltpu.CompilerParams(vmem_limit_bytes=VMEM_LIMIT),
        cost_estimate=pl.CostEstimate(
            flops=6 * units * tokens * width,
            bytes_accessed=2 * (tokens * (2 * width + 3 * units) + 3 * units * width),
            transcendentals=0,
        ),
        name="weight_terms",
    )(tile.reshape(1), *acts, *blocks)


def together(*values):
    return lax.optimization_barrier(values)


def line_body(
    hidden_in,
    cotangent,
    routes,
    gate_values,
    dense_gate,
    dense_up,
    dense_down,
    expert_gate,
    expert_up,
    expert_down,
):
    experts = lax.axis_size("tp")
    me = lax.axis_index("tp")
    ep = lax.axis_index("ep")
    core, chip = lax.rem(ep, 2), lax.div(ep, 2)
    half = dense_gate.shape[0] // 2
    columns = dense_down.shape[1]
    own = jnp.stack([hidden_in, cotangent])

    down = lax.all_gather(dense_down.T, "ep", axis=0, tiled=True)

    def across(value, apart):
        return lax.ppermute(value, "ep", [(i, i ^ apart) for i in range(8)])

    def add(a, b):
        return (a.astype(F32) + b.astype(F32)).astype(BF16)

    def dense(blocks):
        mine, other, partial = dense_block(core, blocks, dense_gate, dense_up, down)
        tokens = [*blocks, *(across(b, 1) for b in blocks)]
        return ([mine, across(other, 1)], tokens), partial

    right1 = lax.ppermute(own, "tp", [(0, 1), (1, 2), (2, 3)])
    left1 = lax.ppermute(own, "tp", [(1, 0), (2, 1), (3, 2)])
    dispatch, weight = slot_tables(routes, gate_values, me, experts)
    sent = slots_to_send(hidden_in, cotangent, dispatch, weight, experts)

    right1, left1, down, sent = together(right1, left1, down, sent)
    got = exchange_slots(sent, experts)
    right2 = lax.ppermute(right1, "tp", [(1, 2), (2, 3)])
    left2 = lax.ppermute(left1, "tp", [(2, 1), (1, 0)])
    first = jnp.where(me < 2, left1, right1)
    both01, partial01 = dense([own, first])
    got, partial01 = together(got, partial01)
    slots = lax.all_gather(got, "ep", axis=0, tiled=False)

    right2, left2, partial01 = together(right2, left2, partial01)
    third = lax.ppermute(
        jnp.where(me == 1, left2, jnp.where(me == 2, right2, own)),
        "tp",
        [(1, 0), (2, 3), (0, 1), (3, 2)],
    )
    second = jnp.where(me < 2, left2, right2)
    both2, partial2 = dense([second])
    slots, partial2 = together(slots, partial2)
    slot_rows, slot_cot = slots[:, 0].reshape(-1, hidden_in.shape[1]), slots[:, 1].reshape(
        -1, hidden_in.shape[1]
    )
    g_gate, g_up, g_down, slot_terms = expert_block(
        slot_rows, slot_cot, expert_gate[0], expert_up[0], expert_down[0]
    )
    in_right = lax.ppermute(partial2, "tp", [(0, 1), (1, 2)])
    in_left = lax.ppermute(partial2, "tp", [(3, 2), (2, 1)])

    acts2, tokens2 = both2
    third, slot_terms, both01, tokens2 = together(third, slot_terms, both01, tokens2)
    both2 = (acts2, tokens2)
    partial0, partial1 = jnp.split(partial01, 2, axis=0)
    both3, partial3 = dense([third])
    partial3, in_right, in_left = together(partial3, in_right, in_left)
    far = lax.ppermute(partial3, "tp", [(0, 3), (3, 0)])
    from_left = lax.ppermute(
        add(jnp.where(me == 2, partial3, partial1), in_right), "tp", [(0, 1), (1, 2), (2, 3)]
    )
    from_right = lax.ppermute(
        add(jnp.where(me == 1, partial3, partial1), in_left), "tp", [(3, 2), (2, 1), (1, 0)]
    )

    acts, tokens = (a + b + c for a, b, c in zip(both01, both2, both3))
    cut = -(-half // 32) * 16
    made = {
        apart: weight_terms(
            jnp.bitwise_xor(chip, apart), acts, tokens, 2 * columns, cut
        )
        for apart in (3, 1, 2, 0)
    }
    low = across(made[3][0], 2)
    high = across(made[3][1], 4)
    low_own = across(made[1][0], 2)
    high_own = across(made[2][1], 4)
    routed = lax.psum_scatter(slot_terms, "ep", scatter_dimension=0, tiled=True)
    low, high, from_left, from_right, far, routed = together(
        low, high, from_left, from_right, far, routed
    )
    routed_input = slots_back(routed, dispatch, experts)
    low = across(add(made[2][0], low), 4)
    high = across(add(made[1][1], high), 2)
    mine, other = final_sum(
        core, (made[0][0], low_own, low), (made[0][1], high_own, high)
    )
    grads = join_halves(core, mine, across(other, 1))
    grad_input = (
        partial0.astype(F32)
        + from_left.astype(F32)
        + from_right.astype(F32)
        + far.astype(F32)
        + routed_input
    ).astype(BF16)
    return (grad_input, grads[1], grads[2], grads[0], g_gate[None], g_up[None], g_down[None])


def general_body(
    hidden_in,
    cotangent,
    routes,
    gate_values,
    dense_gate,
    dense_up,
    dense_down,
    expert_gate,
    expert_up,
    expert_down,
):
    experts = lax.axis_size("tp")
    me = lax.axis_index("tp")
    dispatch, weight = slot_tables(routes, gate_values, me, experts)
    sent = slots_to_send(hidden_in, cotangent, dispatch, weight, experts)
    got = exchange_slots(sent, experts)
    slots = lax.all_gather(got, "ep", axis=0, tiled=False)
    slot_rows, slot_cot = slots[:, 0].reshape(-1, hidden_in.shape[1]), slots[:, 1].reshape(
        -1, hidden_in.shape[1]
    )
    rows = lax.all_gather(hidden_in, "tp", axis=0, tiled=True)
    cots = lax.all_gather(cotangent, "tp", axis=0, tiled=True)
    down = lax.all_gather(dense_down, "ep", axis=1, tiled=True)
    act, grad_gate, grad_up, partial = plain_block(rows, cots, dense_gate, dense_up, down)
    dense_input = lax.psum_scatter(partial, "tp", scatter_dimension=0, tiled=True)
    grads = [
        lax.psum_scatter(
            lax.dot_general(a, b, LEADING, preferred_element_type=F32).astype(BF16),
            "ep",
            scatter_dimension=1,
            tiled=True,
        )
        for a, b in ((act, cots), (grad_gate, rows), (grad_up, rows))
    ]
    g_gate, g_up, g_down, slot_terms = expert_layer(
        slot_rows, slot_cot, expert_gate[0], expert_up[0], expert_down[0]
    )
    routed = lax.psum_scatter(slot_terms, "ep", scatter_dimension=0, tiled=True)
    routed_input = slots_back(routed, dispatch, experts)
    grad_input = (dense_input.astype(F32) + routed_input).astype(BF16)
    return (grad_input, grads[1], grads[2], grads[0], g_gate[None], g_up[None], g_down[None])


def solution(mesh):
    placed = (
        P(("ep", "tp"), None),
        P(("ep", "tp"), None),
        P(("ep", "tp"), None),
        P(("ep", "tp"), None),
        P("tp", None),
        P("tp", None),
        P("tp", "ep"),
        P("tp", "ep", None),
        P("tp", "ep", None),
        P("tp", "ep", None),
    )
    in_line = mesh.shape["tp"] == 4 and mesh.shape["ep"] == 8
    return jax.shard_map(
        line_body if in_line else general_body,
        mesh=mesh,
        in_specs=placed,
        out_specs=(
            P(("ep", "tp"), None),
            P("tp", "ep"),
            P("tp", "ep"),
            P("tp", "ep"),
            P("tp", "ep", None),
            P("tp", "ep", None),
            P("tp", "ep", None),
        ),
        check_vma=False,
    )
```

```python
import jax
import jax.numpy as jnp
from jax import lax
from jax.experimental import pallas as pl
from jax.experimental.pallas import tpu as pltpu
from jax.sharding import PartitionSpec as P

CAP = 4
CONTRACT = (((1,), (1,)), ((), ()))
LEADING = (((0,), (0,)), ((), ()))
F32 = jnp.float32
BF16 = jnp.bfloat16


def swiglu_backward(gate_pre, up_pre, grad_act):
    sigmoid_gate = jax.nn.sigmoid(gate_pre)
    silu_gate = gate_pre * sigmoid_gate
    act = (silu_gate * up_pre).astype(BF16)
    silu_slope = sigmoid_gate * (1.0 + gate_pre * (1.0 - sigmoid_gate))
    grad_gate = (grad_act * up_pre * silu_slope).astype(BF16)
    grad_up = (grad_act * silu_gate).astype(BF16)
    return act, grad_gate, grad_up


def slot_tables(routes, gate_values, me, experts):
    tok_count = routes.shape[0]
    named = lax.rem(me + jnp.arange(experts, dtype=jnp.int32), experts)
    onehot = (routes.reshape(-1)[:, None] == named[None, :]).astype(jnp.int32)
    before = jnp.cumsum(onehot, axis=0) - onehot
    slot = onehot[:, :, None] * (before[:, :, None] == jnp.arange(CAP, dtype=jnp.int32)).astype(
        jnp.int32
    )
    slot = slot.reshape(tok_count, 2, experts * CAP).astype(F32)
    dispatch = jnp.sum(slot, axis=1).T.astype(BF16)
    weight = jnp.sum(slot * gate_values[:, :, None], axis=(0, 1))
    return dispatch, weight


def shift(x, axis, size, by):
    return lax.ppermute(x, axis, [(i, (i + by) % size) for i in range(size)])


def slots_to_send(hidden_in, cotangent, dispatch, weight, experts):
    width = hidden_in.shape[1]
    rows = jnp.dot(dispatch, hidden_in, preferred_element_type=F32).astype(BF16)
    cots = jnp.dot(dispatch, cotangent, preferred_element_type=F32)
    cots = (cots * weight[:, None]).astype(BF16)
    return jnp.stack(
        [rows.reshape(experts, CAP, width), cots.reshape(experts, CAP, width)], axis=1
    )


def exchange_slots(sent, me, experts):
    width = sent.shape[3]
    sent = jnp.roll(sent, me, axis=0)
    got = lax.all_to_all(sent, "tp", split_axis=0, concat_axis=0, tiled=True)
    return got.transpose(1, 0, 2, 3).reshape(2, experts * CAP, width)


def expert_layer(slot_rows, slot_cot, gate_weight, up_weight, down_weight):
    e_gate = lax.dot_general(slot_rows, gate_weight, CONTRACT, preferred_element_type=F32)
    e_up = lax.dot_general(slot_rows, up_weight, CONTRACT, preferred_element_type=F32)
    e_grad_act = lax.dot_general(slot_cot, down_weight, CONTRACT, preferred_element_type=F32)
    e_act, e_grad_gate, e_grad_up = swiglu_backward(e_gate, e_up, e_grad_act)
    g_down = lax.dot_general(e_act, slot_cot, LEADING, preferred_element_type=F32).astype(BF16)
    g_gate = lax.dot_general(e_grad_gate, slot_rows, LEADING, preferred_element_type=F32).astype(
        BF16
    )
    g_up = lax.dot_general(e_grad_up, slot_rows, LEADING, preferred_element_type=F32).astype(BF16)
    terms = jnp.dot(e_grad_gate, gate_weight, preferred_element_type=F32) + jnp.dot(
        e_grad_up, up_weight, preferred_element_type=F32
    )
    return g_gate, g_up, g_down, terms.astype(BF16)


def slots_back(own, dispatch, me, experts):
    width = own.shape[1]
    own = own.reshape(experts, CAP, width)
    back = [
        lax.dynamic_index_in_dim(own, lax.rem(me - k + experts, experts), keepdims=False)
        for k in range(experts)
    ]
    back = jnp.stack(back[:1] + [shift(back[k], "tp", experts, -k) for k in range(1, experts)])
    return lax.dot_general(
        dispatch, back.reshape(experts * CAP, width), LEADING, preferred_element_type=F32
    )


def plain_block(rows, cot, gate, up, down):
    gate_pre = lax.dot_general(rows, gate, CONTRACT, preferred_element_type=F32)
    up_pre = lax.dot_general(rows, up, CONTRACT, preferred_element_type=F32)
    grad_act = lax.dot_general(cot, down, CONTRACT, preferred_element_type=F32)
    act, grad_gate, grad_up = swiglu_backward(gate_pre, up_pre, grad_act)
    partial = jnp.dot(grad_gate, gate, preferred_element_type=F32) + jnp.dot(
        grad_up, up, preferred_element_type=F32
    )
    return act, grad_gate, grad_up, partial.astype(BF16)


VMEM_LIMIT = 24 * 1024 * 1024


def unit_tiles(units):
    return [(start, min(256, units - start)) for start in range(0, units, 256)]


def layer_kernel(rows, cots, gate, up, down, down_turned, turned, partial, col):
    units, width = gate.shape
    for start, size in unit_tiles(units):
        gate_pre, up_pre = [
            lax.dot_general(w[start : start + size], rows, CONTRACT, preferred_element_type=F32)
            for w in (gate, up)
        ]
        if down_turned:
            grad_act = jnp.dot(
                cots, down[:, start : start + size], preferred_element_type=F32
            ).T
        else:
            grad_act = lax.dot_general(
                down[start : start + size], cots, CONTRACT, preferred_element_type=F32
            )
        for i, value in enumerate(swiglu_backward(gate_pre, up_pre, grad_act)):
            turned[i, start : start + size] = value
    grads = [turned[1].T, turned[2].T]
    for j in range(0, width, col):
        partial[:, j : j + col] = (
            jnp.dot(grads[0], gate[:, j : j + col], preferred_element_type=F32)
            + jnp.dot(grads[1], up[:, j : j + col], preferred_element_type=F32)
        ).astype(BF16)


def dense_block(core, rows, cots, gate, up, down):
    count = len(rows)
    tok, width = rows[0].shape[0] * count, rows[0].shape[1]
    units = gate.shape[0]
    half = units // 2

    def kernel(core_ref, *refs):
        ins, refs = refs[: 2 * count], refs[2 * count :]
        gate, up, down, own, other, partial, turned = refs
        rows, cots = [
            part[0][...]
            if count == 1
            else jnp.concatenate([ref[...] for ref in part], axis=0)
            for part in (ins[:count], ins[count:])
        ]
        layer_kernel(rows, cots, gate, up, down, True, turned, partial, 512)
        mine = core_ref[0]
        own[...] = turned[:, pl.ds(pl.multiple_of(mine * half, 16), half), :]
        other[...] = turned[:, pl.ds(pl.multiple_of((1 - mine) * half, 16), half), :]

    vmem = pl.BlockSpec(memory_space=pltpu.VMEM)
    return pl.pallas_call(
        kernel,
        in_specs=[pl.BlockSpec(memory_space=pltpu.SMEM)] + [vmem] * (2 * count + 3),
        out_specs=[vmem, vmem, vmem],
        out_shape=[
            jax.ShapeDtypeStruct((3, half, tok), BF16),
            jax.ShapeDtypeStruct((3, half, tok), BF16),
            jax.ShapeDtypeStruct((tok, width), BF16),
        ],
        scratch_shapes=[pltpu.VMEM((3, units, tok), BF16)],
        compiler_params=pltpu.CompilerParams(vmem_limit_bytes=VMEM_LIMIT),
        cost_estimate=pl.CostEstimate(
            flops=10 * units * width * tok,
            bytes_accessed=6 * units * width + 6 * tok * (width + units),
            transcendentals=units * tok,
        ),
        name="dense_block",
    )(core.reshape(1), *rows, *cots, gate, up, down)


def expert_block(rows, cots, gate, up, down):
    tok, width = rows.shape
    units = gate.shape[0]
    col = width // 4

    def kernel(
        rows, cots, gate, up, down, g_gate, g_up, g_down, partial, turned, made, out_sems
    ):
        layer_kernel(rows[...], cots[...], gate, up, down, False, turned, partial, 512)
        outs = (g_down, g_gate, g_up)
        pending = [None, None]
        step = 0
        for i in range(3):
            right = cots if i == 0 else rows
            for j in range(0, width, col):
                slot = step % 2
                if pending[slot] is not None:
                    pending[slot].wait()
                made[slot] = jnp.dot(
                    turned[i], right[:, j : j + col], preferred_element_type=F32
                ).astype(BF16)
                copy = pltpu.make_async_copy(
                    made.at[slot], outs[i].at[:, pl.ds(j, col)], out_sems.at[slot]
                )
                copy.start()
                pending[slot] = copy
                step += 1
        for copy in pending:
            copy.wait()

    vmem = pl.BlockSpec(memory_space=pltpu.VMEM)
    hbm = pl.BlockSpec(memory_space=pl.ANY)
    grad = jax.ShapeDtypeStruct((units, width), BF16)
    return pl.pallas_call(
        kernel,
        in_specs=[vmem] * 5,
        out_specs=[hbm, hbm, hbm, vmem],
        out_shape=[grad, grad, grad, jax.ShapeDtypeStruct((tok, width), BF16)],
        scratch_shapes=[
            pltpu.VMEM((3, units, tok), BF16),
            pltpu.VMEM((2, units, col), BF16),
            pltpu.SemaphoreType.DMA((2,)),
        ],
        compiler_params=pltpu.CompilerParams(vmem_limit_bytes=VMEM_LIMIT),
        cost_estimate=pl.CostEstimate(
            flops=16 * units * width * tok,
            bytes_accessed=12 * units * width + 6 * tok * width,
            transcendentals=units * tok,
        ),
        name="expert_block",
    )(rows, cots, gate, up, down)


def final_sum(core, lows, highs):
    count = len(lows)
    _, cut, width = lows[0].shape
    units = cut + highs[0].shape[1]
    half = width // 2

    def kernel(core_ref, *refs):
        ins, (mine, other) = refs[:-2], refs[-2:]
        own_first = core_ref[0] == 0
        for i in range(3):
            for begin, group in ((0, ins[:count]), (cut, ins[count:])):
                total = group[0][i].astype(F32)
                for ref in group[1:]:
                    total = total + ref[i].astype(F32)
                left, right = total[:, :half].astype(BF16), total[:, half:].astype(BF16)
                size = total.shape[0]
                mine[i, begin : begin + size] = jnp.where(own_first, left, right)
                other[i, begin : begin + size] = jnp.where(own_first, right, left)

    vmem = pl.BlockSpec(memory_space=pltpu.VMEM)
    shape = jax.ShapeDtypeStruct((3, units, half), BF16)
    return pl.pallas_call(
        kernel,
        in_specs=[pl.BlockSpec(memory_space=pltpu.SMEM)] + [vmem] * (2 * count),
        out_specs=[vmem, vmem],
        out_shape=[shape, shape],
        compiler_params=pltpu.CompilerParams(vmem_limit_bytes=VMEM_LIMIT),
        cost_estimate=pl.CostEstimate(
            flops=3 * count * units * width,
            bytes_accessed=6 * (count + 1) * units * width,
            transcendentals=0,
        ),
        name="final_sum",
    )(core.reshape(1), *lows, *highs)


def join_halves(core, mine, other):
    _, units, width = mine.shape

    def kernel(core_ref, mine, other, *refs):
        outs, sems = refs[:3], refs[3]
        me = core_ref[0]
        copies = []
        for i in range(3):
            for k, (source, place) in enumerate(((mine, me), (other, 1 - me))):
                rows = pl.ds(pl.multiple_of(place * units, 16), units)
                copies.append(
                    pltpu.make_async_copy(source.at[i], outs[i].at[rows], sems.at[i, k])
                )
        for copy in copies:
            copy.start()
        for copy in copies:
            copy.wait()

    anywhere = pl.BlockSpec(memory_space=pl.ANY)
    return pl.pallas_call(
        kernel,
        in_specs=[pl.BlockSpec(memory_space=pltpu.SMEM), anywhere, anywhere],
        out_specs=[anywhere] * 3,
        out_shape=[jax.ShapeDtypeStruct((2 * units, width), BF16)] * 3,
        scratch_shapes=[pltpu.SemaphoreType.DMA((3, 2))],
        compiler_params=pltpu.CompilerParams(vmem_limit_bytes=60 * 1024 * 1024),
        cost_estimate=pl.CostEstimate(
            flops=0, bytes_accessed=24 * units * width, transcendentals=0
        ),
        name="join_halves",
    )(core.reshape(1), mine, other)


def weight_terms(tile, acts, rows, cots, width, cut):
    units = acts[0].shape[1]
    tokens = sum(r.shape[0] for r in rows)
    count = len(rows)

    def kernel(tile_ref, *refs):
        a, b = refs[: len(acts)], refs[len(acts) : -2]
        low, high = refs[-2:]
        rows = jnp.concatenate([ref[...] for ref in b[:count]], axis=0)
        cots = jnp.concatenate([ref[...] for ref in b[count:]], axis=0)
        for i in range(3):
            left = jnp.concatenate([ref[i] for ref in a], axis=1)
            made = jnp.dot(left, cots if i == 0 else rows, preferred_element_type=F32).astype(BF16)
            low[i] = made[:cut]
            high[i] = made[cut:]

    def whole(shape):
        return pl.BlockSpec(shape, lambda i, tile_ref: (0, 0, 0))

    def columns(block):
        return pl.BlockSpec((block.shape[0], width), lambda i, tile_ref: (0, tile_ref[0]))

    return pl.pallas_call(
        kernel,
        grid_spec=pltpu.PrefetchScalarGridSpec(
            num_scalar_prefetch=1,
            grid=(1,),
            in_specs=[whole(a.shape) for a in acts] + [columns(b) for b in (*rows, *cots)],
            out_specs=[whole((3, cut, width)), whole((3, units - cut, width))],
        ),
        out_shape=[
            jax.ShapeDtypeStruct((3, cut, width), BF16),
            jax.ShapeDtypeStruct((3, units - cut, width), BF16),
        ],
        compiler_params=pltpu.CompilerParams(vmem_limit_bytes=VMEM_LIMIT),
        cost_estimate=pl.CostEstimate(
            flops=6 * units * tokens * width,
            bytes_accessed=2 * (tokens * (2 * width + 3 * units) + 3 * units * width),
            transcendentals=0,
        ),
        name="weight_terms",
    )(tile.reshape(1), *acts, *rows, *cots)


def together(*values):
    return lax.optimization_barrier(values)


def line_body(
    hidden_in,
    cotangent,
    routes,
    gate_values,
    dense_gate,
    dense_up,
    dense_down,
    expert_gate,
    expert_up,
    expert_down,
):
    experts = lax.axis_size("tp")
    me = lax.axis_index("tp")
    ep = lax.axis_index("ep")
    core, chip = lax.rem(ep, 2), lax.div(ep, 2)
    half = dense_gate.shape[0] // 2
    columns = dense_down.shape[1]
    own = (hidden_in, cotangent)

    down = lax.all_gather(dense_down.T, "ep", axis=0, tiled=True)

    def along(values, pairs):
        return [lax.ppermute(v, "tp", pairs) for v in values]

    def across(value, apart):
        return lax.ppermute(value, "ep", [(i, i ^ apart) for i in range(8)])

    def add(a, b):
        return (a.astype(F32) + b.astype(F32)).astype(BF16)

    def dense(*blocks):
        rows, cots = [list(x) for x in zip(*blocks)]
        mine, other, partial = dense_block(core, rows, cots, dense_gate, dense_up, down)
        for group in (rows, cots):
            group += [across(x, 1) for x in group]
        return ([mine, across(other, 1)], rows, cots), partial

    right1 = along(own, [(0, 1), (1, 2), (2, 3)])
    left1 = along(own, [(1, 0), (2, 1), (3, 2)])
    dispatch, weight = slot_tables(routes, gate_values, me, experts)
    sent = slots_to_send(hidden_in, cotangent, dispatch, weight, experts)

    got = exchange_slots(sent, me, experts)

    right1[1], left1[1], down = together(right1[1], left1[1], down)
    right2 = along(right1, [(1, 2), (2, 3)])
    left2 = along(left1, [(2, 1), (1, 0)])
    first = [jnp.where(me < 2, a, b) for a, b in zip(left1, right1)]
    both01, partial01 = dense(own, first)
    slots = lax.all_gather(got, "ep", axis=0, tiled=False)
    slots, partial01 = together(slots, partial01)
    slot_rows, slot_cot = slots[:, 0].reshape(-1, hidden_in.shape[1]), slots[:, 1].reshape(
        -1, hidden_in.shape[1]
    )
    g_gate, g_up, g_down, slot_terms = expert_block(
        slot_rows, slot_cot, expert_gate[0], expert_up[0], expert_down[0]
    )

    right2[1], left2[1], partial01, slot_terms = together(
        right2[1], left2[1], partial01, slot_terms
    )
    routed = lax.psum_scatter(slot_terms, "ep", scatter_dimension=0, tiled=True)
    third = along(
        [
            jnp.where(me == 1, a, jnp.where(me == 2, b, c))
            for a, b, c in zip(left2, right2, own)
        ],
        [(1, 0), (2, 3), (0, 1), (3, 2)],
    )
    second = [jnp.where(me < 2, a, b) for a, b in zip(left2, right2)]
    both2, partial2 = dense(second)
    in_right = lax.ppermute(partial2, "tp", [(0, 1), (1, 2)])
    in_left = lax.ppermute(partial2, "tp", [(3, 2), (2, 1)])

    third, partial2, both01, both2, routed = together(third, partial2, both01, both2, routed)
    partial0, partial1 = jnp.split(partial01, 2, axis=0)
    both3, partial3 = dense(third)
    far = lax.ppermute(partial3, "tp", [(0, 3), (3, 0)])
    to_right = add(jnp.where(me == 2, partial3, partial1), in_right)
    to_left = add(jnp.where(me == 1, partial3, partial1), in_left)
    far, to_right, to_left = together(far, to_right, to_left)
    from_left = lax.ppermute(to_right, "tp", [(0, 1), (1, 2), (2, 3)])
    from_right = lax.ppermute(to_left, "tp", [(3, 2), (2, 1), (1, 0)])
    routed_input = slots_back(routed, dispatch, me, experts)

    acts, rows, cots = (
        a + b + c for a, b, c in zip(both01, both2, both3)
    )
    cut = -(-half // 32) * 16
    made = {
        apart: weight_terms(
            jnp.bitwise_xor(chip, apart), acts, rows, cots, 2 * columns, cut
        )
        for apart in (3, 1, 2)
    }
    low = across(made[3][0], 2)
    high = across(made[3][1], 4)
    low_own = across(made[1][0], 2)
    high_own = across(made[2][1], 4)

    low = across(add(made[2][0], low), 4)
    high = across(add(made[1][1], high), 2)
    made[0] = weight_terms(chip, acts, rows, cots, 2 * columns, cut)
    low, high, from_left, from_right = together(low, high, from_left, from_right)
    mine, other = final_sum(
        core, (made[0][0], low_own, low), (made[0][1], high_own, high)
    )
    grads = join_halves(core, mine, across(other, 1))
    grad_input = (
        partial0.astype(F32)
        + from_left.astype(F32)
        + from_right.astype(F32)
        + far.astype(F32)
        + routed_input
    ).astype(BF16)
    return (grad_input, grads[1], grads[2], grads[0], g_gate[None], g_up[None], g_down[None])


def general_body(
    hidden_in,
    cotangent,
    routes,
    gate_values,
    dense_gate,
    dense_up,
    dense_down,
    expert_gate,
    expert_up,
    expert_down,
):
    experts = lax.axis_size("tp")
    me = lax.axis_index("tp")
    dispatch, weight = slot_tables(routes, gate_values, me, experts)
    sent = slots_to_send(hidden_in, cotangent, dispatch, weight, experts)
    got = exchange_slots(sent, me, experts)
    slots = lax.all_gather(got, "ep", axis=0, tiled=False)
    slot_rows, slot_cot = slots[:, 0].reshape(-1, hidden_in.shape[1]), slots[:, 1].reshape(
        -1, hidden_in.shape[1]
    )
    rows = lax.all_gather(hidden_in, "tp", axis=0, tiled=True)
    cots = lax.all_gather(cotangent, "tp", axis=0, tiled=True)
    down = lax.all_gather(dense_down, "ep", axis=1, tiled=True)
    act, grad_gate, grad_up, partial = plain_block(rows, cots, dense_gate, dense_up, down)
    dense_input = lax.psum_scatter(partial, "tp", scatter_dimension=0, tiled=True)
    grads = [
        lax.psum_scatter(
            lax.dot_general(a, b, LEADING, preferred_element_type=F32).astype(BF16),
            "ep",
            scatter_dimension=1,
            tiled=True,
        )
        for a, b in ((act, cots), (grad_gate, rows), (grad_up, rows))
    ]
    g_gate, g_up, g_down, slot_terms = expert_layer(
        slot_rows, slot_cot, expert_gate[0], expert_up[0], expert_down[0]
    )
    routed = lax.psum_scatter(slot_terms, "ep", scatter_dimension=0, tiled=True)
    routed_input = slots_back(routed, dispatch, me, experts)
    grad_input = (dense_input.astype(F32) + routed_input).astype(BF16)
    return (grad_input, grads[1], grads[2], grads[0], g_gate[None], g_up[None], g_down[None])


def solution(mesh):
    placed = (
        P(("ep", "tp"), None),
        P(("ep", "tp"), None),
        P(("ep", "tp"), None),
        P(("ep", "tp"), None),
        P("tp", None),
        P("tp", None),
        P("tp", "ep"),
        P("tp", "ep", None),
        P("tp", "ep", None),
        P("tp", "ep", None),
    )
    in_line = mesh.shape["tp"] == 4 and mesh.shape["ep"] == 8
    return jax.shard_map(
        line_body if in_line else general_body,
        mesh=mesh,
        in_specs=placed,
        out_specs=(
            P(("ep", "tp"), None),
            P("tp", "ep"),
            P("tp", "ep"),
            P("tp", "ep"),
            P("tp", "ep", None),
            P("tp", "ep", None),
            P("tp", "ep", None),
        ),
        check_vma=False,
    )
```

```python
import jax
import jax.numpy as jnp
from jax import lax
from jax.experimental import pallas as pl
from jax.experimental.pallas import tpu as pltpu
from jax.sharding import PartitionSpec as P

CAP = 4
CONTRACT = (((1,), (1,)), ((), ()))
LEADING = (((0,), (0,)), ((), ()))
F32 = jnp.float32
BF16 = jnp.bfloat16


def swiglu_backward(gate_pre, up_pre, grad_act):
    sigmoid_gate = jax.nn.sigmoid(gate_pre)
    silu_gate = gate_pre * sigmoid_gate
    act = (silu_gate * up_pre).astype(BF16)
    silu_slope = sigmoid_gate * (1.0 + gate_pre * (1.0 - sigmoid_gate))
    grad_gate = (grad_act * up_pre * silu_slope).astype(BF16)
    grad_up = (grad_act * silu_gate).astype(BF16)
    return act, grad_gate, grad_up


def slot_tables(routes, gate_values, me, experts):
    tok_count = routes.shape[0]
    named = lax.rem(me + jnp.arange(experts, dtype=jnp.int32), experts)
    onehot = (routes.reshape(-1)[:, None] == named[None, :]).astype(jnp.int32)
    before = jnp.cumsum(onehot, axis=0) - onehot
    slot = onehot[:, :, None] * (before[:, :, None] == jnp.arange(CAP, dtype=jnp.int32)).astype(
        jnp.int32
    )
    slot = slot.reshape(tok_count, 2, experts * CAP).astype(F32)
    dispatch = jnp.sum(slot, axis=1).T.astype(BF16)
    weight = jnp.sum(slot * gate_values[:, :, None], axis=(0, 1))
    return dispatch, weight


def shift(x, axis, size, by):
    return lax.ppermute(x, axis, [(i, (i + by) % size) for i in range(size)])


def slots_to_send(hidden_in, cotangent, dispatch, weight, experts):
    width = hidden_in.shape[1]
    rows = jnp.dot(dispatch, hidden_in, preferred_element_type=F32).astype(BF16)
    cots = jnp.dot(dispatch, cotangent, preferred_element_type=F32)
    cots = (cots * weight[:, None]).astype(BF16)
    return jnp.stack(
        [rows.reshape(experts, CAP, width), cots.reshape(experts, CAP, width)], axis=1
    )


def exchange_slots(sent, me, experts):
    width = sent.shape[3]
    sent = jnp.roll(sent, me, axis=0)
    got = lax.all_to_all(sent, "tp", split_axis=0, concat_axis=0, tiled=True)
    return got.transpose(1, 0, 2, 3).reshape(2, experts * CAP, width)


def expert_layer(slot_rows, slot_cot, gate_weight, up_weight, down_weight):
    e_gate = lax.dot_general(slot_rows, gate_weight, CONTRACT, preferred_element_type=F32)
    e_up = lax.dot_general(slot_rows, up_weight, CONTRACT, preferred_element_type=F32)
    e_grad_act = lax.dot_general(slot_cot, down_weight, CONTRACT, preferred_element_type=F32)
    e_act, e_grad_gate, e_grad_up = swiglu_backward(e_gate, e_up, e_grad_act)
    g_down = lax.dot_general(e_act, slot_cot, LEADING, preferred_element_type=F32).astype(BF16)
    g_gate = lax.dot_general(e_grad_gate, slot_rows, LEADING, preferred_element_type=F32).astype(
        BF16
    )
    g_up = lax.dot_general(e_grad_up, slot_rows, LEADING, preferred_element_type=F32).astype(BF16)
    terms = jnp.dot(e_grad_gate, gate_weight, preferred_element_type=F32) + jnp.dot(
        e_grad_up, up_weight, preferred_element_type=F32
    )
    return g_gate, g_up, g_down, terms.astype(BF16)


def slots_back(own, dispatch, me, experts):
    width = own.shape[1]
    own = own.reshape(experts, CAP, width)
    back = [
        lax.dynamic_index_in_dim(own, lax.rem(me - k + experts, experts), keepdims=False)
        for k in range(experts)
    ]
    back = jnp.stack(back[:1] + [shift(back[k], "tp", experts, -k) for k in range(1, experts)])
    return lax.dot_general(
        dispatch, back.reshape(experts * CAP, width), LEADING, preferred_element_type=F32
    )


def plain_block(rows, cot, gate, up, down):
    gate_pre = lax.dot_general(rows, gate, CONTRACT, preferred_element_type=F32)
    up_pre = lax.dot_general(rows, up, CONTRACT, preferred_element_type=F32)
    grad_act = lax.dot_general(cot, down, CONTRACT, preferred_element_type=F32)
    act, grad_gate, grad_up = swiglu_backward(gate_pre, up_pre, grad_act)
    partial = jnp.dot(grad_gate, gate, preferred_element_type=F32) + jnp.dot(
        grad_up, up, preferred_element_type=F32
    )
    return act, grad_gate, grad_up, partial.astype(BF16)


VMEM_LIMIT = 24 * 1024 * 1024
VMEM_ALL = 60 * 1024 * 1024


def unit_tiles(units):
    return [(start, min(256, units - start)) for start in range(0, units, 256)]


def layer_kernel(rows, cots, gate, up, down, down_turned, turned, partial, col):
    units, width = gate.shape
    for start, size in unit_tiles(units):
        gate_pre, up_pre = [
            lax.dot_general(w[start : start + size], rows, CONTRACT, preferred_element_type=F32)
            for w in (gate, up)
        ]
        if down_turned:
            grad_act = jnp.dot(
                cots, down[:, start : start + size], preferred_element_type=F32
            ).T
        else:
            grad_act = lax.dot_general(
                down[start : start + size], cots, CONTRACT, preferred_element_type=F32
            )
        for i, value in enumerate(swiglu_backward(gate_pre, up_pre, grad_act)):
            turned[i, start : start + size] = value
    grads = [turned[1].T, turned[2].T]
    for j in range(0, width, col):
        partial[:, j : j + col] = (
            jnp.dot(grads[0], gate[:, j : j + col], preferred_element_type=F32)
            + jnp.dot(grads[1], up[:, j : j + col], preferred_element_type=F32)
        ).astype(BF16)


def dense_block(core, blocks, gate, up, down):
    tok, width = blocks[0].shape[1] * len(blocks), blocks[0].shape[2]
    units = gate.shape[0]
    half = units // 2

    def kernel(core_ref, *refs):
        ins, refs = refs[: len(blocks)], refs[len(blocks) :]
        gate, up, down, own, other, partial, turned = refs
        rows, cots = [
            ins[0][k]
            if len(ins) == 1
            else jnp.concatenate([ref[k] for ref in ins], axis=0)
            for k in range(2)
        ]
        layer_kernel(rows, cots, gate, up, down, True, turned, partial, 512)
        mine = core_ref[0]
        own[...] = turned[:, pl.ds(pl.multiple_of(mine * half, 16), half), :]
        other[...] = turned[:, pl.ds(pl.multiple_of((1 - mine) * half, 16), half), :]

    vmem = pl.BlockSpec(memory_space=pltpu.VMEM)
    return pl.pallas_call(
        kernel,
        in_specs=[pl.BlockSpec(memory_space=pltpu.SMEM)] + [vmem] * (len(blocks) + 3),
        out_specs=[vmem, vmem, vmem],
        out_shape=[
            jax.ShapeDtypeStruct((3, half, tok), BF16),
            jax.ShapeDtypeStruct((3, half, tok), BF16),
            jax.ShapeDtypeStruct((tok, width), BF16),
        ],
        scratch_shapes=[pltpu.VMEM((3, units, tok), BF16)],
        compiler_params=pltpu.CompilerParams(vmem_limit_bytes=VMEM_LIMIT),
        cost_estimate=pl.CostEstimate(
            flops=10 * units * width * tok,
            bytes_accessed=6 * units * width + 6 * tok * (width + units),
            transcendentals=units * tok,
        ),
        name="dense_block",
    )(core.reshape(1), *blocks, gate, up, down)


def expert_block(rows, cots, gate, up, down):
    tok, width = rows.shape
    units = gate.shape[0]
    col = width // 4

    def kernel(
        rows, cots, gate, up, down, g_gate, g_up, g_down, partial, turned, made, out_sems
    ):
        layer_kernel(rows[...], cots[...], gate, up, down, False, turned, partial, 512)
        outs = (g_down, g_gate, g_up)
        pending = [None, None]
        step = 0
        for i in range(3):
            right = cots if i == 0 else rows
            for j in range(0, width, col):
                slot = step % 2
                if pending[slot] is not None:
                    pending[slot].wait()
                made[slot] = jnp.dot(
                    turned[i], right[:, j : j + col], preferred_element_type=F32
                ).astype(BF16)
                copy = pltpu.make_async_copy(
                    made.at[slot], outs[i].at[:, pl.ds(j, col)], out_sems.at[slot]
                )
                copy.start()
                pending[slot] = copy
                step += 1
        for copy in pending:
            copy.wait()

    vmem = pl.BlockSpec(memory_space=pltpu.VMEM)
    hbm = pl.BlockSpec(memory_space=pl.ANY)
    grad = jax.ShapeDtypeStruct((units, width), BF16)
    return pl.pallas_call(
        kernel,
        in_specs=[vmem] * 5,
        out_specs=[hbm, hbm, hbm, vmem],
        out_shape=[grad, grad, grad, jax.ShapeDtypeStruct((tok, width), BF16)],
        scratch_shapes=[
            pltpu.VMEM((3, units, tok), BF16),
            pltpu.VMEM((2, units, col), BF16),
            pltpu.SemaphoreType.DMA((2,)),
        ],
        compiler_params=pltpu.CompilerParams(vmem_limit_bytes=VMEM_LIMIT),
        cost_estimate=pl.CostEstimate(
            flops=16 * units * width * tok,
            bytes_accessed=12 * units * width + 6 * tok * width,
            transcendentals=units * tok,
        ),
        name="expert_block",
    )(rows, cots, gate, up, down)


def final_sum(core, lows, highs):
    count = len(lows)
    _, cut, width = lows[0].shape
    units = cut + highs[0].shape[1]
    half = width // 2

    def kernel(core_ref, *refs):
        ins, (mine, other) = refs[:-2], refs[-2:]
        own_first = core_ref[0] == 0
        for i in range(3):
            for begin, group in ((0, ins[:count]), (cut, ins[count:])):
                total = group[0][i].astype(F32)
                for ref in group[1:]:
                    total = total + ref[i].astype(F32)
                left, right = total[:, :half].astype(BF16), total[:, half:].astype(BF16)
                size = total.shape[0]
                mine[i, begin : begin + size] = jnp.where(own_first, left, right)
                other[i, begin : begin + size] = jnp.where(own_first, right, left)

    vmem = pl.BlockSpec(memory_space=pltpu.VMEM)
    shape = jax.ShapeDtypeStruct((3, units, half), BF16)
    return pl.pallas_call(
        kernel,
        in_specs=[pl.BlockSpec(memory_space=pltpu.SMEM)] + [vmem] * (2 * count),
        out_specs=[vmem, vmem],
        out_shape=[shape, shape],
        compiler_params=pltpu.CompilerParams(vmem_limit_bytes=VMEM_LIMIT),
        cost_estimate=pl.CostEstimate(
            flops=3 * count * units * width,
            bytes_accessed=6 * (count + 1) * units * width,
            transcendentals=0,
        ),
        name="final_sum",
    )(core.reshape(1), *lows, *highs)


def join_halves(core, mine, other):
    _, units, width = mine.shape

    def kernel(core_ref, mine, other, *outs):
        me = core_ref[0]
        for i in range(3):
            outs[i][pl.ds(pl.multiple_of(me * units, 16), units), :] = mine[i]
            outs[i][pl.ds(pl.multiple_of((1 - me) * units, 16), units), :] = other[i]

    vmem = pl.BlockSpec(memory_space=pltpu.VMEM)
    return pl.pallas_call(
        kernel,
        in_specs=[pl.BlockSpec(memory_space=pltpu.SMEM), vmem, vmem],
        out_specs=[vmem] * 3,
        out_shape=[jax.ShapeDtypeStruct((2 * units, width), BF16)] * 3,
        compiler_params=pltpu.CompilerParams(vmem_limit_bytes=VMEM_ALL),
        cost_estimate=pl.CostEstimate(
            flops=0, bytes_accessed=24 * units * width, transcendentals=0
        ),
        name="join_halves",
    )(core.reshape(1), mine, other)


def weight_terms(tile, acts, blocks, width, cut):
    units = acts[0].shape[1]
    tokens = sum(b.shape[1] for b in blocks)

    def kernel(tile_ref, *refs):
        a, b = refs[: len(acts)], refs[len(acts) : -2]
        low, high = refs[-2:]
        rows = jnp.concatenate([ref[0] for ref in b], axis=0)
        cots = jnp.concatenate([ref[1] for ref in b], axis=0)
        for i in range(3):
            left = jnp.concatenate([ref[i] for ref in a], axis=1)
            made = jnp.dot(left, cots if i == 0 else rows, preferred_element_type=F32).astype(BF16)
            low[i] = made[:cut]
            high[i] = made[cut:]

    def whole(shape):
        return pl.BlockSpec(shape, lambda i, tile_ref: (0, 0, 0))

    def columns(block):
        return pl.BlockSpec((*block.shape[:2], width), lambda i, tile_ref: (0, 0, tile_ref[0]))

    return pl.pallas_call(
        kernel,
        grid_spec=pltpu.PrefetchScalarGridSpec(
            num_scalar_prefetch=1,
            grid=(1,),
            in_specs=[whole(a.shape) for a in acts] + [columns(b) for b in blocks],
            out_specs=[whole((3, cut, width)), whole((3, units - cut, width))],
        ),
        out_shape=[
            jax.ShapeDtypeStruct((3, cut, width), BF16),
            jax.ShapeDtypeStruct((3, units - cut, width), BF16),
        ],
        compiler_params=pltpu.CompilerParams(vmem_limit_bytes=VMEM_ALL),
        cost_estimate=pl.CostEstimate(
            flops=6 * units * tokens * width,
            bytes_accessed=2 * (tokens * (2 * width + 3 * units) + 3 * units * width),
            transcendentals=0,
        ),
        name="weight_terms",
    )(tile.reshape(1), *acts, *blocks)


def together(*values):
    return lax.optimization_barrier(values)


def line_body(
    hidden_in,
    cotangent,
    routes,
    gate_values,
    dense_gate,
    dense_up,
    dense_down,
    expert_gate,
    expert_up,
    expert_down,
):
    experts = lax.axis_size("tp")
    me = lax.axis_index("tp")
    ep = lax.axis_index("ep")
    core, chip = lax.rem(ep, 2), lax.div(ep, 2)
    half = dense_gate.shape[0] // 2
    columns = dense_down.shape[1]
    own = jnp.stack([hidden_in, cotangent])

    down = lax.all_gather(dense_down.T, "ep", axis=0, tiled=True)

    def outer(value):
        return lax.ppermute(value, "tp", [(0, 1), (1, 0), (2, 3), (3, 2)])

    def middle(value):
        return lax.ppermute(value, "tp", [(0, 0), (1, 2), (2, 1), (3, 3)])

    def across(value, apart):
        return lax.ppermute(value, "ep", [(i, i ^ apart) for i in range(8)])

    def add(a, b):
        return (a.astype(F32) + b.astype(F32)).astype(BF16)

    def dense(blocks):
        mine, other, partial = dense_block(core, blocks, dense_gate, dense_up, down)
        tokens = [*blocks, *(across(b, 1) for b in blocks)]
        return ([mine, across(other, 1)], tokens), partial

    inner = (me == 1) | (me == 2)
    from_outer, from_middle = outer(own), middle(own)
    dispatch, weight = slot_tables(routes, gate_values, me, experts)
    sent = slots_to_send(hidden_in, cotangent, dispatch, weight, experts)
    got = exchange_slots(sent, me, experts)

    from_outer, from_middle, down, got = together(from_outer, from_middle, down, got)
    far_rows = outer(from_middle)
    near_rows = middle(jnp.where(inner, from_outer, own))
    slots = lax.all_gather(got, "ep", axis=0, tiled=False)
    first = jnp.where(inner, from_middle, from_outer)
    both01, partial01 = dense([own, first])

    far_rows, near_rows, partial01 = together(far_rows, near_rows, partial01)
    third = outer(near_rows)
    second = jnp.where(inner, near_rows, far_rows)
    both2, partial2 = dense([second])
    slots, partial2 = together(slots, partial2)
    slot_rows, slot_cot = slots[:, 0].reshape(-1, hidden_in.shape[1]), slots[:, 1].reshape(
        -1, hidden_in.shape[1]
    )
    g_gate, g_up, g_down, slot_terms = expert_block(
        slot_rows, slot_cot, expert_gate[0], expert_up[0], expert_down[0]
    )
    from_end = lax.ppermute(partial2, "tp", [(0, 1), (3, 2)])
    from_inner = middle(partial2)

    acts2, tokens2 = both2
    third, slot_terms, both01, tokens2 = together(third, slot_terms, both01, tokens2)
    both2 = (acts2, tokens2)
    routed = lax.psum_scatter(slot_terms, "ep", scatter_dimension=0, tiled=True)
    partial0, partial1 = jnp.split(partial01, 2, axis=0)
    both3, partial3 = dense([third])
    far = lax.ppermute(partial3, "tp", [(0, 3), (3, 0), (1, 1), (2, 2)])
    to_outer = jnp.where(inner, add(partial3, from_inner), partial1)
    to_middle = add(partial1, from_end)

    acts, tokens = (a + b + c for a, b, c in zip(both01, both2, both3))
    cut = -(-half // 32) * 16
    made = {
        apart: weight_terms(
            jnp.bitwise_xor(chip, apart), acts, tokens, 2 * columns, cut
        )
        for apart in (3, 1, 2, 0)
    }
    low = across(made[3][0], 2)
    high = across(made[3][1], 4)
    low_own = across(made[1][0], 2)
    high_own = across(made[2][1], 4)
    far, to_outer, to_middle, routed, made[0] = together(
        far, to_outer, to_middle, routed, made[0]
    )
    routed_input = slots_back(routed, dispatch, me, experts)
    near = outer(to_outer)
    across_middle = middle(to_middle)
    low, high, made[0] = together(low, high, made[0])
    low = across(add(made[2][0], low), 4)
    high = across(add(made[1][1], high), 2)
    low, high, near, across_middle = together(low, high, near, across_middle)
    mine, other = final_sum(
        core, (made[0][0], low_own, low), (made[0][1], high_own, high)
    )
    grads = join_halves(core, mine, across(other, 1))
    grad_input = (
        partial0.astype(F32)
        + near.astype(F32)
        + jnp.where(inner, across_middle, far).astype(F32)
        + routed_input
    ).astype(BF16)
    return (grad_input, grads[1], grads[2], grads[0], g_gate[None], g_up[None], g_down[None])


def general_body(
    hidden_in,
    cotangent,
    routes,
    gate_values,
    dense_gate,
    dense_up,
    dense_down,
    expert_gate,
    expert_up,
    expert_down,
):
    experts = lax.axis_size("tp")
    me = lax.axis_index("tp")
    dispatch, weight = slot_tables(routes, gate_values, me, experts)
    sent = slots_to_send(hidden_in, cotangent, dispatch, weight, experts)
    got = exchange_slots(sent, me, experts)
    slots = lax.all_gather(got, "ep", axis=0, tiled=False)
    slot_rows, slot_cot = slots[:, 0].reshape(-1, hidden_in.shape[1]), slots[:, 1].reshape(
        -1, hidden_in.shape[1]
    )
    rows = lax.all_gather(hidden_in, "tp", axis=0, tiled=True)
    cots = lax.all_gather(cotangent, "tp", axis=0, tiled=True)
    down = lax.all_gather(dense_down, "ep", axis=1, tiled=True)
    act, grad_gate, grad_up, partial = plain_block(rows, cots, dense_gate, dense_up, down)
    dense_input = lax.psum_scatter(partial, "tp", scatter_dimension=0, tiled=True)
    grads = [
        lax.psum_scatter(
            lax.dot_general(a, b, LEADING, preferred_element_type=F32).astype(BF16),
            "ep",
            scatter_dimension=1,
            tiled=True,
        )
        for a, b in ((act, cots), (grad_gate, rows), (grad_up, rows))
    ]
    g_gate, g_up, g_down, slot_terms = expert_layer(
        slot_rows, slot_cot, expert_gate[0], expert_up[0], expert_down[0]
    )
    routed = lax.psum_scatter(slot_terms, "ep", scatter_dimension=0, tiled=True)
    routed_input = slots_back(routed, dispatch, me, experts)
    grad_input = (dense_input.astype(F32) + routed_input).astype(BF16)
    return (grad_input, grads[1], grads[2], grads[0], g_gate[None], g_up[None], g_down[None])


def solution(mesh):
    placed = (
        P(("ep", "tp"), None),
        P(("ep", "tp"), None),
        P(("ep", "tp"), None),
        P(("ep", "tp"), None),
        P("tp", None),
        P("tp", None),
        P("tp", "ep"),
        P("tp", "ep", None),
        P("tp", "ep", None),
        P("tp", "ep", None),
    )
    in_line = mesh.shape["tp"] == 4 and mesh.shape["ep"] == 8
    return jax.shard_map(
        line_body if in_line else general_body,
        mesh=mesh,
        in_specs=placed,
        out_specs=(
            P(("ep", "tp"), None),
            P("tp", "ep"),
            P("tp", "ep"),
            P("tp", "ep"),
            P("tp", "ep", None),
            P("tp", "ep", None),
            P("tp", "ep", None),
        ),
        check_vma=False,
    )
```

```python
import jax
import jax.numpy as jnp
from jax import lax
from jax.experimental import pallas as pl
from jax.experimental.pallas import tpu as pltpu
from jax.sharding import PartitionSpec as P

CAP = 4
CONTRACT = (((1,), (1,)), ((), ()))
LEADING = (((0,), (0,)), ((), ()))
F32 = jnp.float32
BF16 = jnp.bfloat16


def swiglu_backward(gate_pre, up_pre, grad_act):
    sigmoid_gate = jax.nn.sigmoid(gate_pre)
    silu_gate = gate_pre * sigmoid_gate
    act = (silu_gate * up_pre).astype(BF16)
    silu_slope = sigmoid_gate * (1.0 + gate_pre * (1.0 - sigmoid_gate))
    grad_gate = (grad_act * up_pre * silu_slope).astype(BF16)
    grad_up = (grad_act * silu_gate).astype(BF16)
    return act, grad_gate, grad_up


def slot_tables(routes, gate_values, me, experts):
    tok_count = routes.shape[0]
    named = lax.rem(me + jnp.arange(experts, dtype=jnp.int32), experts)
    onehot = (routes.reshape(-1)[:, None] == named[None, :]).astype(jnp.int32)
    before = jnp.cumsum(onehot, axis=0) - onehot
    slot = onehot[:, :, None] * (before[:, :, None] == jnp.arange(CAP, dtype=jnp.int32)).astype(
        jnp.int32
    )
    slot = slot.reshape(tok_count, 2, experts * CAP).astype(F32)
    dispatch = jnp.sum(slot, axis=1).T.astype(BF16)
    weight = jnp.sum(slot * gate_values[:, :, None], axis=(0, 1))
    return dispatch, weight


def shift(x, axis, size, by):
    return lax.ppermute(x, axis, [(i, (i + by) % size) for i in range(size)])


def slots_to_send(hidden_in, cotangent, dispatch, weight, experts):
    width = hidden_in.shape[1]
    rows = jnp.dot(dispatch, hidden_in, preferred_element_type=F32).astype(BF16)
    cots = jnp.dot(dispatch, cotangent, preferred_element_type=F32)
    cots = (cots * weight[:, None]).astype(BF16)
    return jnp.stack(
        [rows.reshape(experts, CAP, width), cots.reshape(experts, CAP, width)], axis=1
    )


def exchange_slots(sent, me, experts):
    width = sent.shape[3]
    sent = jnp.roll(sent, me, axis=0)
    got = lax.all_to_all(sent, "tp", split_axis=0, concat_axis=0, tiled=True)
    return got.transpose(1, 0, 2, 3).reshape(2, experts * CAP, width)


def expert_layer(slot_rows, slot_cot, gate_weight, up_weight, down_weight):
    e_gate = lax.dot_general(slot_rows, gate_weight, CONTRACT, preferred_element_type=F32)
    e_up = lax.dot_general(slot_rows, up_weight, CONTRACT, preferred_element_type=F32)
    e_grad_act = lax.dot_general(slot_cot, down_weight, CONTRACT, preferred_element_type=F32)
    e_act, e_grad_gate, e_grad_up = swiglu_backward(e_gate, e_up, e_grad_act)
    g_down = lax.dot_general(e_act, slot_cot, LEADING, preferred_element_type=F32).astype(BF16)
    g_gate = lax.dot_general(e_grad_gate, slot_rows, LEADING, preferred_element_type=F32).astype(
        BF16
    )
    g_up = lax.dot_general(e_grad_up, slot_rows, LEADING, preferred_element_type=F32).astype(BF16)
    terms = jnp.dot(e_grad_gate, gate_weight, preferred_element_type=F32) + jnp.dot(
        e_grad_up, up_weight, preferred_element_type=F32
    )
    return g_gate, g_up, g_down, terms.astype(BF16)


def slots_back(own, dispatch, me, experts):
    width = own.shape[1]
    own = own.reshape(experts, CAP, width)
    back = [
        lax.dynamic_index_in_dim(own, lax.rem(me - k + experts, experts), keepdims=False)
        for k in range(experts)
    ]
    back = jnp.stack(back[:1] + [shift(back[k], "tp", experts, -k) for k in range(1, experts)])
    return lax.dot_general(
        dispatch, back.reshape(experts * CAP, width), LEADING, preferred_element_type=F32
    )


def plain_block(rows, cot, gate, up, down):
    gate_pre = lax.dot_general(rows, gate, CONTRACT, preferred_element_type=F32)
    up_pre = lax.dot_general(rows, up, CONTRACT, preferred_element_type=F32)
    grad_act = lax.dot_general(cot, down, CONTRACT, preferred_element_type=F32)
    act, grad_gate, grad_up = swiglu_backward(gate_pre, up_pre, grad_act)
    partial = jnp.dot(grad_gate, gate, preferred_element_type=F32) + jnp.dot(
        grad_up, up, preferred_element_type=F32
    )
    return act, grad_gate, grad_up, partial.astype(BF16)


VMEM_LIMIT = 24 * 1024 * 1024
VMEM_ALL = 60 * 1024 * 1024


def unit_tiles(units):
    return [(start, min(256, units - start)) for start in range(0, units, 256)]


def layer_kernel(rows, cots, gate, up, down, down_turned, turned, partial, col):
    units, width = gate.shape
    for start, size in unit_tiles(units):
        gate_pre, up_pre = [
            lax.dot_general(w[start : start + size], rows, CONTRACT, preferred_element_type=F32)
            for w in (gate, up)
        ]
        if down_turned:
            grad_act = jnp.dot(
                cots, down[:, start : start + size], preferred_element_type=F32
            ).T
        else:
            grad_act = lax.dot_general(
                down[start : start + size], cots, CONTRACT, preferred_element_type=F32
            )
        for i, value in enumerate(swiglu_backward(gate_pre, up_pre, grad_act)):
            turned[i, start : start + size] = value
    grads = [turned[1].T, turned[2].T]
    for j in range(0, width, col):
        partial[:, j : j + col] = (
            jnp.dot(grads[0], gate[:, j : j + col], preferred_element_type=F32)
            + jnp.dot(grads[1], up[:, j : j + col], preferred_element_type=F32)
        ).astype(BF16)


def dense_block(core, blocks, gate, up, down):
    tok, width = blocks[0].shape[1] * len(blocks), blocks[0].shape[2]
    units = gate.shape[0]
    half = units // 2

    def kernel(core_ref, *refs):
        ins, refs = refs[: len(blocks)], refs[len(blocks) :]
        gate, up, down, own, other, partial, turned = refs
        rows, cots = [
            ins[0][k]
            if len(ins) == 1
            else jnp.concatenate([ref[k] for ref in ins], axis=0)
            for k in range(2)
        ]
        layer_kernel(rows, cots, gate, up, down, True, turned, partial, 512)
        mine = core_ref[0]
        own[...] = turned[:, pl.ds(pl.multiple_of(mine * half, 16), half), :]
        other[...] = turned[:, pl.ds(pl.multiple_of((1 - mine) * half, 16), half), :]

    vmem = pl.BlockSpec(memory_space=pltpu.VMEM)
    return pl.pallas_call(
        kernel,
        in_specs=[pl.BlockSpec(memory_space=pltpu.SMEM)] + [vmem] * (len(blocks) + 3),
        out_specs=[vmem, vmem, vmem],
        out_shape=[
            jax.ShapeDtypeStruct((3, half, tok), BF16),
            jax.ShapeDtypeStruct((3, half, tok), BF16),
            jax.ShapeDtypeStruct((tok, width), BF16),
        ],
        scratch_shapes=[pltpu.VMEM((3, units, tok), BF16)],
        compiler_params=pltpu.CompilerParams(vmem_limit_bytes=VMEM_LIMIT),
        cost_estimate=pl.CostEstimate(
            flops=10 * units * width * tok,
            bytes_accessed=6 * units * width + 6 * tok * (width + units),
            transcendentals=units * tok,
        ),
        name="dense_block",
    )(core.reshape(1), *blocks, gate, up, down)


def expert_block(rows, cots, gate, up, down):
    tok, width = rows.shape
    units = gate.shape[0]
    col = width // 4

    def kernel(
        rows, cots, gate, up, down, g_gate, g_up, g_down, partial, turned, made, out_sems
    ):
        layer_kernel(rows[...], cots[...], gate, up, down, False, turned, partial, 512)
        outs = (g_down, g_gate, g_up)
        pending = [None, None]
        step = 0
        for i in range(3):
            right = cots if i == 0 else rows
            for j in range(0, width, col):
                slot = step % 2
                if pending[slot] is not None:
                    pending[slot].wait()
                made[slot] = jnp.dot(
                    turned[i], right[:, j : j + col], preferred_element_type=F32
                ).astype(BF16)
                copy = pltpu.make_async_copy(
                    made.at[slot], outs[i].at[:, pl.ds(j, col)], out_sems.at[slot]
                )
                copy.start()
                pending[slot] = copy
                step += 1
        for copy in pending:
            copy.wait()

    vmem = pl.BlockSpec(memory_space=pltpu.VMEM)
    hbm = pl.BlockSpec(memory_space=pl.ANY)
    grad = jax.ShapeDtypeStruct((units, width), BF16)
    return pl.pallas_call(
        kernel,
        in_specs=[vmem] * 5,
        out_specs=[hbm, hbm, hbm, vmem],
        out_shape=[grad, grad, grad, jax.ShapeDtypeStruct((tok, width), BF16)],
        scratch_shapes=[
            pltpu.VMEM((3, units, tok), BF16),
            pltpu.VMEM((2, units, col), BF16),
            pltpu.SemaphoreType.DMA((2,)),
        ],
        compiler_params=pltpu.CompilerParams(vmem_limit_bytes=VMEM_LIMIT),
        cost_estimate=pl.CostEstimate(
            flops=16 * units * width * tok,
            bytes_accessed=12 * units * width + 6 * tok * width,
            transcendentals=units * tok,
        ),
        name="expert_block",
    )(rows, cots, gate, up, down)


def final_sum(core, lows, highs):
    count = len(lows)
    _, cut, width = lows[0].shape
    units = cut + highs[0].shape[1]
    half = width // 2

    def kernel(core_ref, *refs):
        ins, (mine, other) = refs[:-2], refs[-2:]
        own_first = core_ref[0] == 0
        for i in range(3):
            for begin, group in ((0, ins[:count]), (cut, ins[count:])):
                total = group[0][i].astype(F32)
                for ref in group[1:]:
                    total = total + ref[i].astype(F32)
                left, right = total[:, :half].astype(BF16), total[:, half:].astype(BF16)
                size = total.shape[0]
                mine[i, begin : begin + size] = jnp.where(own_first, left, right)
                other[i, begin : begin + size] = jnp.where(own_first, right, left)

    vmem = pl.BlockSpec(memory_space=pltpu.VMEM)
    shape = jax.ShapeDtypeStruct((3, units, half), BF16)
    return pl.pallas_call(
        kernel,
        in_specs=[pl.BlockSpec(memory_space=pltpu.SMEM)] + [vmem] * (2 * count),
        out_specs=[vmem, vmem],
        out_shape=[shape, shape],
        compiler_params=pltpu.CompilerParams(vmem_limit_bytes=VMEM_LIMIT),
        cost_estimate=pl.CostEstimate(
            flops=3 * count * units * width,
            bytes_accessed=6 * (count + 1) * units * width,
            transcendentals=0,
        ),
        name="final_sum",
    )(core.reshape(1), *lows, *highs)


def join_halves(core, mine, other):
    _, units, width = mine.shape

    def kernel(core_ref, mine, other, *outs):
        first = core_ref[0] == 0
        for i in range(3):
            a, b = mine[i], other[i]
            joined = jnp.concatenate([jnp.where(first, a, b), jnp.where(first, b, a)], axis=0)
            outs[i][...] = joined.T

    vmem = pl.BlockSpec(memory_space=pltpu.VMEM)
    grads = pl.pallas_call(
        kernel,
        in_specs=[pl.BlockSpec(memory_space=pltpu.SMEM), vmem, vmem],
        out_specs=[vmem] * 3,
        out_shape=[jax.ShapeDtypeStruct((width, 2 * units), BF16)] * 3,
        compiler_params=pltpu.CompilerParams(vmem_limit_bytes=VMEM_ALL),
        cost_estimate=pl.CostEstimate(
            flops=0, bytes_accessed=24 * units * width, transcendentals=0
        ),
        name="join_halves",
    )(core.reshape(1), mine, other)
    return [grad.T for grad in grads]


def weight_terms(tile, acts, blocks, width, cut):
    units = acts[0].shape[1]
    tokens = sum(b.shape[1] for b in blocks)

    def kernel(tile_ref, *refs):
        a, b = refs[: len(acts)], refs[len(acts) : -2]
        low, high = refs[-2:]
        rows = jnp.concatenate([ref[0] for ref in b], axis=0)
        cots = jnp.concatenate([ref[1] for ref in b], axis=0)
        for i in range(3):
            left = jnp.concatenate([ref[i] for ref in a], axis=1)
            made = jnp.dot(left, cots if i == 0 else rows, preferred_element_type=F32).astype(BF16)
            low[i] = made[:cut]
            high[i] = made[cut:]

    def whole(shape):
        return pl.BlockSpec(shape, lambda i, tile_ref: (0, 0, 0))

    def columns(block):
        return pl.BlockSpec((*block.shape[:2], width), lambda i, tile_ref: (0, 0, tile_ref[0]))

    return pl.pallas_call(
        kernel,
        grid_spec=pltpu.PrefetchScalarGridSpec(
            num_scalar_prefetch=1,
            grid=(1,),
            in_specs=[whole(a.shape) for a in acts] + [columns(b) for b in blocks],
            out_specs=[whole((3, cut, width)), whole((3, units - cut, width))],
        ),
        out_shape=[
            jax.ShapeDtypeStruct((3, cut, width), BF16),
            jax.ShapeDtypeStruct((3, units - cut, width), BF16),
        ],
        compiler_params=pltpu.CompilerParams(vmem_limit_bytes=VMEM_ALL),
        cost_estimate=pl.CostEstimate(
            flops=6 * units * tokens * width,
            bytes_accessed=2 * (tokens * (2 * width + 3 * units) + 3 * units * width),
            transcendentals=0,
        ),
        name="weight_terms",
    )(tile.reshape(1), *acts, *blocks)


def together(*values):
    return lax.optimization_barrier(values)


def line_body(
    hidden_in,
    cotangent,
    routes,
    gate_values,
    dense_gate,
    dense_up,
    dense_down,
    expert_gate,
    expert_up,
    expert_down,
):
    experts = lax.axis_size("tp")
    me = lax.axis_index("tp")
    ep = lax.axis_index("ep")
    core, chip = lax.rem(ep, 2), lax.div(ep, 2)
    half = dense_gate.shape[0] // 2
    columns = dense_down.shape[1]
    own = jnp.stack([hidden_in, cotangent])

    down = lax.all_gather(dense_down.T, "ep", axis=0, tiled=True)

    def pairs(value):
        return lax.ppermute(value, "tp", [(0, 1), (1, 0), (2, 3), (3, 2)])

    def mirror(value):
        return lax.ppermute(value, "tp", [(0, 3), (1, 2), (2, 1), (3, 0)])

    def across(value, apart):
        return lax.ppermute(value, "ep", [(i, i ^ apart) for i in range(8)])

    def add(a, b):
        return (a.astype(F32) + b.astype(F32)).astype(BF16)

    def dense(blocks):
        mine, other, partial = dense_block(core, blocks, dense_gate, dense_up, down)
        tokens = [*blocks, *(across(b, 1) for b in blocks)]
        return ([mine, across(other, 1)], tokens), partial

    mirrored, paired = mirror(own), pairs(own)
    dispatch, weight = slot_tables(routes, gate_values, me, experts)
    sent = slots_to_send(hidden_in, cotangent, dispatch, weight, experts)
    got = exchange_slots(sent, me, experts)
    both0, partial0 = dense([own])

    mirrored, paired, partial0, got = together(mirrored, paired, partial0, got)
    last = pairs(mirrored)
    slots = lax.all_gather(got, "ep", axis=0, tiled=False)
    both12, partial12 = dense([paired, mirrored])
    slots, partial12 = together(slots, partial12)
    slot_rows, slot_cot = slots[:, 0].reshape(-1, hidden_in.shape[1]), slots[:, 1].reshape(
        -1, hidden_in.shape[1]
    )
    g_gate, g_up, g_down, slot_terms = expert_block(
        slot_rows, slot_cot, expert_gate[0], expert_up[0], expert_down[0]
    )

    last, slot_terms, both0, both12 = together(last, slot_terms, both0, both12)
    routed = lax.psum_scatter(slot_terms, "ep", scatter_dimension=0, tiled=True)
    both3, partial3 = dense([last])
    paired_partial, mirrored_partial = jnp.split(partial12, 2, axis=0)
    from_last = pairs(partial3)

    acts, tokens = (a + b + c for a, b, c in zip(both0, both12, both3))
    cut = -(-half // 32) * 16
    made = {3: weight_terms(jnp.bitwise_xor(chip, 3), acts, tokens, 2 * columns, cut)}
    made[3], chip = together(made[3], chip)
    for apart in (1, 2, 0):
        made[apart] = weight_terms(
            jnp.bitwise_xor(chip, apart), acts, tokens, 2 * columns, cut
        )
    low = across(made[3][0], 2)
    high = across(made[3][1], 4)
    low_own = across(made[1][0], 2)
    high_own = across(made[2][1], 4)
    from_last, routed, made[0] = together(from_last, routed, made[0])
    from_mirror = mirror(add(mirrored_partial, from_last))
    from_pair = pairs(paired_partial)
    routed_input = slots_back(routed, dispatch, me, experts)
    low, high, made[0] = together(low, high, made[0])
    low = across(add(made[2][0], low), 4)
    high = across(add(made[1][1], high), 2)
    low, high, from_pair, from_mirror, routed_input = together(
        low, high, from_pair, from_mirror, routed_input
    )
    mine, other = final_sum(
        core, (made[0][0], low_own, low), (made[0][1], high_own, high)
    )
    grads = join_halves(core, mine, across(other, 1))
    grad_input = (
        partial0.astype(F32)
        + from_pair.astype(F32)
        + from_mirror.astype(F32)
        + routed_input
    ).astype(BF16)
    return (grad_input, grads[1], grads[2], grads[0], g_gate[None], g_up[None], g_down[None])


def general_body(
    hidden_in,
    cotangent,
    routes,
    gate_values,
    dense_gate,
    dense_up,
    dense_down,
    expert_gate,
    expert_up,
    expert_down,
):
    experts = lax.axis_size("tp")
    me = lax.axis_index("tp")
    dispatch, weight = slot_tables(routes, gate_values, me, experts)
    sent = slots_to_send(hidden_in, cotangent, dispatch, weight, experts)
    got = exchange_slots(sent, me, experts)
    slots = lax.all_gather(got, "ep", axis=0, tiled=False)
    slot_rows, slot_cot = slots[:, 0].reshape(-1, hidden_in.shape[1]), slots[:, 1].reshape(
        -1, hidden_in.shape[1]
    )
    rows = lax.all_gather(hidden_in, "tp", axis=0, tiled=True)
    cots = lax.all_gather(cotangent, "tp", axis=0, tiled=True)
    down = lax.all_gather(dense_down, "ep", axis=1, tiled=True)
    act, grad_gate, grad_up, partial = plain_block(rows, cots, dense_gate, dense_up, down)
    dense_input = lax.psum_scatter(partial, "tp", scatter_dimension=0, tiled=True)
    grads = [
        lax.psum_scatter(
            lax.dot_general(a, b, LEADING, preferred_element_type=F32).astype(BF16),
            "ep",
            scatter_dimension=1,
            tiled=True,
        )
        for a, b in ((act, cots), (grad_gate, rows), (grad_up, rows))
    ]
    g_gate, g_up, g_down, slot_terms = expert_layer(
        slot_rows, slot_cot, expert_gate[0], expert_up[0], expert_down[0]
    )
    routed = lax.psum_scatter(slot_terms, "ep", scatter_dimension=0, tiled=True)
    routed_input = slots_back(routed, dispatch, me, experts)
    grad_input = (dense_input.astype(F32) + routed_input).astype(BF16)
    return (grad_input, grads[1], grads[2], grads[0], g_gate[None], g_up[None], g_down[None])


def solution(mesh):
    placed = (
        P(("ep", "tp"), None),
        P(("ep", "tp"), None),
        P(("ep", "tp"), None),
        P(("ep", "tp"), None),
        P("tp", None),
        P("tp", None),
        P("tp", "ep"),
        P("tp", "ep", None),
        P("tp", "ep", None),
        P("tp", "ep", None),
    )
    in_line = mesh.shape["tp"] == 4 and mesh.shape["ep"] == 8
    return jax.shard_map(
        line_body if in_line else general_body,
        mesh=mesh,
        in_specs=placed,
        out_specs=(
            P(("ep", "tp"), None),
            P("tp", "ep"),
            P("tp", "ep"),
            P("tp", "ep"),
            P("tp", "ep", None),
            P("tp", "ep", None),
            P("tp", "ep", None),
        ),
        check_vma=False,
    )
```

```python
import jax
import jax.numpy as jnp
from jax import lax
from jax.experimental import pallas as pl
from jax.experimental.pallas import tpu as pltpu
from jax.sharding import PartitionSpec as P

CAP = 4
CONTRACT = (((1,), (1,)), ((), ()))
LEADING = (((0,), (0,)), ((), ()))
F32 = jnp.float32
BF16 = jnp.bfloat16


def swiglu_backward(gate_pre, up_pre, grad_act):
    sigmoid_gate = jax.nn.sigmoid(gate_pre)
    silu_gate = gate_pre * sigmoid_gate
    act = (silu_gate * up_pre).astype(BF16)
    silu_slope = sigmoid_gate * (1.0 + gate_pre * (1.0 - sigmoid_gate))
    grad_gate = (grad_act * up_pre * silu_slope).astype(BF16)
    grad_up = (grad_act * silu_gate).astype(BF16)
    return act, grad_gate, grad_up


def slot_tables(routes, gate_values, me, experts):
    tok_count = routes.shape[0]
    named = lax.rem(me + jnp.arange(experts, dtype=jnp.int32), experts)
    onehot = (routes.reshape(-1)[:, None] == named[None, :]).astype(jnp.int32)
    before = jnp.cumsum(onehot, axis=0) - onehot
    slot = onehot[:, :, None] * (before[:, :, None] == jnp.arange(CAP, dtype=jnp.int32)).astype(
        jnp.int32
    )
    slot = slot.reshape(tok_count, 2, experts * CAP).astype(F32)
    dispatch = jnp.sum(slot, axis=1).T.astype(BF16)
    weight = jnp.sum(slot * gate_values[:, :, None], axis=(0, 1))
    return dispatch, weight


def shift(x, axis, size, by):
    return lax.ppermute(x, axis, [(i, (i + by) % size) for i in range(size)])


def slots_to_send(hidden_in, cotangent, dispatch, weight, experts):
    width = hidden_in.shape[1]
    rows = jnp.dot(dispatch, hidden_in, preferred_element_type=F32).astype(BF16)
    cots = jnp.dot(dispatch, cotangent, preferred_element_type=F32)
    cots = (cots * weight[:, None]).astype(BF16)
    return jnp.stack(
        [rows.reshape(experts, CAP, width), cots.reshape(experts, CAP, width)], axis=1
    )


def exchange_slots(sent, me, experts):
    width = sent.shape[3]
    sent = jnp.roll(sent, me, axis=0)
    got = lax.all_to_all(sent, "tp", split_axis=0, concat_axis=0, tiled=True)
    return got.transpose(1, 0, 2, 3).reshape(2, experts * CAP, width)


def expert_layer(slot_rows, slot_cot, gate_weight, up_weight, down_weight):
    e_gate = lax.dot_general(slot_rows, gate_weight, CONTRACT, preferred_element_type=F32)
    e_up = lax.dot_general(slot_rows, up_weight, CONTRACT, preferred_element_type=F32)
    e_grad_act = lax.dot_general(slot_cot, down_weight, CONTRACT, preferred_element_type=F32)
    e_act, e_grad_gate, e_grad_up = swiglu_backward(e_gate, e_up, e_grad_act)
    g_down = lax.dot_general(e_act, slot_cot, LEADING, preferred_element_type=F32).astype(BF16)
    g_gate = lax.dot_general(e_grad_gate, slot_rows, LEADING, preferred_element_type=F32).astype(
        BF16
    )
    g_up = lax.dot_general(e_grad_up, slot_rows, LEADING, preferred_element_type=F32).astype(BF16)
    terms = jnp.dot(e_grad_gate, gate_weight, preferred_element_type=F32) + jnp.dot(
        e_grad_up, up_weight, preferred_element_type=F32
    )
    return g_gate, g_up, g_down, terms.astype(BF16)


def slots_back(own, dispatch, me, experts):
    width = own.shape[1]
    own = own.reshape(experts, CAP, width)
    back = [
        lax.dynamic_index_in_dim(own, lax.rem(me - k + experts, experts), keepdims=False)
        for k in range(experts)
    ]
    back = jnp.stack(back[:1] + [shift(back[k], "tp", experts, -k) for k in range(1, experts)])
    return lax.dot_general(
        dispatch, back.reshape(experts * CAP, width), LEADING, preferred_element_type=F32
    )


def plain_block(rows, cot, gate, up, down):
    gate_pre = lax.dot_general(rows, gate, CONTRACT, preferred_element_type=F32)
    up_pre = lax.dot_general(rows, up, CONTRACT, preferred_element_type=F32)
    grad_act = lax.dot_general(cot, down, CONTRACT, preferred_element_type=F32)
    act, grad_gate, grad_up = swiglu_backward(gate_pre, up_pre, grad_act)
    partial = jnp.dot(grad_gate, gate, preferred_element_type=F32) + jnp.dot(
        grad_up, up, preferred_element_type=F32
    )
    return act, grad_gate, grad_up, partial.astype(BF16)


VMEM_LIMIT = 20 * 1024 * 1024
VMEM_ALL = 60 * 1024 * 1024


def unit_tiles(units):
    return [(start, min(256, units - start)) for start in range(0, units, 256)]


def layer_kernel(rows, cots, gate, up, down, down_turned, turned, partial, col):
    units, width = gate.shape
    for start, size in unit_tiles(units):
        gate_pre, up_pre = [
            lax.dot_general(w[start : start + size], rows, CONTRACT, preferred_element_type=F32)
            for w in (gate, up)
        ]
        if down_turned:
            grad_act = jnp.dot(
                cots, down[:, start : start + size], preferred_element_type=F32
            ).T
        else:
            grad_act = lax.dot_general(
                down[start : start + size], cots, CONTRACT, preferred_element_type=F32
            )
        for i, value in enumerate(swiglu_backward(gate_pre, up_pre, grad_act)):
            turned[i, start : start + size] = value
    grads = [turned[1].T, turned[2].T]
    for j in range(0, width, col):
        partial[:, j : j + col] = (
            jnp.dot(grads[0], gate[:, j : j + col], preferred_element_type=F32)
            + jnp.dot(grads[1], up[:, j : j + col], preferred_element_type=F32)
        ).astype(BF16)


def dense_block(core, blocks, gate, up, down):
    tok, width = blocks[0].shape[1] * len(blocks), blocks[0].shape[2]
    units = gate.shape[0]
    half = units // 2

    def kernel(core_ref, *refs):
        ins, refs = refs[: len(blocks)], refs[len(blocks) :]
        gate, up, down, own, other, partial, turned = refs
        rows, cots = [
            ins[0][k]
            if len(ins) == 1
            else jnp.concatenate([ref[k] for ref in ins], axis=0)
            for k in range(2)
        ]
        layer_kernel(rows, cots, gate, up, down, True, turned, partial, 512)
        mine = core_ref[0]
        own[...] = turned[:, pl.ds(pl.multiple_of(mine * half, 16), half), :]
        other[...] = turned[:, pl.ds(pl.multiple_of((1 - mine) * half, 16), half), :]

    vmem = pl.BlockSpec(memory_space=pltpu.VMEM)
    return pl.pallas_call(
        kernel,
        in_specs=[pl.BlockSpec(memory_space=pltpu.SMEM)] + [vmem] * (len(blocks) + 3),
        out_specs=[vmem, vmem, vmem],
        out_shape=[
            jax.ShapeDtypeStruct((3, half, tok), BF16),
            jax.ShapeDtypeStruct((3, half, tok), BF16),
            jax.ShapeDtypeStruct((tok, width), BF16),
        ],
        scratch_shapes=[pltpu.VMEM((3, units, tok), BF16)],
        compiler_params=pltpu.CompilerParams(vmem_limit_bytes=VMEM_LIMIT),
        cost_estimate=pl.CostEstimate(
            flops=10 * units * width * tok,
            bytes_accessed=6 * units * width + 6 * tok * (width + units),
            transcendentals=units * tok,
        ),
        name="dense_block",
    )(core.reshape(1), *blocks, gate, up, down)


def expert_block(rows, cots, gate, up, down):
    tok, width = rows.shape
    units = gate.shape[0]
    col = 512

    def kernel(
        rows, cots, gate, up, down, g_gate, g_up, g_down, partial, turned, made, out_sems
    ):
        layer_kernel(rows[...], cots[...], gate, up, down, False, turned, partial, 512)
        outs = (g_down, g_gate, g_up)
        pending = [None, None]
        step = 0
        for i in range(3):
            right = cots if i == 0 else rows
            for j in range(0, width, col):
                slot = step % 2
                if pending[slot] is not None:
                    pending[slot].wait()
                made[slot] = jnp.dot(
                    turned[i], right[:, j : j + col], preferred_element_type=F32
                ).astype(BF16)
                copy = pltpu.make_async_copy(
                    made.at[slot], outs[i].at[:, pl.ds(j, col)], out_sems.at[slot]
                )
                copy.start()
                pending[slot] = copy
                step += 1
        for copy in pending:
            copy.wait()

    vmem = pl.BlockSpec(memory_space=pltpu.VMEM)
    hbm = pl.BlockSpec(memory_space=pl.ANY)
    grad = jax.ShapeDtypeStruct((units, width), BF16)
    return pl.pallas_call(
        kernel,
        in_specs=[vmem] * 5,
        out_specs=[hbm, hbm, hbm, vmem],
        out_shape=[grad, grad, grad, jax.ShapeDtypeStruct((tok, width), BF16)],
        scratch_shapes=[
            pltpu.VMEM((3, units, tok), BF16),
            pltpu.VMEM((2, units, col), BF16),
            pltpu.SemaphoreType.DMA((2,)),
        ],
        compiler_params=pltpu.CompilerParams(vmem_limit_bytes=VMEM_LIMIT),
        cost_estimate=pl.CostEstimate(
            flops=16 * units * width * tok,
            bytes_accessed=12 * units * width + 6 * tok * width,
            transcendentals=units * tok,
        ),
        name="expert_block",
    )(rows, cots, gate, up, down)


def final_sum(core, lows, highs):
    cut, width = lows[2].shape[1:]
    units = cut + highs[2].shape[1]
    half = width // 2

    def kernel(core_ref, *refs):
        ins, (mine, other) = refs[:-2], refs[-2:]
        own_first = core_ref[0] == 0
        for i in range(3):
            for begin, (own, near, far) in ((0, ins[:3]), (cut, ins[3:])):
                total = own[i, :, width:].astype(F32) + near[i, :, width:].astype(F32)
                total = total + far[i].astype(F32)
                left, right = total[:, :half].astype(BF16), total[:, half:].astype(BF16)
                size = total.shape[0]
                mine[i, begin : begin + size] = jnp.where(own_first, left, right)
                other[i, begin : begin + size] = jnp.where(own_first, right, left)

    vmem = pl.BlockSpec(memory_space=pltpu.VMEM)
    shape = jax.ShapeDtypeStruct((3, units, half), BF16)
    return pl.pallas_call(
        kernel,
        in_specs=[pl.BlockSpec(memory_space=pltpu.SMEM)] + [vmem] * 6,
        out_specs=[vmem, vmem],
        out_shape=[shape, shape],
        compiler_params=pltpu.CompilerParams(vmem_limit_bytes=VMEM_LIMIT),
        cost_estimate=pl.CostEstimate(
            flops=9 * units * width,
            bytes_accessed=24 * units * width,
            transcendentals=0,
        ),
        name="final_sum",
    )(core.reshape(1), *lows, *highs)


def join_halves(core, mine, other):
    _, units, width = mine.shape

    def kernel(core_ref, mine, other, *outs):
        first = core_ref[0] == 0
        for i in range(3):
            a, b = mine[i], other[i]
            joined = jnp.concatenate([jnp.where(first, a, b), jnp.where(first, b, a)], axis=0)
            outs[i][...] = joined.T

    vmem = pl.BlockSpec(memory_space=pltpu.VMEM)
    grads = pl.pallas_call(
        kernel,
        in_specs=[pl.BlockSpec(memory_space=pltpu.SMEM), vmem, vmem],
        out_specs=[vmem] * 3,
        out_shape=[jax.ShapeDtypeStruct((width, 2 * units), BF16)] * 3,
        compiler_params=pltpu.CompilerParams(vmem_limit_bytes=VMEM_ALL),
        cost_estimate=pl.CostEstimate(
            flops=0, bytes_accessed=24 * units * width, transcendentals=0
        ),
        name="join_halves",
    )(core.reshape(1), mine, other)
    return [grad.T for grad in grads]


def weight_terms(tiles, acts, blocks, width, begin, end):
    units = acts[0].shape[1]
    tokens = sum(b.shape[1] for b in blocks)
    size = end - begin

    def kernel(tile_ref, *refs):
        a, b, out = refs[: len(acts)], refs[len(acts) : -1], refs[-1]
        rows = jnp.concatenate([ref[0] for ref in b], axis=0)
        cots = jnp.concatenate([ref[1] for ref in b], axis=0)
        for i in range(3):
            left = jnp.concatenate([ref[i, begin:end] for ref in a], axis=1)
            out[i] = jnp.dot(
                left, cots if i == 0 else rows, preferred_element_type=F32
            ).astype(BF16)

    def whole(shape):
        return pl.BlockSpec(shape, lambda j, tile_ref: (0, 0, 0))

    def columns(block):
        return pl.BlockSpec((*block.shape[:2], width), lambda j, tile_ref: (0, 0, tile_ref[j]))

    return pl.pallas_call(
        kernel,
        grid_spec=pltpu.PrefetchScalarGridSpec(
            num_scalar_prefetch=1,
            grid=(2,),
            in_specs=[whole(a.shape) for a in acts] + [columns(b) for b in blocks],
            out_specs=pl.BlockSpec((3, size, width), lambda j, tile_ref: (0, 0, j)),
        ),
        out_shape=jax.ShapeDtypeStruct((3, size, 2 * width), BF16),
        compiler_params=pltpu.CompilerParams(vmem_limit_bytes=VMEM_ALL),
        cost_estimate=pl.CostEstimate(
            flops=12 * size * tokens * width,
            bytes_accessed=2 * (tokens * (4 * width + 3 * units) + 6 * size * width),
            transcendentals=0,
        ),
        name="weight_terms",
    )(jnp.stack(tiles), *acts, *blocks)


def together(*values):
    return lax.optimization_barrier(values)


def line_body(
    hidden_in,
    cotangent,
    routes,
    gate_values,
    dense_gate,
    dense_up,
    dense_down,
    expert_gate,
    expert_up,
    expert_down,
):
    experts = lax.axis_size("tp")
    me = lax.axis_index("tp")
    ep = lax.axis_index("ep")
    core, chip = lax.rem(ep, 2), lax.div(ep, 2)
    half = dense_gate.shape[0] // 2
    columns = dense_down.shape[1]
    own = jnp.stack([hidden_in, cotangent])

    down = lax.all_gather(dense_down.T, "ep", axis=0, tiled=True)

    def pairs(value):
        return lax.ppermute(value, "tp", [(0, 1), (1, 0), (2, 3), (3, 2)])

    def mirror(value):
        return lax.ppermute(value, "tp", [(0, 3), (1, 2), (2, 1), (3, 0)])

    def across(value, apart):
        return lax.ppermute(value, "ep", [(i, i ^ apart) for i in range(8)])

    def add(a, b):
        return (a.astype(F32) + b.astype(F32)).astype(BF16)

    def dense(blocks):
        mine, other, partial = dense_block(core, blocks, dense_gate, dense_up, down)
        tokens = [*blocks, *(across(b, 1) for b in blocks)]
        return ([mine, across(other, 1)], tokens), partial

    mirrored, paired = mirror(own), pairs(own)
    dispatch, weight = slot_tables(routes, gate_values, me, experts)
    sent = slots_to_send(hidden_in, cotangent, dispatch, weight, experts)
    got = exchange_slots(sent, me, experts)
    both0, partial0 = dense([own])

    got, partial0, both0 = together(got, partial0, both0)

    mirrored, paired, got = together(mirrored, paired, got)
    last = pairs(mirrored)
    slots = lax.all_gather(got, "ep", axis=0, tiled=False)
    both12, partial12 = dense([paired, mirrored])
    slots, partial12 = together(slots, partial12)
    slot_rows, slot_cot = slots[:, 0].reshape(-1, hidden_in.shape[1]), slots[:, 1].reshape(
        -1, hidden_in.shape[1]
    )
    g_gate, g_up, g_down, slot_terms = expert_block(
        slot_rows, slot_cot, expert_gate[0], expert_up[0], expert_down[0]
    )

    last, slot_terms, both0, both12 = together(last, slot_terms, both0, both12)
    routed = lax.psum_scatter(slot_terms, "ep", scatter_dimension=0, tiled=True)
    both3, partial3 = dense([last])
    paired_partial, mirrored_partial = jnp.split(partial12, 2, axis=0)
    from_last = pairs(partial3)

    acts, tokens = (a + b + c for a, b, c in zip(both0, both12, both3))
    cut, width = -(-half // 32) * 16, 2 * columns
    x_chip, y_chip, xy_chip = [jnp.bitwise_xor(chip, k) for k in (1, 2, 3)]
    low_sent = weight_terms((xy_chip, x_chip), acts, tokens, width, 0, cut)
    high_sent = weight_terms((xy_chip, y_chip), acts, tokens, width, cut, half)
    low_kept = weight_terms((y_chip, chip), acts, tokens, width, 0, cut)
    high_kept = weight_terms((x_chip, chip), acts, tokens, width, cut, half)
    low_near, high_near = across(low_sent, 2), across(high_sent, 4)
    routed_input = slots_back(routed, dispatch, me, experts)
    from_last, routed_input, low_kept, high_kept = together(
        from_last, routed_input, low_kept, high_kept
    )
    from_mirror = mirror(add(mirrored_partial, from_last))
    from_pair = pairs(paired_partial)
    low_near, high_near, low_kept, high_kept = together(
        low_near, high_near, low_kept, high_kept
    )
    low_far = across(add(low_kept[:, :, :width], low_near[:, :, :width]), 4)
    high_far = across(add(high_kept[:, :, :width], high_near[:, :, :width]), 2)
    low_far, high_far, from_pair, from_mirror = together(
        low_far, high_far, from_pair, from_mirror
    )
    mine, other = final_sum(
        core, (low_kept, low_near, low_far), (high_kept, high_near, high_far)
    )
    grads = join_halves(core, mine, across(other, 1))
    grad_input = (
        partial0.astype(F32)
        + from_pair.astype(F32)
        + from_mirror.astype(F32)
        + routed_input
    ).astype(BF16)
    return (grad_input, grads[1], grads[2], grads[0], g_gate[None], g_up[None], g_down[None])


def general_body(
    hidden_in,
    cotangent,
    routes,
    gate_values,
    dense_gate,
    dense_up,
    dense_down,
    expert_gate,
    expert_up,
    expert_down,
):
    experts = lax.axis_size("tp")
    me = lax.axis_index("tp")
    dispatch, weight = slot_tables(routes, gate_values, me, experts)
    sent = slots_to_send(hidden_in, cotangent, dispatch, weight, experts)
    got = exchange_slots(sent, me, experts)
    slots = lax.all_gather(got, "ep", axis=0, tiled=False)
    slot_rows, slot_cot = slots[:, 0].reshape(-1, hidden_in.shape[1]), slots[:, 1].reshape(
        -1, hidden_in.shape[1]
    )
    rows = lax.all_gather(hidden_in, "tp", axis=0, tiled=True)
    cots = lax.all_gather(cotangent, "tp", axis=0, tiled=True)
    down = lax.all_gather(dense_down, "ep", axis=1, tiled=True)
    act, grad_gate, grad_up, partial = plain_block(rows, cots, dense_gate, dense_up, down)
    dense_input = lax.psum_scatter(partial, "tp", scatter_dimension=0, tiled=True)
    grads = [
        lax.psum_scatter(
            lax.dot_general(a, b, LEADING, preferred_element_type=F32).astype(BF16),
            "ep",
            scatter_dimension=1,
            tiled=True,
        )
        for a, b in ((act, cots), (grad_gate, rows), (grad_up, rows))
    ]
    g_gate, g_up, g_down, slot_terms = expert_layer(
        slot_rows, slot_cot, expert_gate[0], expert_up[0], expert_down[0]
    )
    routed = lax.psum_scatter(slot_terms, "ep", scatter_dimension=0, tiled=True)
    routed_input = slots_back(routed, dispatch, me, experts)
    grad_input = (dense_input.astype(F32) + routed_input).astype(BF16)
    return (grad_input, grads[1], grads[2], grads[0], g_gate[None], g_up[None], g_down[None])


def solution(mesh):
    placed = (
        P(("ep", "tp"), None),
        P(("ep", "tp"), None),
        P(("ep", "tp"), None),
        P(("ep", "tp"), None),
        P("tp", None),
        P("tp", None),
        P("tp", "ep"),
        P("tp", "ep", None),
        P("tp", "ep", None),
        P("tp", "ep", None),
    )
    in_line = mesh.shape["tp"] == 4 and mesh.shape["ep"] == 8
    return jax.shard_map(
        line_body if in_line else general_body,
        mesh=mesh,
        in_specs=placed,
        out_specs=(
            P(("ep", "tp"), None),
            P("tp", "ep"),
            P("tp", "ep"),
            P("tp", "ep"),
            P("tp", "ep", None),
            P("tp", "ep", None),
            P("tp", "ep", None),
        ),
        check_vma=False,
    )
```

```python
import jax
import jax.numpy as jnp
from jax import lax
from jax.experimental import pallas as pl
from jax.experimental.pallas import tpu as pltpu
from jax.sharding import PartitionSpec as P

CAP = 4
CONTRACT = (((1,), (1,)), ((), ()))
LEADING = (((0,), (0,)), ((), ()))
F32 = jnp.float32
BF16 = jnp.bfloat16


def swiglu_backward(gate_pre, up_pre, grad_act):
    sigmoid_gate = jax.nn.sigmoid(gate_pre)
    silu_gate = gate_pre * sigmoid_gate
    act = (silu_gate * up_pre).astype(BF16)
    silu_slope = sigmoid_gate * (1.0 + gate_pre * (1.0 - sigmoid_gate))
    grad_gate = (grad_act * up_pre * silu_slope).astype(BF16)
    grad_up = (grad_act * silu_gate).astype(BF16)
    return act, grad_gate, grad_up


def slot_tables(routes, gate_values, me, experts):
    tok_count = routes.shape[0]
    named = lax.rem(me + jnp.arange(experts, dtype=jnp.int32), experts)
    onehot = (routes.reshape(-1)[:, None] == named[None, :]).astype(jnp.int32)
    before = jnp.cumsum(onehot, axis=0) - onehot
    slot = onehot[:, :, None] * (before[:, :, None] == jnp.arange(CAP, dtype=jnp.int32)).astype(
        jnp.int32
    )
    slot = slot.reshape(tok_count, 2, experts * CAP).astype(F32)
    dispatch = jnp.sum(slot, axis=1).T.astype(BF16)
    weight = jnp.sum(slot * gate_values[:, :, None], axis=(0, 1))
    return dispatch, weight


def shift(x, axis, size, by):
    return lax.ppermute(x, axis, [(i, (i + by) % size) for i in range(size)])


def slots_to_send(hidden_in, cotangent, dispatch, weight, experts):
    width = hidden_in.shape[1]
    rows = jnp.dot(dispatch, hidden_in, preferred_element_type=F32).astype(BF16)
    cots = jnp.dot(dispatch, cotangent, preferred_element_type=F32)
    cots = (cots * weight[:, None]).astype(BF16)
    return jnp.stack(
        [rows.reshape(experts, CAP, width), cots.reshape(experts, CAP, width)], axis=1
    )


def exchange_slots(sent, me, experts):
    width = sent.shape[3]
    sent = jnp.roll(sent, me, axis=0)
    got = lax.all_to_all(sent, "tp", split_axis=0, concat_axis=0, tiled=True)
    return got.transpose(1, 0, 2, 3).reshape(2, experts * CAP, width)


def expert_layer(slot_rows, slot_cot, gate_weight, up_weight, down_weight):
    e_gate = lax.dot_general(slot_rows, gate_weight, CONTRACT, preferred_element_type=F32)
    e_up = lax.dot_general(slot_rows, up_weight, CONTRACT, preferred_element_type=F32)
    e_grad_act = lax.dot_general(slot_cot, down_weight, CONTRACT, preferred_element_type=F32)
    e_act, e_grad_gate, e_grad_up = swiglu_backward(e_gate, e_up, e_grad_act)
    g_down = lax.dot_general(e_act, slot_cot, LEADING, preferred_element_type=F32).astype(BF16)
    g_gate = lax.dot_general(e_grad_gate, slot_rows, LEADING, preferred_element_type=F32).astype(
        BF16
    )
    g_up = lax.dot_general(e_grad_up, slot_rows, LEADING, preferred_element_type=F32).astype(BF16)
    terms = jnp.dot(e_grad_gate, gate_weight, preferred_element_type=F32) + jnp.dot(
        e_grad_up, up_weight, preferred_element_type=F32
    )
    return g_gate, g_up, g_down, terms.astype(BF16)


def slots_back(own, dispatch, me, experts):
    width = own.shape[1]
    own = own.reshape(experts, CAP, width)
    back = lax.all_to_all(own, "tp", split_axis=0, concat_axis=0, tiled=True)
    dispatch = jnp.roll(dispatch.reshape(experts, CAP, -1), me, axis=0)
    return lax.dot_general(
        dispatch.reshape(experts * CAP, -1),
        back.reshape(experts * CAP, width),
        LEADING,
        preferred_element_type=F32,
    )


def plain_block(rows, cot, gate, up, down):
    gate_pre = lax.dot_general(rows, gate, CONTRACT, preferred_element_type=F32)
    up_pre = lax.dot_general(rows, up, CONTRACT, preferred_element_type=F32)
    grad_act = lax.dot_general(cot, down, CONTRACT, preferred_element_type=F32)
    act, grad_gate, grad_up = swiglu_backward(gate_pre, up_pre, grad_act)
    partial = jnp.dot(grad_gate, gate, preferred_element_type=F32) + jnp.dot(
        grad_up, up, preferred_element_type=F32
    )
    return act, grad_gate, grad_up, partial.astype(BF16)


VMEM_LIMIT = 20 * 1024 * 1024
VMEM_ALL = 60 * 1024 * 1024


def unit_tiles(units):
    return [(start, min(256, units - start)) for start in range(0, units, 256)]


def layer_kernel(rows, cots, gate, up, down, down_turned, turned, partial, col, ready=None):
    units, width = gate.shape
    for t, (start, size) in enumerate(unit_tiles(units)):
        if ready is not None:
            ready(t)
        gate_pre, up_pre = [
            lax.dot_general(w[start : start + size], rows, CONTRACT, preferred_element_type=F32)
            for w in (gate, up)
        ]
        if down_turned:
            grad_act = jnp.dot(
                cots, down[:, start : start + size], preferred_element_type=F32
            ).T
        else:
            grad_act = lax.dot_general(
                down[start : start + size], cots, CONTRACT, preferred_element_type=F32
            )
        for i, value in enumerate(swiglu_backward(gate_pre, up_pre, grad_act)):
            turned[i, start : start + size] = value
    grads = [turned[1].T, turned[2].T]
    for j in range(0, width, col):
        partial[:, j : j + col] = (
            jnp.dot(grads[0], gate[:, j : j + col], preferred_element_type=F32)
            + jnp.dot(grads[1], up[:, j : j + col], preferred_element_type=F32)
        ).astype(BF16)


def dense_block(core, blocks, gate, up, down):
    tok, width = blocks[0].shape[1] * len(blocks), blocks[0].shape[2]
    units = gate.shape[0]
    half = units // 2

    def kernel(core_ref, *refs):
        ins, refs = refs[: len(blocks)], refs[len(blocks) :]
        gate, up, down, own, other, partial, turned = refs
        rows, cots = [
            ins[0][k]
            if len(ins) == 1
            else jnp.concatenate([ref[k] for ref in ins], axis=0)
            for k in range(2)
        ]
        layer_kernel(rows, cots, gate, up, down, True, turned, partial, 512)
        mine = core_ref[0]
        own[...] = turned[:, pl.ds(pl.multiple_of(mine * half, 16), half), :]
        other[...] = turned[:, pl.ds(pl.multiple_of((1 - mine) * half, 16), half), :]

    vmem = pl.BlockSpec(memory_space=pltpu.VMEM)
    return pl.pallas_call(
        kernel,
        in_specs=[pl.BlockSpec(memory_space=pltpu.SMEM)] + [vmem] * (len(blocks) + 3),
        out_specs=[vmem, vmem, vmem],
        out_shape=[
            jax.ShapeDtypeStruct((3, half, tok), BF16),
            jax.ShapeDtypeStruct((3, half, tok), BF16),
            jax.ShapeDtypeStruct((tok, width), BF16),
        ],
        scratch_shapes=[pltpu.VMEM((3, units, tok), BF16)],
        compiler_params=pltpu.CompilerParams(vmem_limit_bytes=VMEM_LIMIT),
        cost_estimate=pl.CostEstimate(
            flops=10 * units * width * tok,
            bytes_accessed=6 * units * width + 6 * tok * (width + units),
            transcendentals=units * tok,
        ),
        name="dense_block",
    )(core.reshape(1), *blocks, gate, up, down)


def expert_block(rows, cots, gate, up, down):
    tok, width = rows.shape
    units = gate.shape[0]
    col = 512
    tiles = unit_tiles(units)

    def kernel(
        rows, cots, gate, up, down, g_gate, g_up, g_down, partial, loaded, turned, made, sems, out_sems
    ):
        copies = [
            [
                pltpu.make_async_copy(
                    source.at[pl.ds(start, size)], loaded.at[w, pl.ds(start, size)], sems.at[w, t]
                )
                for w, source in enumerate((gate, up, down))
            ]
            for t, (start, size) in enumerate(tiles)
        ]
        for group in copies:
            for copy in group:
                copy.start()

        def ready(t):
            for copy in copies[t]:
                copy.wait()

        layer_kernel(
            rows[...], cots[...], *[loaded.at[w] for w in range(3)], False, turned, partial, 512, ready
        )
        outs = (g_down, g_gate, g_up)
        pending = [None, None]
        step = 0
        for i in range(3):
            right = cots if i == 0 else rows
            for j in range(0, width, col):
                slot = step % 2
                if pending[slot] is not None:
                    pending[slot].wait()
                made[slot] = jnp.dot(
                    turned[i], right[:, j : j + col], preferred_element_type=F32
                ).astype(BF16)
                copy = pltpu.make_async_copy(
                    made.at[slot], outs[i].at[:, pl.ds(j, col)], out_sems.at[slot]
                )
                copy.start()
                pending[slot] = copy
                step += 1
        for copy in pending:
            copy.wait()

    vmem = pl.BlockSpec(memory_space=pltpu.VMEM)
    hbm = pl.BlockSpec(memory_space=pl.ANY)
    grad = jax.ShapeDtypeStruct((units, width), BF16)
    return pl.pallas_call(
        kernel,
        in_specs=[vmem, vmem, hbm, hbm, hbm],
        out_specs=[hbm, hbm, hbm, vmem],
        out_shape=[grad, grad, grad, jax.ShapeDtypeStruct((tok, width), BF16)],
        scratch_shapes=[
            pltpu.VMEM((3, units, width), BF16),
            pltpu.VMEM((3, units, tok), BF16),
            pltpu.VMEM((2, units, col), BF16),
            pltpu.SemaphoreType.DMA((3, len(tiles))),
            pltpu.SemaphoreType.DMA((2,)),
        ],
        compiler_params=pltpu.CompilerParams(vmem_limit_bytes=VMEM_ALL),
        cost_estimate=pl.CostEstimate(flops=1, bytes_accessed=1, transcendentals=0),
        name="expert_block",
    )(rows, cots, gate, up, down)


def final_sum(core, lows, highs):
    cut, width = lows[2].shape[1:]
    units = cut + highs[2].shape[1]
    half = width // 2

    def kernel(core_ref, *refs):
        ins, (mine, other) = refs[:-2], refs[-2:]
        own_first = core_ref[0] == 0
        for i in range(3):
            for begin, (own, near, far) in ((0, ins[:3]), (cut, ins[3:])):
                total = own[i, :, width:].astype(F32) + near[i, :, width:].astype(F32)
                total = total + far[i].astype(F32)
                left, right = total[:, :half].astype(BF16), total[:, half:].astype(BF16)
                size = total.shape[0]
                mine[i, begin : begin + size] = jnp.where(own_first, left, right)
                other[i, begin : begin + size] = jnp.where(own_first, right, left)

    vmem = pl.BlockSpec(memory_space=pltpu.VMEM)
    shape = jax.ShapeDtypeStruct((3, units, half), BF16)
    return pl.pallas_call(
        kernel,
        in_specs=[pl.BlockSpec(memory_space=pltpu.SMEM)] + [vmem] * 6,
        out_specs=[vmem, vmem],
        out_shape=[shape, shape],
        compiler_params=pltpu.CompilerParams(vmem_limit_bytes=VMEM_LIMIT),
        cost_estimate=pl.CostEstimate(
            flops=9 * units * width,
            bytes_accessed=24 * units * width,
            transcendentals=0,
        ),
        name="final_sum",
    )(core.reshape(1), *lows, *highs)


def join_halves(core, mine, other):
    _, units, width = mine.shape

    def kernel(core_ref, mine, other, *outs):
        first = core_ref[0] == 0
        for i in range(3):
            a, b = mine[i], other[i]
            joined = jnp.concatenate([jnp.where(first, a, b), jnp.where(first, b, a)], axis=0)
            outs[i][...] = joined.T

    vmem = pl.BlockSpec(memory_space=pltpu.VMEM)
    grads = pl.pallas_call(
        kernel,
        in_specs=[pl.BlockSpec(memory_space=pltpu.SMEM), vmem, vmem],
        out_specs=[vmem] * 3,
        out_shape=[jax.ShapeDtypeStruct((width, 2 * units), BF16)] * 3,
        compiler_params=pltpu.CompilerParams(vmem_limit_bytes=VMEM_ALL),
        cost_estimate=pl.CostEstimate(
            flops=0, bytes_accessed=24 * units * width, transcendentals=0
        ),
        name="join_halves",
    )(core.reshape(1), mine, other)
    return [grad.T for grad in grads]


def weight_terms(tiles, acts, blocks, width, begin, end):
    units = acts[0].shape[1]
    tokens = sum(b.shape[1] for b in blocks)
    size = end - begin

    def kernel(tile_ref, *refs):
        a, b, out = refs[: len(acts)], refs[len(acts) : -1], refs[-1]
        rows = jnp.concatenate([ref[0] for ref in b], axis=0)
        cots = jnp.concatenate([ref[1] for ref in b], axis=0)
        for i in range(3):
            left = jnp.concatenate([ref[i, begin:end] for ref in a], axis=1)
            out[i] = jnp.dot(
                left, cots if i == 0 else rows, preferred_element_type=F32
            ).astype(BF16)

    def whole(shape):
        return pl.BlockSpec(shape, lambda j, tile_ref: (0, 0, 0))

    def columns(block):
        return pl.BlockSpec((*block.shape[:2], width), lambda j, tile_ref: (0, 0, tile_ref[j]))

    return pl.pallas_call(
        kernel,
        grid_spec=pltpu.PrefetchScalarGridSpec(
            num_scalar_prefetch=1,
            grid=(2,),
            in_specs=[whole(a.shape) for a in acts] + [columns(b) for b in blocks],
            out_specs=pl.BlockSpec((3, size, width), lambda j, tile_ref: (0, 0, j)),
        ),
        out_shape=jax.ShapeDtypeStruct((3, size, 2 * width), BF16),
        compiler_params=pltpu.CompilerParams(vmem_limit_bytes=VMEM_ALL),
        cost_estimate=pl.CostEstimate(
            flops=12 * size * tokens * width,
            bytes_accessed=2 * (tokens * (4 * width + 3 * units) + 6 * size * width),
            transcendentals=0,
        ),
        name="weight_terms",
    )(jnp.stack(tiles), *acts, *blocks)


def together(*values):
    return lax.optimization_barrier(values)


def line_body(
    hidden_in,
    cotangent,
    routes,
    gate_values,
    dense_gate,
    dense_up,
    dense_down,
    expert_gate,
    expert_up,
    expert_down,
):
    experts = lax.axis_size("tp")
    me = lax.axis_index("tp")
    ep = lax.axis_index("ep")
    core, chip = lax.rem(ep, 2), lax.div(ep, 2)
    half = dense_gate.shape[0] // 2
    columns = dense_down.shape[1]
    own = jnp.stack([hidden_in, cotangent])

    down = lax.all_gather(dense_down.T, "ep", axis=0, tiled=True)

    def pairs(value):
        return lax.ppermute(value, "tp", [(0, 1), (1, 0), (2, 3), (3, 2)])

    def mirror(value):
        return lax.ppermute(value, "tp", [(0, 3), (1, 2), (2, 1), (3, 0)])

    def across(value, apart):
        return lax.ppermute(value, "ep", [(i, i ^ apart) for i in range(8)])

    def add(a, b):
        return (a.astype(F32) + b.astype(F32)).astype(BF16)

    def dense(blocks):
        mine, other, partial = dense_block(core, blocks, dense_gate, dense_up, down)
        tokens = [*blocks, *(across(b, 1) for b in blocks)]
        return ([mine, across(other, 1)], tokens), partial

    mirrored, paired = mirror(own), pairs(own)
    dispatch, weight = slot_tables(routes, gate_values, me, experts)
    sent = slots_to_send(hidden_in, cotangent, dispatch, weight, experts)
    got = exchange_slots(sent, me, experts)
    both0, partial0 = dense([own])

    got, partial0, both0 = together(got, partial0, both0)

    mirrored, paired, got = together(mirrored, paired, got)
    last = pairs(mirrored)
    slots = lax.all_gather(got, "ep", axis=0, tiled=False)
    both12, partial12 = dense([paired, mirrored])

    last, both12, slots = together(last, both12, slots)
    both3, partial3 = dense([last])
    paired_partial, mirrored_partial = jnp.split(partial12, 2, axis=0)
    from_last = pairs(partial3)

    acts, tokens = (a + b + c for a, b, c in zip(both0, both12, both3))
    cut, width = -(-half // 32) * 16, 2 * columns
    x_chip, y_chip, xy_chip = [jnp.bitwise_xor(chip, k) for k in (1, 2, 3)]
    low_sent = weight_terms((xy_chip, x_chip), acts, tokens, width, 0, cut)
    high_sent = weight_terms((xy_chip, y_chip), acts, tokens, width, cut, half)
    low_sent, chip, from_last = together(low_sent, chip, from_last)
    low_kept = weight_terms((y_chip, chip), acts, tokens, width, 0, cut)
    high_kept = weight_terms((x_chip, chip), acts, tokens, width, cut, half)
    low_near, high_near = across(low_sent, 2), across(high_sent, 4)
    from_mirror = mirror(add(mirrored_partial, from_last))

    slots, low_kept, high_kept = together(slots, low_kept, high_kept)
    slot_rows, slot_cot = slots[:, 0].reshape(-1, hidden_in.shape[1]), slots[:, 1].reshape(
        -1, hidden_in.shape[1]
    )
    g_gate, g_up, g_down, slot_terms = expert_block(
        slot_rows, slot_cot, expert_gate[0], expert_up[0], expert_down[0]
    )
    low_near, high_near, slot_terms, from_mirror, paired_partial = together(
        low_near, high_near, slot_terms, from_mirror, paired_partial
    )
    from_pair = pairs(paired_partial)
    low_far = across(add(low_kept[:, :, :width], low_near[:, :, :width]), 4)
    high_far = across(add(high_kept[:, :, :width], high_near[:, :, :width]), 2)
    routed = lax.psum_scatter(slot_terms, "ep", scatter_dimension=0, tiled=True)
    routed_input = slots_back(routed, dispatch, me, experts)
    mine, other = final_sum(
        core, (low_kept, low_near, low_far), (high_kept, high_near, high_far)
    )
    mine, from_pair = together(mine, from_pair)
    grads = join_halves(core, mine, across(other, 1))
    grad_input = (
        partial0.astype(F32)
        + from_pair.astype(F32)
        + from_mirror.astype(F32)
        + routed_input
    ).astype(BF16)
    return (grad_input, grads[1], grads[2], grads[0], g_gate[None], g_up[None], g_down[None])


def general_body(
    hidden_in,
    cotangent,
    routes,
    gate_values,
    dense_gate,
    dense_up,
    dense_down,
    expert_gate,
    expert_up,
    expert_down,
):
    experts = lax.axis_size("tp")
    me = lax.axis_index("tp")
    dispatch, weight = slot_tables(routes, gate_values, me, experts)
    sent = slots_to_send(hidden_in, cotangent, dispatch, weight, experts)
    got = exchange_slots(sent, me, experts)
    slots = lax.all_gather(got, "ep", axis=0, tiled=False)
    slot_rows, slot_cot = slots[:, 0].reshape(-1, hidden_in.shape[1]), slots[:, 1].reshape(
        -1, hidden_in.shape[1]
    )
    rows = lax.all_gather(hidden_in, "tp", axis=0, tiled=True)
    cots = lax.all_gather(cotangent, "tp", axis=0, tiled=True)
    down = lax.all_gather(dense_down, "ep", axis=1, tiled=True)
    act, grad_gate, grad_up, partial = plain_block(rows, cots, dense_gate, dense_up, down)
    dense_input = lax.psum_scatter(partial, "tp", scatter_dimension=0, tiled=True)
    grads = [
        lax.psum_scatter(
            lax.dot_general(a, b, LEADING, preferred_element_type=F32).astype(BF16),
            "ep",
            scatter_dimension=1,
            tiled=True,
        )
        for a, b in ((act, cots), (grad_gate, rows), (grad_up, rows))
    ]
    g_gate, g_up, g_down, slot_terms = expert_layer(
        slot_rows, slot_cot, expert_gate[0], expert_up[0], expert_down[0]
    )
    routed = lax.psum_scatter(slot_terms, "ep", scatter_dimension=0, tiled=True)
    routed_input = slots_back(routed, dispatch, me, experts)
    grad_input = (dense_input.astype(F32) + routed_input).astype(BF16)
    return (grad_input, grads[1], grads[2], grads[0], g_gate[None], g_up[None], g_down[None])


def solution(mesh):
    placed = (
        P(("ep", "tp"), None),
        P(("ep", "tp"), None),
        P(("ep", "tp"), None),
        P(("ep", "tp"), None),
        P("tp", None),
        P("tp", None),
        P("tp", "ep"),
        P("tp", "ep", None),
        P("tp", "ep", None),
        P("tp", "ep", None),
    )
    in_line = mesh.shape["tp"] == 4 and mesh.shape["ep"] == 8
    return jax.shard_map(
        line_body if in_line else general_body,
        mesh=mesh,
        in_specs=placed,
        out_specs=(
            P(("ep", "tp"), None),
            P("tp", "ep"),
            P("tp", "ep"),
            P("tp", "ep"),
            P("tp", "ep", None),
            P("tp", "ep", None),
            P("tp", "ep", None),
        ),
        check_vma=False,
    )
```

```python
import jax
import jax.numpy as jnp
from jax import lax
from jax.experimental import pallas as pl
from jax.experimental.pallas import tpu as pltpu
from jax.sharding import PartitionSpec as P

CAP = 4
CONTRACT = (((1,), (1,)), ((), ()))
LEADING = (((0,), (0,)), ((), ()))
F32 = jnp.float32
BF16 = jnp.bfloat16


def swiglu_backward(gate_pre, up_pre, grad_act):
    sigmoid_gate = jax.nn.sigmoid(gate_pre)
    silu_gate = gate_pre * sigmoid_gate
    act = (silu_gate * up_pre).astype(BF16)
    silu_slope = sigmoid_gate * (1.0 + gate_pre * (1.0 - sigmoid_gate))
    grad_gate = (grad_act * up_pre * silu_slope).astype(BF16)
    grad_up = (grad_act * silu_gate).astype(BF16)
    return act, grad_gate, grad_up


def slot_tables(routes, gate_values, me, experts):
    tok_count = routes.shape[0]
    named = lax.rem(me + jnp.arange(experts, dtype=jnp.int32), experts)
    onehot = (routes.reshape(-1)[:, None] == named[None, :]).astype(jnp.int32)
    before = jnp.cumsum(onehot, axis=0) - onehot
    slot = onehot[:, :, None] * (before[:, :, None] == jnp.arange(CAP, dtype=jnp.int32)).astype(
        jnp.int32
    )
    slot = slot.reshape(tok_count, 2, experts * CAP).astype(F32)
    dispatch = jnp.sum(slot, axis=1).T.astype(BF16)
    weight = jnp.sum(slot * gate_values[:, :, None], axis=(0, 1))
    return dispatch, weight


def shift(x, axis, size, by):
    return lax.ppermute(x, axis, [(i, (i + by) % size) for i in range(size)])


def slots_to_send(hidden_in, cotangent, dispatch, weight, experts):
    width = hidden_in.shape[1]
    rows = jnp.dot(dispatch, hidden_in, preferred_element_type=F32).astype(BF16)
    cots = jnp.dot(dispatch, cotangent, preferred_element_type=F32)
    cots = (cots * weight[:, None]).astype(BF16)
    return jnp.stack(
        [rows.reshape(experts, CAP, width), cots.reshape(experts, CAP, width)], axis=1
    )


def exchange_slots(sent, me, experts):
    width = sent.shape[3]
    sent = jnp.roll(sent, me, axis=0)
    got = lax.all_to_all(sent, "tp", split_axis=0, concat_axis=0, tiled=True)
    return got.transpose(1, 0, 2, 3).reshape(2, experts * CAP, width)


def expert_layer(slot_rows, slot_cot, gate_weight, up_weight, down_weight):
    e_gate = lax.dot_general(slot_rows, gate_weight, CONTRACT, preferred_element_type=F32)
    e_up = lax.dot_general(slot_rows, up_weight, CONTRACT, preferred_element_type=F32)
    e_grad_act = lax.dot_general(slot_cot, down_weight, CONTRACT, preferred_element_type=F32)
    e_act, e_grad_gate, e_grad_up = swiglu_backward(e_gate, e_up, e_grad_act)
    g_down = lax.dot_general(e_act, slot_cot, LEADING, preferred_element_type=F32).astype(BF16)
    g_gate = lax.dot_general(e_grad_gate, slot_rows, LEADING, preferred_element_type=F32).astype(
        BF16
    )
    g_up = lax.dot_general(e_grad_up, slot_rows, LEADING, preferred_element_type=F32).astype(BF16)
    terms = jnp.dot(e_grad_gate, gate_weight, preferred_element_type=F32) + jnp.dot(
        e_grad_up, up_weight, preferred_element_type=F32
    )
    return g_gate, g_up, g_down, terms.astype(BF16)


def slots_back(own, dispatch, me, experts):
    width = own.shape[1]
    own = own.reshape(experts, CAP, width)
    back = lax.all_to_all(own, "tp", split_axis=0, concat_axis=0, tiled=True)
    dispatch = jnp.roll(dispatch.reshape(experts, CAP, -1), me, axis=0)
    return lax.dot_general(
        dispatch.reshape(experts * CAP, -1),
        back.reshape(experts * CAP, width),
        LEADING,
        preferred_element_type=F32,
    )


def plain_block(rows, cot, gate, up, down):
    gate_pre = lax.dot_general(rows, gate, CONTRACT, preferred_element_type=F32)
    up_pre = lax.dot_general(rows, up, CONTRACT, preferred_element_type=F32)
    grad_act = lax.dot_general(cot, down, CONTRACT, preferred_element_type=F32)
    act, grad_gate, grad_up = swiglu_backward(gate_pre, up_pre, grad_act)
    partial = jnp.dot(grad_gate, gate, preferred_element_type=F32) + jnp.dot(
        grad_up, up, preferred_element_type=F32
    )
    return act, grad_gate, grad_up, partial.astype(BF16)


VMEM_LIMIT = 20 * 1024 * 1024
VMEM_ALL = 60 * 1024 * 1024


def unit_tiles(units):
    return [(start, min(256, units - start)) for start in range(0, units, 256)]


def layer_kernel(rows, cots, gate, up, down, down_turned, turned, partials, col, ready=None):
    units, width = gate.shape
    for t, (start, size) in enumerate(unit_tiles(units)):
        if ready is not None:
            ready(t)
        gate_pre, up_pre = [
            lax.dot_general(w[start : start + size], rows, CONTRACT, preferred_element_type=F32)
            for w in (gate, up)
        ]
        if down_turned:
            grad_act = jnp.dot(
                cots, down[:, start : start + size], preferred_element_type=F32
            ).T
        else:
            grad_act = lax.dot_general(
                down[start : start + size], cots, CONTRACT, preferred_element_type=F32
            )
        for i, value in enumerate(swiglu_backward(gate_pre, up_pre, grad_act)):
            turned[i, start : start + size] = value
    grads = [turned[1].T, turned[2].T]
    for j in range(0, width, col):
        made = (
            jnp.dot(grads[0], gate[:, j : j + col], preferred_element_type=F32)
            + jnp.dot(grads[1], up[:, j : j + col], preferred_element_type=F32)
        ).astype(BF16)
        begin = 0
        for partial in partials:
            end = begin + partial.shape[0]
            partial[:, j : j + col] = made[begin:end]
            begin = end


def dense_block(core, blocks, gate, up, down):
    tok, width = blocks[0].shape[1] * len(blocks), blocks[0].shape[2]
    units = gate.shape[0]
    half = units // 2

    def kernel(core_ref, *refs):
        ins, refs = refs[: len(blocks)], refs[len(blocks) :]
        gate, up, down, own, other = refs[:5]
        partials, turned = refs[5:-1], refs[-1]
        rows, cots = [
            ins[0][k]
            if len(ins) == 1
            else jnp.concatenate([ref[k] for ref in ins], axis=0)
            for k in range(2)
        ]
        layer_kernel(rows, cots, gate, up, down, True, turned, partials, 512)
        mine = core_ref[0]
        own[...] = turned[:, pl.ds(pl.multiple_of(mine * half, 16), half), :]
        other[...] = turned[:, pl.ds(pl.multiple_of((1 - mine) * half, 16), half), :]

    vmem = pl.BlockSpec(memory_space=pltpu.VMEM)
    return pl.pallas_call(
        kernel,
        in_specs=[pl.BlockSpec(memory_space=pltpu.SMEM)] + [vmem] * (len(blocks) + 3),
        out_specs=[vmem] * (2 + len(blocks)),
        out_shape=[
            jax.ShapeDtypeStruct((3, half, tok), BF16),
            jax.ShapeDtypeStruct((3, half, tok), BF16),
            *[jax.ShapeDtypeStruct(b.shape[1:], BF16) for b in blocks],
        ],
        scratch_shapes=[pltpu.VMEM((3, units, tok), BF16)],
        compiler_params=pltpu.CompilerParams(vmem_limit_bytes=VMEM_LIMIT),
        cost_estimate=pl.CostEstimate(
            flops=10 * units * width * tok,
            bytes_accessed=6 * units * width + 6 * tok * (width + units),
            transcendentals=units * tok,
        ),
        name="dense_block",
    )(core.reshape(1), *blocks, gate, up, down)


def expert_block(rows, cots, gate, up, down):
    tok, width = rows.shape
    units = gate.shape[0]
    col = 512
    tiles = unit_tiles(units)

    def kernel(
        rows, cots, gate, up, down, g_gate, g_up, g_down, partial, loaded, turned, made, sems, out_sems
    ):
        copies = [
            [
                pltpu.make_async_copy(
                    source.at[pl.ds(start, size)], loaded.at[w, pl.ds(start, size)], sems.at[w, t]
                )
                for w, source in enumerate((gate, up, down))
            ]
            for t, (start, size) in enumerate(tiles)
        ]
        for group in copies:
            for copy in group:
                copy.start()

        def ready(t):
            for copy in copies[t]:
                copy.wait()

        layer_kernel(
            rows[...], cots[...], *[loaded.at[w] for w in range(3)], False, turned, (partial,), 512, ready
        )
        outs = (g_down, g_gate, g_up)
        pending = [None, None]
        step = 0
        for i in range(3):
            right = cots if i == 0 else rows
            for j in range(0, width, col):
                slot = step % 2
                if pending[slot] is not None:
                    pending[slot].wait()
                made[slot] = jnp.dot(
                    turned[i], right[:, j : j + col], preferred_element_type=F32
                ).astype(BF16)
                copy = pltpu.make_async_copy(
                    made.at[slot], outs[i].at[:, pl.ds(j, col)], out_sems.at[slot]
                )
                copy.start()
                pending[slot] = copy
                step += 1
        for copy in pending:
            copy.wait()

    vmem = pl.BlockSpec(memory_space=pltpu.VMEM)
    hbm = pl.BlockSpec(memory_space=pl.ANY)
    grad = jax.ShapeDtypeStruct((units, width), BF16)
    return pl.pallas_call(
        kernel,
        in_specs=[vmem, vmem, hbm, hbm, hbm],
        out_specs=[hbm, hbm, hbm, vmem],
        out_shape=[grad, grad, grad, jax.ShapeDtypeStruct((tok, width), BF16)],
        scratch_shapes=[
            pltpu.VMEM((3, units, width), BF16),
            pltpu.VMEM((3, units, tok), BF16),
            pltpu.VMEM((2, units, col), BF16),
            pltpu.SemaphoreType.DMA((3, len(tiles))),
            pltpu.SemaphoreType.DMA((2,)),
        ],
        compiler_params=pltpu.CompilerParams(vmem_limit_bytes=VMEM_ALL),
        cost_estimate=pl.CostEstimate(flops=1, bytes_accessed=1, transcendentals=0),
        name="expert_block",
    )(rows, cots, gate, up, down)


def final_sum(core, lows, highs):
    cut, width = lows[2].shape[1:]
    units = cut + highs[2].shape[1]
    half = width // 2

    def kernel(core_ref, *refs):
        ins, (mine, other) = refs[:-2], refs[-2:]
        own_first = core_ref[0] == 0
        for i in range(3):
            for begin, (own, near, far) in ((0, ins[:3]), (cut, ins[3:])):
                total = own[i, :, width:].astype(F32) + near[i, :, width:].astype(F32)
                total = total + far[i].astype(F32)
                left, right = total[:, :half].astype(BF16), total[:, half:].astype(BF16)
                size = total.shape[0]
                mine[i, begin : begin + size] = jnp.where(own_first, left, right)
                other[i, begin : begin + size] = jnp.where(own_first, right, left)

    vmem = pl.BlockSpec(memory_space=pltpu.VMEM)
    shape = jax.ShapeDtypeStruct((3, units, half), BF16)
    return pl.pallas_call(
        kernel,
        in_specs=[pl.BlockSpec(memory_space=pltpu.SMEM)] + [vmem] * 6,
        out_specs=[vmem, vmem],
        out_shape=[shape, shape],
        compiler_params=pltpu.CompilerParams(vmem_limit_bytes=VMEM_LIMIT),
        cost_estimate=pl.CostEstimate(
            flops=9 * units * width,
            bytes_accessed=24 * units * width,
            transcendentals=0,
        ),
        name="final_sum",
    )(core.reshape(1), *lows, *highs)


def join_halves(core, mine, other):
    _, units, width = mine.shape

    def kernel(core_ref, mine, other, *outs):
        first = core_ref[0] == 0
        for i in range(3):
            a, b = mine[i], other[i]
            joined = jnp.concatenate([jnp.where(first, a, b), jnp.where(first, b, a)], axis=0)
            outs[i][...] = joined.T

    vmem = pl.BlockSpec(memory_space=pltpu.VMEM)
    grads = pl.pallas_call(
        kernel,
        in_specs=[pl.BlockSpec(memory_space=pltpu.SMEM), vmem, vmem],
        out_specs=[vmem] * 3,
        out_shape=[jax.ShapeDtypeStruct((width, 2 * units), BF16)] * 3,
        compiler_params=pltpu.CompilerParams(vmem_limit_bytes=VMEM_ALL),
        cost_estimate=pl.CostEstimate(
            flops=0, bytes_accessed=24 * units * width, transcendentals=0
        ),
        name="join_halves",
    )(core.reshape(1), mine, other)
    return [grad.T for grad in grads]


def weight_terms(tiles, acts, blocks, width, begin, end):
    units = acts[0].shape[1]
    tokens = sum(b.shape[1] for b in blocks)
    size = end - begin

    def kernel(tile_ref, *refs):
        a, b, out = refs[: len(acts)], refs[len(acts) : -1], refs[-1]
        rows = jnp.concatenate([ref[0] for ref in b], axis=0)
        cots = jnp.concatenate([ref[1] for ref in b], axis=0)
        for i in range(3):
            left = jnp.concatenate([ref[i, begin:end] for ref in a], axis=1)
            out[i] = jnp.dot(
                left, cots if i == 0 else rows, preferred_element_type=F32
            ).astype(BF16)

    def whole(shape):
        return pl.BlockSpec(shape, lambda j, tile_ref: (0, 0, 0))

    def columns(block):
        return pl.BlockSpec((*block.shape[:2], width), lambda j, tile_ref: (0, 0, tile_ref[j]))

    return pl.pallas_call(
        kernel,
        grid_spec=pltpu.PrefetchScalarGridSpec(
            num_scalar_prefetch=1,
            grid=(2,),
            in_specs=[whole(a.shape) for a in acts] + [columns(b) for b in blocks],
            out_specs=pl.BlockSpec((3, size, width), lambda j, tile_ref: (0, 0, j)),
        ),
        out_shape=jax.ShapeDtypeStruct((3, size, 2 * width), BF16),
        compiler_params=pltpu.CompilerParams(vmem_limit_bytes=VMEM_ALL),
        cost_estimate=pl.CostEstimate(
            flops=12 * size * tokens * width,
            bytes_accessed=2 * (tokens * (4 * width + 3 * units) + 6 * size * width),
            transcendentals=0,
        ),
        name="weight_terms",
    )(tiles, *acts, *blocks)


def routed_rows(hidden_in, cotangent, routes, gate_values, experts):
    tok, width = hidden_in.shape
    count = experts * 2 * CAP

    def kernel(rows, cots, routes, gates, out):
        line = lax.broadcasted_iota(jnp.int32, (count, tok), 0)
        expert, slot = line // (2 * CAP), lax.rem(line, CAP)
        first, second = routes[0:1] == expert, routes[1:2] == expert
        named = jnp.where(first | second, 1.0, 0.0)
        earlier = lax.broadcasted_iota(jnp.int32, (tok, tok), 0) < lax.broadcasted_iota(
            jnp.int32, (tok, tok), 1
        )
        before = jnp.dot(
            named.astype(BF16),
            jnp.where(earlier, 1.0, 0.0).astype(BF16),
            preferred_element_type=F32,
        )
        taken = jnp.where(before == slot.astype(F32), named, 0.0)
        weight = jnp.where(first, gates[0:1], 0.0) + jnp.where(second, gates[1:2], 0.0)
        weight = jnp.sum(taken * weight, axis=1, keepdims=True)
        taken = taken.astype(BF16)
        kept = lax.broadcasted_iota(jnp.int32, (count, 1), 0)
        is_cot = lax.rem(kept, 2 * CAP) >= CAP
        for j in range(0, width, 512):
            columns = slice(j, j + 512)
            row_part = jnp.dot(taken, rows[:, columns], preferred_element_type=F32)
            cot_part = jnp.dot(taken, cots[:, columns], preferred_element_type=F32) * weight
            out[:, columns] = jnp.where(is_cot, cot_part, row_part).astype(BF16)

    vmem = pl.BlockSpec(memory_space=pltpu.VMEM)
    return pl.pallas_call(
        kernel,
        in_specs=[vmem] * 4,
        out_specs=vmem,
        out_shape=jax.ShapeDtypeStruct((count, width), BF16),
        compiler_params=pltpu.CompilerParams(vmem_limit_bytes=VMEM_LIMIT),
        cost_estimate=pl.CostEstimate(
            flops=4 * count * tok * width, bytes_accessed=4 * tok * width, transcendentals=0
        ),
        name="routed_rows",
    )(hidden_in, cotangent, routes.T, gate_values.T)


def together(*values):
    return lax.optimization_barrier(values)


def line_body(
    hidden_in,
    cotangent,
    routes,
    gate_values,
    dense_gate,
    dense_up,
    dense_down,
    expert_gate,
    expert_up,
    expert_down,
):
    experts = lax.axis_size("tp")
    me = lax.axis_index("tp")
    ep = lax.axis_index("ep")
    core, chip = lax.rem(ep, 2), lax.div(ep, 2)
    half = dense_gate.shape[0] // 2
    columns = dense_down.shape[1]
    down = lax.all_gather(dense_down.T, "ep", axis=0, tiled=True)

    def pairs(value):
        return lax.ppermute(value, "tp", [(0, 1), (1, 0), (2, 3), (3, 2)])

    def mirror(value):
        return lax.ppermute(value, "tp", [(0, 3), (1, 2), (2, 1), (3, 0)])

    def across(value, apart):
        return lax.ppermute(value, "ep", [(i, i ^ apart) for i in range(8)])

    def add(a, b):
        return (a.astype(F32) + b.astype(F32)).astype(BF16)

    def dense(blocks):
        mine, other, *partials = dense_block(core, blocks, dense_gate, dense_up, down)
        tokens = [*blocks, *(across(b, 1) for b in blocks)]
        return ([mine, across(other, 1)], tokens), partials

    sent = routed_rows(hidden_in, cotangent, routes, gate_values, experts)
    got = lax.all_to_all(sent, "tp", split_axis=0, concat_axis=0, tiled=True)

    own, got = together(jnp.stack([hidden_in, cotangent]), got)
    mirrored, paired = mirror(own), pairs(own)
    slots = lax.all_gather(got, "ep", axis=0, tiled=False)
    both0, (partial0,) = dense([own])
    dispatch, _ = slot_tables(routes, gate_values, me, experts)
    slots = slots.reshape(-1, 2, CAP, hidden_in.shape[1])
    slot_rows, slot_cot = [slots[:, k].reshape(-1, hidden_in.shape[1]) for k in range(2)]
    g_gate, g_up, g_down, slot_terms = expert_block(
        slot_rows, slot_cot, expert_gate[0], expert_up[0], expert_down[0]
    )
    x_chip, y_chip, xy_chip = [jnp.bitwise_xor(chip, k) for k in (1, 2, 3)]
    chip_tiles = [
        jnp.stack(t)
        for t in ((xy_chip, x_chip), (xy_chip, y_chip), (y_chip, chip), (x_chip, chip))
    ]

    mirrored, paired, slot_terms, both0, dispatch, chip_tiles = together(
        mirrored, paired, slot_terms, both0, dispatch, chip_tiles
    )
    routed = lax.psum_scatter(slot_terms, "ep", scatter_dimension=0, tiled=True)
    last = pairs(mirrored)
    both12, (paired_partial, mirrored_partial) = dense([paired, mirrored])

    last, both12, routed = together(last, both12, routed)
    both3, (partial3,) = dense([last])
    from_last = pairs(partial3)

    acts, tokens = (a + b + c for a, b, c in zip(both0, both12, both3))
    cut, width = -(-half // 32) * 16, 2 * columns
    low_sent = weight_terms(chip_tiles[0], acts, tokens, width, 0, cut)
    high_sent = weight_terms(chip_tiles[1], acts, tokens, width, cut, half)
    low_sent, chip_tiles, from_last = together(low_sent, chip_tiles, from_last)
    low_kept = weight_terms(chip_tiles[2], acts, tokens, width, 0, cut)
    high_kept = weight_terms(chip_tiles[3], acts, tokens, width, cut, half)
    low_near, high_near = across(low_sent, 2), across(high_sent, 4)
    from_mirror = mirror(add(mirrored_partial, from_last))
    low_near, high_near, low_kept, high_kept, from_mirror, paired_partial, routed = together(
        low_near, high_near, low_kept, high_kept, from_mirror, paired_partial, routed
    )
    from_pair = pairs(paired_partial)
    low_far = across(add(low_kept[:, :, :width], low_near[:, :, :width]), 4)
    high_far = across(add(high_kept[:, :, :width], high_near[:, :, :width]), 2)
    routed_input = slots_back(routed, dispatch, me, experts)
    mine, other = final_sum(
        core, (low_kept, low_near, low_far), (high_kept, high_near, high_far)
    )
    mine, from_pair = together(mine, from_pair)
    grads = join_halves(core, mine, across(other, 1))
    grad_input = (
        partial0.astype(F32)
        + from_pair.astype(F32)
        + from_mirror.astype(F32)
        + routed_input
    ).astype(BF16)
    return (grad_input, grads[1], grads[2], grads[0], g_gate[None], g_up[None], g_down[None])


def general_body(
    hidden_in,
    cotangent,
    routes,
    gate_values,
    dense_gate,
    dense_up,
    dense_down,
    expert_gate,
    expert_up,
    expert_down,
):
    experts = lax.axis_size("tp")
    me = lax.axis_index("tp")
    dispatch, weight = slot_tables(routes, gate_values, me, experts)
    sent = slots_to_send(hidden_in, cotangent, dispatch, weight, experts)
    got = exchange_slots(sent, me, experts)
    slots = lax.all_gather(got, "ep", axis=0, tiled=False)
    slot_rows, slot_cot = slots[:, 0].reshape(-1, hidden_in.shape[1]), slots[:, 1].reshape(
        -1, hidden_in.shape[1]
    )
    rows = lax.all_gather(hidden_in, "tp", axis=0, tiled=True)
    cots = lax.all_gather(cotangent, "tp", axis=0, tiled=True)
    down = lax.all_gather(dense_down, "ep", axis=1, tiled=True)
    act, grad_gate, grad_up, partial = plain_block(rows, cots, dense_gate, dense_up, down)
    dense_input = lax.psum_scatter(partial, "tp", scatter_dimension=0, tiled=True)
    grads = [
        lax.psum_scatter(
            lax.dot_general(a, b, LEADING, preferred_element_type=F32).astype(BF16),
            "ep",
            scatter_dimension=1,
            tiled=True,
        )
        for a, b in ((act, cots), (grad_gate, rows), (grad_up, rows))
    ]
    g_gate, g_up, g_down, slot_terms = expert_layer(
        slot_rows, slot_cot, expert_gate[0], expert_up[0], expert_down[0]
    )
    routed = lax.psum_scatter(slot_terms, "ep", scatter_dimension=0, tiled=True)
    routed_input = slots_back(routed, dispatch, me, experts)
    grad_input = (dense_input.astype(F32) + routed_input).astype(BF16)
    return (grad_input, grads[1], grads[2], grads[0], g_gate[None], g_up[None], g_down[None])


def solution(mesh):
    placed = (
        P(("ep", "tp"), None),
        P(("ep", "tp"), None),
        P(("ep", "tp"), None),
        P(("ep", "tp"), None),
        P("tp", None),
        P("tp", None),
        P("tp", "ep"),
        P("tp", "ep", None),
        P("tp", "ep", None),
        P("tp", "ep", None),
    )
    in_line = mesh.shape["tp"] == 4 and mesh.shape["ep"] == 8
    return jax.shard_map(
        line_body if in_line else general_body,
        mesh=mesh,
        in_specs=placed,
        out_specs=(
            P(("ep", "tp"), None),
            P("tp", "ep"),
            P("tp", "ep"),
            P("tp", "ep"),
            P("tp", "ep", None),
            P("tp", "ep", None),
            P("tp", "ep", None),
        ),
        check_vma=False,
    )
```

```python
import jax
import jax.numpy as jnp
from jax import lax
from jax.experimental import pallas as pl
from jax.experimental.pallas import tpu as pltpu
from jax.sharding import PartitionSpec as P

CAP = 4
CONTRACT = (((1,), (1,)), ((), ()))
LEADING = (((0,), (0,)), ((), ()))
F32 = jnp.float32
BF16 = jnp.bfloat16


def swiglu_backward(gate_pre, up_pre, grad_act):
    sigmoid_gate = jax.nn.sigmoid(gate_pre)
    silu_gate = gate_pre * sigmoid_gate
    act = (silu_gate * up_pre).astype(BF16)
    silu_slope = sigmoid_gate * (1.0 + gate_pre * (1.0 - sigmoid_gate))
    grad_gate = (grad_act * up_pre * silu_slope).astype(BF16)
    grad_up = (grad_act * silu_gate).astype(BF16)
    return act, grad_gate, grad_up


def slot_tables(routes, gate_values, me, experts):
    tok_count = routes.shape[0]
    named = lax.rem(me + jnp.arange(experts, dtype=jnp.int32), experts)
    onehot = (routes.reshape(-1)[:, None] == named[None, :]).astype(jnp.int32)
    before = jnp.cumsum(onehot, axis=0) - onehot
    slot = onehot[:, :, None] * (before[:, :, None] == jnp.arange(CAP, dtype=jnp.int32)).astype(
        jnp.int32
    )
    slot = slot.reshape(tok_count, 2, experts * CAP).astype(F32)
    dispatch = jnp.sum(slot, axis=1).T.astype(BF16)
    weight = jnp.sum(slot * gate_values[:, :, None], axis=(0, 1))
    return dispatch, weight


def shift(x, axis, size, by):
    return lax.ppermute(x, axis, [(i, (i + by) % size) for i in range(size)])


def slots_to_send(hidden_in, cotangent, dispatch, weight, experts):
    width = hidden_in.shape[1]
    rows = jnp.dot(dispatch, hidden_in, preferred_element_type=F32).astype(BF16)
    cots = jnp.dot(dispatch, cotangent, preferred_element_type=F32)
    cots = (cots * weight[:, None]).astype(BF16)
    return jnp.stack(
        [rows.reshape(experts, CAP, width), cots.reshape(experts, CAP, width)], axis=1
    )


def exchange_slots(sent, me, experts):
    width = sent.shape[3]
    sent = jnp.roll(sent, me, axis=0)
    got = lax.all_to_all(sent, "tp", split_axis=0, concat_axis=0, tiled=True)
    return got.transpose(1, 0, 2, 3).reshape(2, experts * CAP, width)


def expert_layer(slot_rows, slot_cot, gate_weight, up_weight, down_weight):
    e_gate = lax.dot_general(slot_rows, gate_weight, CONTRACT, preferred_element_type=F32)
    e_up = lax.dot_general(slot_rows, up_weight, CONTRACT, preferred_element_type=F32)
    e_grad_act = lax.dot_general(slot_cot, down_weight, CONTRACT, preferred_element_type=F32)
    e_act, e_grad_gate, e_grad_up = swiglu_backward(e_gate, e_up, e_grad_act)
    g_down = lax.dot_general(e_act, slot_cot, LEADING, preferred_element_type=F32).astype(BF16)
    g_gate = lax.dot_general(e_grad_gate, slot_rows, LEADING, preferred_element_type=F32).astype(
        BF16
    )
    g_up = lax.dot_general(e_grad_up, slot_rows, LEADING, preferred_element_type=F32).astype(BF16)
    terms = jnp.dot(e_grad_gate, gate_weight, preferred_element_type=F32) + jnp.dot(
        e_grad_up, up_weight, preferred_element_type=F32
    )
    return g_gate, g_up, g_down, terms.astype(BF16)


def slots_back(own, experts):
    own = own.reshape(experts, CAP, own.shape[1])
    return lax.all_to_all(own, "tp", split_axis=0, concat_axis=0, tiled=True)


def to_tokens(back, dispatch, me, experts):
    dispatch = jnp.roll(dispatch.reshape(experts, CAP, -1), me, axis=0)
    return lax.dot_general(
        dispatch.reshape(experts * CAP, -1),
        back.reshape(experts * CAP, -1),
        LEADING,
        preferred_element_type=F32,
    )


def plain_block(rows, cot, gate, up, down):
    gate_pre = lax.dot_general(rows, gate, CONTRACT, preferred_element_type=F32)
    up_pre = lax.dot_general(rows, up, CONTRACT, preferred_element_type=F32)
    grad_act = lax.dot_general(cot, down, CONTRACT, preferred_element_type=F32)
    act, grad_gate, grad_up = swiglu_backward(gate_pre, up_pre, grad_act)
    partial = jnp.dot(grad_gate, gate, preferred_element_type=F32) + jnp.dot(
        grad_up, up, preferred_element_type=F32
    )
    return act, grad_gate, grad_up, partial.astype(BF16)


VMEM_LIMIT = 20 * 1024 * 1024
VMEM_ALL = 60 * 1024 * 1024


def unit_tiles(units):
    return [(start, min(256, units - start)) for start in range(0, units, 256)]


def layer_kernel(rows, cots, gate, up, down, down_turned, turned, partials, col, ready=None):
    units, width = gate.shape
    for t, (start, size) in enumerate(unit_tiles(units)):
        if ready is not None:
            ready(t)
        gate_pre, up_pre = [
            lax.dot_general(w[start : start + size], rows, CONTRACT, preferred_element_type=F32)
            for w in (gate, up)
        ]
        if down_turned:
            grad_act = jnp.dot(
                cots, down[:, start : start + size], preferred_element_type=F32
            ).T
        else:
            grad_act = lax.dot_general(
                down[start : start + size], cots, CONTRACT, preferred_element_type=F32
            )
        for i, value in enumerate(swiglu_backward(gate_pre, up_pre, grad_act)):
            turned[i, start : start + size] = value
    grads = [turned[1].T, turned[2].T]
    for j in range(0, width, col):
        made = (
            jnp.dot(grads[0], gate[:, j : j + col], preferred_element_type=F32)
            + jnp.dot(grads[1], up[:, j : j + col], preferred_element_type=F32)
        ).astype(BF16)
        begin = 0
        for partial in partials:
            end = begin + partial.shape[0]
            partial[:, j : j + col] = made[begin:end]
            begin = end


def dense_block(core, blocks, gate, up, down):
    tok, width = blocks[0].shape[1] * len(blocks), blocks[0].shape[2]
    units = gate.shape[0]
    half = units // 2
    tiles = unit_tiles(units)

    def kernel(core_ref, *refs):
        ins, refs = refs[: len(blocks)], refs[len(blocks) :]
        gate, up, down, own, other = refs[:5]
        partials, (gate_in, up_in, down_in, turned, sems) = refs[5:-5], refs[-5:]
        copies = [
            [
                pltpu.make_async_copy(
                    source.at[pl.ds(start, size)], target.at[pl.ds(start, size)], sems.at[w, t]
                )
                for w, (source, target) in enumerate(((gate, gate_in), (up, up_in)))
            ]
            for t, (start, size) in enumerate(tiles)
        ]
        copies[0].append(pltpu.make_async_copy(down, down_in, sems.at[2, 0]))
        for group in copies:
            for copy in group:
                copy.start()

        def ready(t):
            for copy in copies[t]:
                copy.wait()

        rows, cots = [
            ins[0][k]
            if len(ins) == 1
            else jnp.concatenate([ref[k] for ref in ins], axis=0)
            for k in range(2)
        ]
        layer_kernel(rows, cots, gate_in, up_in, down_in, True, turned, partials, 512, ready)
        mine = core_ref[0]
        own[...] = turned[:, pl.ds(pl.multiple_of(mine * half, 16), half), :]
        other[...] = turned[:, pl.ds(pl.multiple_of((1 - mine) * half, 16), half), :]

    vmem = pl.BlockSpec(memory_space=pltpu.VMEM)
    hbm = pl.BlockSpec(memory_space=pl.ANY)
    return pl.pallas_call(
        kernel,
        in_specs=[pl.BlockSpec(memory_space=pltpu.SMEM)] + [vmem] * len(blocks) + [hbm] * 3,
        out_specs=[vmem] * (2 + len(blocks)),
        out_shape=[
            jax.ShapeDtypeStruct((3, half, tok), BF16),
            jax.ShapeDtypeStruct((3, half, tok), BF16),
            *[jax.ShapeDtypeStruct(b.shape[1:], BF16) for b in blocks],
        ],
        scratch_shapes=[
            pltpu.VMEM((units, width), BF16),
            pltpu.VMEM((units, width), BF16),
            pltpu.VMEM((width, units), BF16),
            pltpu.VMEM((3, units, tok), BF16),
            pltpu.SemaphoreType.DMA((3, len(tiles))),
        ],
        compiler_params=pltpu.CompilerParams(vmem_limit_bytes=VMEM_ALL),
        cost_estimate=pl.CostEstimate(
            flops=10 * units * width * tok,
            bytes_accessed=6 * units * width + 6 * tok * (width + units),
            transcendentals=units * tok,
        ),
        name="dense_block",
    )(core.reshape(1), *blocks, gate, up, down)


def expert_block(rows, cots, gate, up, down):
    tok, width = rows.shape
    units = gate.shape[0]
    col = 512
    tiles = unit_tiles(units)

    def kernel(
        rows, cots, gate, up, down, g_gate, g_up, g_down, partial, loaded, turned, made, sems, out_sems
    ):
        copies = [
            [
                pltpu.make_async_copy(
                    source.at[pl.ds(start, size)], loaded.at[w, pl.ds(start, size)], sems.at[w, t]
                )
                for w, source in enumerate((gate, up, down))
            ]
            for t, (start, size) in enumerate(tiles)
        ]
        for group in copies:
            for copy in group:
                copy.start()

        def ready(t):
            for copy in copies[t]:
                copy.wait()

        layer_kernel(
            rows[...], cots[...], *[loaded.at[w] for w in range(3)], False, turned, (partial,), 512, ready
        )
        outs = (g_down, g_gate, g_up)
        pending = [None, None]
        step = 0
        for i in range(3):
            right = cots if i == 0 else rows
            for j in range(0, width, col):
                slot = step % 2
                if pending[slot] is not None:
                    pending[slot].wait()
                made[slot] = jnp.dot(
                    turned[i], right[:, j : j + col], preferred_element_type=F32
                ).astype(BF16)
                copy = pltpu.make_async_copy(
                    made.at[slot], outs[i].at[:, pl.ds(j, col)], out_sems.at[slot]
                )
                copy.start()
                pending[slot] = copy
                step += 1
        for copy in pending:
            copy.wait()

    vmem = pl.BlockSpec(memory_space=pltpu.VMEM)
    hbm = pl.BlockSpec(memory_space=pl.ANY)
    grad = jax.ShapeDtypeStruct((units, width), BF16)
    return pl.pallas_call(
        kernel,
        in_specs=[vmem, vmem, hbm, hbm, hbm],
        out_specs=[hbm, hbm, hbm, vmem],
        out_shape=[grad, grad, grad, jax.ShapeDtypeStruct((tok, width), BF16)],
        scratch_shapes=[
            pltpu.VMEM((3, units, width), BF16),
            pltpu.VMEM((3, units, tok), BF16),
            pltpu.VMEM((2, units, col), BF16),
            pltpu.SemaphoreType.DMA((3, len(tiles))),
            pltpu.SemaphoreType.DMA((2,)),
        ],
        compiler_params=pltpu.CompilerParams(vmem_limit_bytes=VMEM_ALL),
        cost_estimate=pl.CostEstimate(flops=1, bytes_accessed=1, transcendentals=0),
        name="expert_block",
    )(rows, cots, gate, up, down)


def final_sum(core, lows, highs):
    cut, width = lows[2].shape[1:]
    units = cut + highs[2].shape[1]
    half = width // 2

    def kernel(core_ref, *refs):
        ins, (mine, other) = refs[:-2], refs[-2:]
        own_first = core_ref[0] == 0
        for i in range(3):
            for begin, (own, near, far) in ((0, ins[:3]), (cut, ins[3:])):
                total = own[i, :, width:].astype(F32) + near[i, :, width:].astype(F32)
                total = total + far[i].astype(F32)
                left, right = total[:, :half].astype(BF16), total[:, half:].astype(BF16)
                size = total.shape[0]
                mine[i, begin : begin + size] = jnp.where(own_first, left, right)
                other[i, begin : begin + size] = jnp.where(own_first, right, left)

    vmem = pl.BlockSpec(memory_space=pltpu.VMEM)
    shape = jax.ShapeDtypeStruct((3, units, half), BF16)
    return pl.pallas_call(
        kernel,
        in_specs=[pl.BlockSpec(memory_space=pltpu.SMEM)] + [vmem] * 6,
        out_specs=[vmem, vmem],
        out_shape=[shape, shape],
        compiler_params=pltpu.CompilerParams(vmem_limit_bytes=VMEM_LIMIT),
        cost_estimate=pl.CostEstimate(
            flops=9 * units * width,
            bytes_accessed=24 * units * width,
            transcendentals=0,
        ),
        name="final_sum",
    )(core.reshape(1), *lows, *highs)


def join_halves(core, mine, other):
    _, units, width = mine.shape

    def kernel(core_ref, mine, other, *outs):
        first = core_ref[0] == 0
        for i in range(3):
            a, b = mine[i], other[i]
            joined = jnp.concatenate([jnp.where(first, a, b), jnp.where(first, b, a)], axis=0)
            outs[i][...] = joined.T

    vmem = pl.BlockSpec(memory_space=pltpu.VMEM)
    grads = pl.pallas_call(
        kernel,
        in_specs=[pl.BlockSpec(memory_space=pltpu.SMEM), vmem, vmem],
        out_specs=[vmem] * 3,
        out_shape=[jax.ShapeDtypeStruct((width, 2 * units), BF16)] * 3,
        compiler_params=pltpu.CompilerParams(vmem_limit_bytes=VMEM_ALL),
        cost_estimate=pl.CostEstimate(
            flops=0, bytes_accessed=24 * units * width, transcendentals=0
        ),
        name="join_halves",
    )(core.reshape(1), mine, other)
    return [grad.T for grad in grads]


def weight_terms(tiles, acts, blocks, width, begin, end):
    units = acts[0].shape[1]
    tokens = sum(b.shape[1] for b in blocks)
    size = end - begin

    def kernel(tile_ref, *refs):
        a, b, out = refs[: len(acts)], refs[len(acts) : -1], refs[-1]
        rows = jnp.concatenate([ref[0] for ref in b], axis=0)
        cots = jnp.concatenate([ref[1] for ref in b], axis=0)
        for i in range(3):
            left = jnp.concatenate([ref[i, begin:end] for ref in a], axis=1)
            out[i] = jnp.dot(
                left, cots if i == 0 else rows, preferred_element_type=F32
            ).astype(BF16)

    def whole(shape):
        return pl.BlockSpec(shape, lambda j, tile_ref: (0, 0, 0))

    def columns(block):
        return pl.BlockSpec((*block.shape[:2], width), lambda j, tile_ref: (0, 0, tile_ref[j]))

    return pl.pallas_call(
        kernel,
        grid_spec=pltpu.PrefetchScalarGridSpec(
            num_scalar_prefetch=1,
            grid=(2,),
            in_specs=[whole(a.shape) for a in acts] + [columns(b) for b in blocks],
            out_specs=pl.BlockSpec((3, size, width), lambda j, tile_ref: (0, 0, j)),
        ),
        out_shape=jax.ShapeDtypeStruct((3, size, 2 * width), BF16),
        compiler_params=pltpu.CompilerParams(vmem_limit_bytes=VMEM_ALL),
        cost_estimate=pl.CostEstimate(
            flops=12 * size * tokens * width,
            bytes_accessed=2 * (tokens * (4 * width + 3 * units) + 6 * size * width),
            transcendentals=0,
        ),
        name="weight_terms",
    )(tiles, *acts, *blocks)


def routed_rows(hidden_in, cotangent, routes, gate_values, experts):
    tok, width = hidden_in.shape
    count = experts * 2 * CAP

    def kernel(rows, cots, routes, gates, out):
        line = lax.broadcasted_iota(jnp.int32, (count, tok), 0)
        expert, slot = line // (2 * CAP), lax.rem(line, CAP)
        first, second = routes[0:1] == expert, routes[1:2] == expert
        named = jnp.where(first | second, 1.0, 0.0)
        earlier = lax.broadcasted_iota(jnp.int32, (tok, tok), 0) < lax.broadcasted_iota(
            jnp.int32, (tok, tok), 1
        )
        before = jnp.dot(
            named.astype(BF16),
            jnp.where(earlier, 1.0, 0.0).astype(BF16),
            preferred_element_type=F32,
        )
        taken = jnp.where(before == slot.astype(F32), named, 0.0)
        weight = jnp.where(first, gates[0:1], 0.0) + jnp.where(second, gates[1:2], 0.0)
        weight = jnp.sum(taken * weight, axis=1, keepdims=True)
        taken = taken.astype(BF16)
        kept = lax.broadcasted_iota(jnp.int32, (count, 1), 0)
        is_cot = lax.rem(kept, 2 * CAP) >= CAP
        for j in range(0, width, 512):
            columns = slice(j, j + 512)
            row_part = jnp.dot(taken, rows[:, columns], preferred_element_type=F32)
            cot_part = jnp.dot(taken, cots[:, columns], preferred_element_type=F32) * weight
            out[:, columns] = jnp.where(is_cot, cot_part, row_part).astype(BF16)

    vmem = pl.BlockSpec(memory_space=pltpu.VMEM)
    return pl.pallas_call(
        kernel,
        in_specs=[vmem] * 4,
        out_specs=vmem,
        out_shape=jax.ShapeDtypeStruct((count, width), BF16),
        compiler_params=pltpu.CompilerParams(vmem_limit_bytes=VMEM_LIMIT),
        cost_estimate=pl.CostEstimate(
            flops=4 * count * tok * width, bytes_accessed=4 * tok * width, transcendentals=0
        ),
        name="routed_rows",
    )(hidden_in, cotangent, routes.T, gate_values.T)


def together(*values):
    return lax.optimization_barrier(values)


def line_body(
    hidden_in,
    cotangent,
    routes,
    gate_values,
    dense_gate,
    dense_up,
    dense_down,
    expert_gate,
    expert_up,
    expert_down,
):
    experts = lax.axis_size("tp")
    me = lax.axis_index("tp")
    ep = lax.axis_index("ep")
    core, chip = lax.rem(ep, 2), lax.div(ep, 2)
    half = dense_gate.shape[0] // 2
    columns = dense_down.shape[1]
    down = lax.all_gather(dense_down.T, "ep", axis=0, tiled=True)

    def pairs(value):
        return lax.ppermute(value, "tp", [(0, 1), (1, 0), (2, 3), (3, 2)])

    def mirror(value):
        return lax.ppermute(value, "tp", [(0, 3), (1, 2), (2, 1), (3, 0)])

    def across(value, apart):
        return lax.ppermute(value, "ep", [(i, i ^ apart) for i in range(8)])

    def add(a, b):
        return (a.astype(F32) + b.astype(F32)).astype(BF16)

    def dense(blocks):
        mine, other, *partials = dense_block(core, blocks, dense_gate, dense_up, down)
        tokens = [*blocks, *(across(b, 1) for b in blocks)]
        return ([mine, across(other, 1)], tokens), partials

    sent = routed_rows(hidden_in, cotangent, routes, gate_values, experts)
    got = lax.all_to_all(sent, "tp", split_axis=0, concat_axis=0, tiled=True)

    own, got = together(jnp.stack([hidden_in, cotangent]), got)
    mirrored, paired = mirror(own), pairs(own)
    got, down = together(got, down)
    slots = lax.all_gather(got, "ep", axis=0, tiled=False)
    both0, (partial0,) = dense([own])
    dispatch, _ = slot_tables(routes, gate_values, me, experts)
    slots = slots.reshape(-1, 2, CAP, hidden_in.shape[1])
    slot_rows, slot_cot = [slots[:, k].reshape(-1, hidden_in.shape[1]) for k in range(2)]
    g_gate, g_up, g_down, slot_terms = expert_block(
        slot_rows, slot_cot, expert_gate[0], expert_up[0], expert_down[0]
    )
    x_chip, y_chip, xy_chip = [jnp.bitwise_xor(chip, k) for k in (1, 2, 3)]
    chip_tiles = [
        jnp.stack(t)
        for t in ((xy_chip, x_chip), (xy_chip, y_chip), (y_chip, chip), (x_chip, chip))
    ]

    mirrored, paired, slot_terms, both0, dispatch, chip_tiles = together(
        mirrored, paired, slot_terms, both0, dispatch, chip_tiles
    )
    routed = lax.psum_scatter(slot_terms, "ep", scatter_dimension=0, tiled=True)
    last = pairs(mirrored)
    both12, (paired_partial, mirrored_partial) = dense([paired, mirrored])

    back = slots_back(routed, experts)
    last, both12, back = together(last, both12, back)
    both3, (partial3,) = dense([last])
    from_last = pairs(partial3)

    acts, tokens = (a + b + c for a, b, c in zip(both0, both12, both3))
    cut, width = -(-half // 32) * 16, 2 * columns
    low_sent = weight_terms(chip_tiles[0], acts, tokens, width, 0, cut)
    high_sent = weight_terms(chip_tiles[1], acts, tokens, width, cut, half)
    low_sent, chip_tiles, from_last = together(low_sent, chip_tiles, from_last)
    low_kept = weight_terms(chip_tiles[2], acts, tokens, width, 0, cut)
    high_kept = weight_terms(chip_tiles[3], acts, tokens, width, cut, half)
    low_near, high_near = across(low_sent, 2), across(high_sent, 4)
    from_mirror = mirror(add(mirrored_partial, from_last))
    low_near, high_near, low_kept, high_kept, from_mirror, paired_partial = together(
        low_near, high_near, low_kept, high_kept, from_mirror, paired_partial
    )
    from_pair = pairs(paired_partial)
    low_far = across(add(low_kept[:, :, :width], low_near[:, :, :width]), 4)
    high_far = across(add(high_kept[:, :, :width], high_near[:, :, :width]), 2)
    routed_input = to_tokens(back, dispatch, me, experts)
    mine, other = final_sum(
        core, (low_kept, low_near, low_far), (high_kept, high_near, high_far)
    )
    mine, from_pair = together(mine, from_pair)
    grads = join_halves(core, mine, across(other, 1))
    grad_input = (
        partial0.astype(F32)
        + from_pair.astype(F32)
        + from_mirror.astype(F32)
        + routed_input
    ).astype(BF16)
    return (grad_input, grads[1], grads[2], grads[0], g_gate[None], g_up[None], g_down[None])


def general_body(
    hidden_in,
    cotangent,
    routes,
    gate_values,
    dense_gate,
    dense_up,
    dense_down,
    expert_gate,
    expert_up,
    expert_down,
):
    experts = lax.axis_size("tp")
    me = lax.axis_index("tp")
    dispatch, weight = slot_tables(routes, gate_values, me, experts)
    sent = slots_to_send(hidden_in, cotangent, dispatch, weight, experts)
    got = exchange_slots(sent, me, experts)
    slots = lax.all_gather(got, "ep", axis=0, tiled=False)
    slot_rows, slot_cot = slots[:, 0].reshape(-1, hidden_in.shape[1]), slots[:, 1].reshape(
        -1, hidden_in.shape[1]
    )
    rows = lax.all_gather(hidden_in, "tp", axis=0, tiled=True)
    cots = lax.all_gather(cotangent, "tp", axis=0, tiled=True)
    down = lax.all_gather(dense_down, "ep", axis=1, tiled=True)
    act, grad_gate, grad_up, partial = plain_block(rows, cots, dense_gate, dense_up, down)
    dense_input = lax.psum_scatter(partial, "tp", scatter_dimension=0, tiled=True)
    grads = [
        lax.psum_scatter(
            lax.dot_general(a, b, LEADING, preferred_element_type=F32).astype(BF16),
            "ep",
            scatter_dimension=1,
            tiled=True,
        )
        for a, b in ((act, cots), (grad_gate, rows), (grad_up, rows))
    ]
    g_gate, g_up, g_down, slot_terms = expert_layer(
        slot_rows, slot_cot, expert_gate[0], expert_up[0], expert_down[0]
    )
    routed = lax.psum_scatter(slot_terms, "ep", scatter_dimension=0, tiled=True)
    routed_input = to_tokens(slots_back(routed, experts), dispatch, me, experts)
    grad_input = (dense_input.astype(F32) + routed_input).astype(BF16)
    return (grad_input, grads[1], grads[2], grads[0], g_gate[None], g_up[None], g_down[None])


def solution(mesh):
    placed = (
        P(("ep", "tp"), None),
        P(("ep", "tp"), None),
        P(("ep", "tp"), None),
        P(("ep", "tp"), None),
        P("tp", None),
        P("tp", None),
        P("tp", "ep"),
        P("tp", "ep", None),
        P("tp", "ep", None),
        P("tp", "ep", None),
    )
    in_line = mesh.shape["tp"] == 4 and mesh.shape["ep"] == 8
    return jax.shard_map(
        line_body if in_line else general_body,
        mesh=mesh,
        in_specs=placed,
        out_specs=(
            P(("ep", "tp"), None),
            P("tp", "ep"),
            P("tp", "ep"),
            P("tp", "ep"),
            P("tp", "ep", None),
            P("tp", "ep", None),
            P("tp", "ep", None),
        ),
        check_vma=False,
    )
```

```python
import jax
import jax.numpy as jnp
from jax import lax
from jax.experimental import pallas as pl
from jax.experimental.pallas import tpu as pltpu
from jax.sharding import PartitionSpec as P

CAP = 4
CONTRACT = (((1,), (1,)), ((), ()))
LEADING = (((0,), (0,)), ((), ()))
F32 = jnp.float32
BF16 = jnp.bfloat16


def swiglu_backward(gate_pre, up_pre, grad_act):
    sigmoid_gate = jax.nn.sigmoid(gate_pre)
    silu_gate = gate_pre * sigmoid_gate
    act = (silu_gate * up_pre).astype(BF16)
    silu_slope = sigmoid_gate * (1.0 + gate_pre * (1.0 - sigmoid_gate))
    grad_gate = (grad_act * up_pre * silu_slope).astype(BF16)
    grad_up = (grad_act * silu_gate).astype(BF16)
    return act, grad_gate, grad_up


def slot_tables(routes, gate_values, me, experts):
    tok_count = routes.shape[0]
    named = lax.rem(me + jnp.arange(experts, dtype=jnp.int32), experts)
    onehot = (routes.reshape(-1)[:, None] == named[None, :]).astype(jnp.int32)
    before = jnp.cumsum(onehot, axis=0) - onehot
    slot = onehot[:, :, None] * (before[:, :, None] == jnp.arange(CAP, dtype=jnp.int32)).astype(
        jnp.int32
    )
    slot = slot.reshape(tok_count, 2, experts * CAP).astype(F32)
    dispatch = jnp.sum(slot, axis=1).T.astype(BF16)
    weight = jnp.sum(slot * gate_values[:, :, None], axis=(0, 1))
    return dispatch, weight


def shift(x, axis, size, by):
    return lax.ppermute(x, axis, [(i, (i + by) % size) for i in range(size)])


def slots_to_send(hidden_in, cotangent, dispatch, weight, experts):
    width = hidden_in.shape[1]
    rows = jnp.dot(dispatch, hidden_in, preferred_element_type=F32).astype(BF16)
    cots = jnp.dot(dispatch, cotangent, preferred_element_type=F32)
    cots = (cots * weight[:, None]).astype(BF16)
    return jnp.stack(
        [rows.reshape(experts, CAP, width), cots.reshape(experts, CAP, width)], axis=1
    )


def exchange_slots(sent, me, experts):
    width = sent.shape[3]
    sent = jnp.roll(sent, me, axis=0)
    got = lax.all_to_all(sent, "tp", split_axis=0, concat_axis=0, tiled=True)
    return got.transpose(1, 0, 2, 3).reshape(2, experts * CAP, width)


def expert_layer(slot_rows, slot_cot, gate_weight, up_weight, down_weight):
    e_gate = lax.dot_general(slot_rows, gate_weight, CONTRACT, preferred_element_type=F32)
    e_up = lax.dot_general(slot_rows, up_weight, CONTRACT, preferred_element_type=F32)
    e_grad_act = lax.dot_general(slot_cot, down_weight, CONTRACT, preferred_element_type=F32)
    e_act, e_grad_gate, e_grad_up = swiglu_backward(e_gate, e_up, e_grad_act)
    g_down = lax.dot_general(e_act, slot_cot, LEADING, preferred_element_type=F32).astype(BF16)
    g_gate = lax.dot_general(e_grad_gate, slot_rows, LEADING, preferred_element_type=F32).astype(
        BF16
    )
    g_up = lax.dot_general(e_grad_up, slot_rows, LEADING, preferred_element_type=F32).astype(BF16)
    terms = jnp.dot(e_grad_gate, gate_weight, preferred_element_type=F32) + jnp.dot(
        e_grad_up, up_weight, preferred_element_type=F32
    )
    return g_gate, g_up, g_down, terms.astype(BF16)


def slots_back(own, experts):
    own = own.reshape(experts, CAP, own.shape[1])
    return lax.all_to_all(own, "tp", split_axis=0, concat_axis=0, tiled=True)


def to_tokens(back, dispatch, me, experts):
    dispatch = jnp.roll(dispatch.reshape(experts, CAP, -1), me, axis=0)
    return lax.dot_general(
        dispatch.reshape(experts * CAP, -1),
        back.reshape(experts * CAP, -1),
        LEADING,
        preferred_element_type=F32,
    )


def plain_block(rows, cot, gate, up, down):
    gate_pre = lax.dot_general(rows, gate, CONTRACT, preferred_element_type=F32)
    up_pre = lax.dot_general(rows, up, CONTRACT, preferred_element_type=F32)
    grad_act = lax.dot_general(cot, down, CONTRACT, preferred_element_type=F32)
    act, grad_gate, grad_up = swiglu_backward(gate_pre, up_pre, grad_act)
    partial = jnp.dot(grad_gate, gate, preferred_element_type=F32) + jnp.dot(
        grad_up, up, preferred_element_type=F32
    )
    return act, grad_gate, grad_up, partial.astype(BF16)


VMEM_LIMIT = 20 * 1024 * 1024
VMEM_ALL = 60 * 1024 * 1024


def unit_tiles(units):
    return [(start, min(256, units - start)) for start in range(0, units, 256)]


def layer_kernel(rows, cots, gate, up, down, down_turned, turned, partials, col, ready=None):
    units, width = gate.shape
    for t, (start, size) in enumerate(unit_tiles(units)):
        if ready is not None:
            ready(t)
        gate_pre, up_pre = [
            lax.dot_general(w[start : start + size], rows, CONTRACT, preferred_element_type=F32)
            for w in (gate, up)
        ]
        if down_turned:
            grad_act = jnp.dot(
                cots, down[:, start : start + size], preferred_element_type=F32
            ).T
        else:
            grad_act = lax.dot_general(
                down[start : start + size], cots, CONTRACT, preferred_element_type=F32
            )
        for i, value in enumerate(swiglu_backward(gate_pre, up_pre, grad_act)):
            turned[i, start : start + size] = value
    grads = [turned[1].T, turned[2].T]
    for j in range(0, width, col):
        made = (
            jnp.dot(grads[0], gate[:, j : j + col], preferred_element_type=F32)
            + jnp.dot(grads[1], up[:, j : j + col], preferred_element_type=F32)
        ).astype(BF16)
        begin = 0
        for partial in partials:
            end = begin + partial.shape[0]
            partial[:, j : j + col] = made[begin:end]
            begin = end


def dense_block(core, blocks, gate, up, down):
    tok, width = blocks[0].shape[1] * len(blocks), blocks[0].shape[2]
    units = gate.shape[0]
    half = units // 2
    tiles = unit_tiles(units)

    def kernel(core_ref, *refs):
        ins, refs = refs[: len(blocks)], refs[len(blocks) :]
        gate, up, down, own, other = refs[:5]
        partials, (gate_in, up_in, down_in, turned, sems) = refs[5:-5], refs[-5:]
        copies = [
            [
                pltpu.make_async_copy(
                    source.at[pl.ds(start, size)], target.at[pl.ds(start, size)], sems.at[w, t]
                )
                for w, (source, target) in enumerate(((gate, gate_in), (up, up_in)))
            ]
            for t, (start, size) in enumerate(tiles)
        ]
        copies[0].append(pltpu.make_async_copy(down, down_in, sems.at[2, 0]))
        for group in copies:
            for copy in group:
                copy.start()

        def ready(t):
            for copy in copies[t]:
                copy.wait()

        rows, cots = [
            ins[0][k]
            if len(ins) == 1
            else jnp.concatenate([ref[k] for ref in ins], axis=0)
            for k in range(2)
        ]
        layer_kernel(rows, cots, gate_in, up_in, down_in, True, turned, partials, 512, ready)
        mine = core_ref[0]
        own[...] = turned[:, pl.ds(pl.multiple_of(mine * half, 16), half), :]
        other[...] = turned[:, pl.ds(pl.multiple_of((1 - mine) * half, 16), half), :]

    vmem = pl.BlockSpec(memory_space=pltpu.VMEM)
    hbm = pl.BlockSpec(memory_space=pl.ANY)
    return pl.pallas_call(
        kernel,
        in_specs=[pl.BlockSpec(memory_space=pltpu.SMEM)] + [vmem] * len(blocks) + [hbm] * 3,
        out_specs=[vmem] * (2 + len(blocks)),
        out_shape=[
            jax.ShapeDtypeStruct((3, half, tok), BF16),
            jax.ShapeDtypeStruct((3, half, tok), BF16),
            *[jax.ShapeDtypeStruct(b.shape[1:], BF16) for b in blocks],
        ],
        scratch_shapes=[
            pltpu.VMEM((units, width), BF16),
            pltpu.VMEM((units, width), BF16),
            pltpu.VMEM((width, units), BF16),
            pltpu.VMEM((3, units, tok), BF16),
            pltpu.SemaphoreType.DMA((3, len(tiles))),
        ],
        compiler_params=pltpu.CompilerParams(vmem_limit_bytes=VMEM_ALL),
        cost_estimate=pl.CostEstimate(
            flops=10 * units * width * tok,
            bytes_accessed=6 * units * width + 6 * tok * (width + units),
            transcendentals=units * tok,
        ),
        name="dense_block",
    )(core.reshape(1), *blocks, gate, up, down)


def expert_block(slots, gate, up, down):
    devices, _, per_device, width = slots.shape
    tok = devices * per_device
    units = gate.shape[0]
    col = 512
    tiles = unit_tiles(units)

    def kernel(
        slots, gate, up, down, g_gate, g_up, g_down, partial, loaded, turned, made, sems, out_sems
    ):
        rows, cots = [
            jnp.concatenate([slots[i, k] for i in range(devices)], axis=0) for k in range(2)
        ]
        copies = [
            [
                pltpu.make_async_copy(
                    source.at[pl.ds(start, size)], loaded.at[w, pl.ds(start, size)], sems.at[w, t]
                )
                for w, source in enumerate((gate, up, down))
            ]
            for t, (start, size) in enumerate(tiles)
        ]
        for group in copies:
            for copy in group:
                copy.start()

        def ready(t):
            for copy in copies[t]:
                copy.wait()

        layer_kernel(
            rows, cots, *[loaded.at[w] for w in range(3)], False, turned, (partial,), 512, ready
        )
        outs = (g_down, g_gate, g_up)
        pending = [None, None]
        step = 0
        for i in range(3):
            right = cots if i == 0 else rows
            for j in range(0, width, col):
                slot = step % 2
                if pending[slot] is not None:
                    pending[slot].wait()
                made[slot] = jnp.dot(
                    turned[i], right[:, j : j + col], preferred_element_type=F32
                ).astype(BF16)
                copy = pltpu.make_async_copy(
                    made.at[slot], outs[i].at[:, pl.ds(j, col)], out_sems.at[slot]
                )
                copy.start()
                pending[slot] = copy
                step += 1
        for copy in pending:
            copy.wait()

    vmem = pl.BlockSpec(memory_space=pltpu.VMEM)
    hbm = pl.BlockSpec(memory_space=pl.ANY)
    grad = jax.ShapeDtypeStruct((units, width), BF16)
    return pl.pallas_call(
        kernel,
        in_specs=[vmem, hbm, hbm, hbm],
        out_specs=[hbm, hbm, hbm, vmem],
        out_shape=[grad, grad, grad, jax.ShapeDtypeStruct((tok, width), BF16)],
        scratch_shapes=[
            pltpu.VMEM((3, units, width), BF16),
            pltpu.VMEM((3, units, tok), BF16),
            pltpu.VMEM((2, units, col), BF16),
            pltpu.SemaphoreType.DMA((3, len(tiles))),
            pltpu.SemaphoreType.DMA((2,)),
        ],
        compiler_params=pltpu.CompilerParams(vmem_limit_bytes=VMEM_ALL),
        cost_estimate=pl.CostEstimate(flops=1, bytes_accessed=1, transcendentals=0),
        name="expert_block",
    )(slots, gate, up, down)


def final_sum(core, lows, highs):
    cut, width = lows[2].shape[1:]
    units = cut + highs[2].shape[1]
    half = width // 2

    def kernel(core_ref, *refs):
        ins, (mine, other) = refs[:-2], refs[-2:]
        own_first = core_ref[0] == 0
        for i in range(3):
            for begin, (own, near, far) in ((0, ins[:3]), (cut, ins[3:])):
                total = own[i, :, width:].astype(F32) + near[i, :, width:].astype(F32)
                total = total + far[i].astype(F32)
                left, right = total[:, :half].astype(BF16), total[:, half:].astype(BF16)
                size = total.shape[0]
                mine[i, begin : begin + size] = jnp.where(own_first, left, right)
                other[i, begin : begin + size] = jnp.where(own_first, right, left)

    vmem = pl.BlockSpec(memory_space=pltpu.VMEM)
    shape = jax.ShapeDtypeStruct((3, units, half), BF16)
    return pl.pallas_call(
        kernel,
        in_specs=[pl.BlockSpec(memory_space=pltpu.SMEM)] + [vmem] * 6,
        out_specs=[vmem, vmem],
        out_shape=[shape, shape],
        compiler_params=pltpu.CompilerParams(vmem_limit_bytes=VMEM_LIMIT),
        cost_estimate=pl.CostEstimate(
            flops=9 * units * width,
            bytes_accessed=24 * units * width,
            transcendentals=0,
        ),
        name="final_sum",
    )(core.reshape(1), *lows, *highs)


def join_halves(core, mine, other):
    _, units, width = mine.shape

    def kernel(core_ref, mine, other, *outs):
        first = core_ref[0] == 0
        for i in range(3):
            a, b = mine[i], other[i]
            joined = jnp.concatenate([jnp.where(first, a, b), jnp.where(first, b, a)], axis=0)
            outs[i][...] = joined.T

    vmem = pl.BlockSpec(memory_space=pltpu.VMEM)
    grads = pl.pallas_call(
        kernel,
        in_specs=[pl.BlockSpec(memory_space=pltpu.SMEM), vmem, vmem],
        out_specs=[vmem] * 3,
        out_shape=[jax.ShapeDtypeStruct((width, 2 * units), BF16)] * 3,
        compiler_params=pltpu.CompilerParams(vmem_limit_bytes=VMEM_ALL),
        cost_estimate=pl.CostEstimate(
            flops=0, bytes_accessed=24 * units * width, transcendentals=0
        ),
        name="join_halves",
    )(core.reshape(1), mine, other)
    return [grad.T for grad in grads]


def weight_terms(tiles, acts, blocks, width, begin, end):
    units = acts[0].shape[1]
    tokens = sum(b.shape[1] for b in blocks)
    size = end - begin

    def kernel(tile_ref, *refs):
        a, b, out = refs[: len(acts)], refs[len(acts) : -1], refs[-1]
        rows = jnp.concatenate([ref[0] for ref in b], axis=0)
        cots = jnp.concatenate([ref[1] for ref in b], axis=0)
        for i in range(3):
            left = jnp.concatenate([ref[i, begin:end] for ref in a], axis=1)
            out[i] = jnp.dot(
                left, cots if i == 0 else rows, preferred_element_type=F32
            ).astype(BF16)

    def whole(shape):
        return pl.BlockSpec(shape, lambda j, tile_ref: (0, 0, 0))

    def columns(block):
        return pl.BlockSpec((*block.shape[:2], width), lambda j, tile_ref: (0, 0, tile_ref[j]))

    return pl.pallas_call(
        kernel,
        grid_spec=pltpu.PrefetchScalarGridSpec(
            num_scalar_prefetch=1,
            grid=(2,),
            in_specs=[whole(a.shape) for a in acts] + [columns(b) for b in blocks],
            out_specs=pl.BlockSpec((3, size, width), lambda j, tile_ref: (0, 0, j)),
        ),
        out_shape=jax.ShapeDtypeStruct((3, size, 2 * width), BF16),
        compiler_params=pltpu.CompilerParams(vmem_limit_bytes=VMEM_ALL),
        cost_estimate=pl.CostEstimate(
            flops=12 * size * tokens * width,
            bytes_accessed=2 * (tokens * (4 * width + 3 * units) + 6 * size * width),
            transcendentals=0,
        ),
        name="weight_terms",
    )(tiles, *acts, *blocks)


def routed_rows(hidden_in, cotangent, routes, gate_values, experts):
    tok, width = hidden_in.shape
    count = experts * 2 * CAP

    def kernel(rows, cots, routes, gates, out):
        line = lax.broadcasted_iota(jnp.int32, (count, tok), 0)
        expert, slot = line // (2 * CAP), lax.rem(line, CAP)
        first, second = routes[0:1] == expert, routes[1:2] == expert
        named = jnp.where(first | second, 1.0, 0.0)
        earlier = lax.broadcasted_iota(jnp.int32, (tok, tok), 0) < lax.broadcasted_iota(
            jnp.int32, (tok, tok), 1
        )
        before = jnp.dot(
            named.astype(BF16),
            jnp.where(earlier, 1.0, 0.0).astype(BF16),
            preferred_element_type=F32,
        )
        taken = jnp.where(before == slot.astype(F32), named, 0.0)
        weight = jnp.where(first, gates[0:1], 0.0) + jnp.where(second, gates[1:2], 0.0)
        weight = jnp.sum(taken * weight, axis=1, keepdims=True)
        taken = taken.astype(BF16)
        kept = lax.broadcasted_iota(jnp.int32, (count, 1), 0)
        is_cot = lax.rem(kept, 2 * CAP) >= CAP
        for j in range(0, width, 512):
            columns = slice(j, j + 512)
            row_part = jnp.dot(taken, rows[:, columns], preferred_element_type=F32)
            cot_part = jnp.dot(taken, cots[:, columns], preferred_element_type=F32) * weight
            out[:, columns] = jnp.where(is_cot, cot_part, row_part).astype(BF16)

    vmem = pl.BlockSpec(memory_space=pltpu.VMEM)
    return pl.pallas_call(
        kernel,
        in_specs=[vmem] * 4,
        out_specs=vmem,
        out_shape=jax.ShapeDtypeStruct((count, width), BF16),
        compiler_params=pltpu.CompilerParams(vmem_limit_bytes=VMEM_LIMIT),
        cost_estimate=pl.CostEstimate(
            flops=4 * count * tok * width, bytes_accessed=4 * tok * width, transcendentals=0
        ),
        name="routed_rows",
    )(hidden_in, cotangent, routes.T, gate_values.T)


def together(*values):
    return lax.optimization_barrier(values)


def line_body(
    hidden_in,
    cotangent,
    routes,
    gate_values,
    dense_gate,
    dense_up,
    dense_down,
    expert_gate,
    expert_up,
    expert_down,
):
    experts = lax.axis_size("tp")
    me = lax.axis_index("tp")
    ep = lax.axis_index("ep")
    core, chip = lax.rem(ep, 2), lax.div(ep, 2)
    half = dense_gate.shape[0] // 2
    columns = dense_down.shape[1]
    down = lax.all_gather(dense_down.T, "ep", axis=0, tiled=True)

    def pairs(value):
        return lax.ppermute(value, "tp", [(0, 1), (1, 0), (2, 3), (3, 2)])

    def mirror(value):
        return lax.ppermute(value, "tp", [(0, 3), (1, 2), (2, 1), (3, 0)])

    def across(value, apart):
        return lax.ppermute(value, "ep", [(i, i ^ apart) for i in range(8)])

    def add(a, b):
        return (a.astype(F32) + b.astype(F32)).astype(BF16)

    def dense(blocks):
        mine, other, *partials = dense_block(core, blocks, dense_gate, dense_up, down)
        tokens = [*blocks, *(across(b, 1) for b in blocks)]
        return ([mine, across(other, 1)], tokens), partials

    own = jnp.stack([hidden_in, cotangent])
    mirrored, paired = mirror(own), pairs(own)
    sent = routed_rows(hidden_in, cotangent, routes, gate_values, experts)
    got = lax.all_to_all(sent, "tp", split_axis=0, concat_axis=0, tiled=True)
    got = got.reshape(experts, 2, CAP, -1).transpose(1, 0, 2, 3).reshape(2, experts * CAP, -1)
    dispatch, _ = slot_tables(routes, gate_values, me, experts)
    x_chip, y_chip, xy_chip = [jnp.bitwise_xor(chip, k) for k in (1, 2, 3)]
    chip_tiles = [
        jnp.stack(t)
        for t in ((xy_chip, x_chip), (xy_chip, y_chip), (y_chip, chip), (x_chip, chip))
    ]
    both0, (partial0,) = dense([own])
    got, partial0, both0, dispatch, chip_tiles = together(
        got, partial0, both0, dispatch, chip_tiles
    )

    mirrored, paired, got = together(mirrored, paired, got)
    last = pairs(mirrored)
    slots = lax.all_gather(got, "ep", axis=0, tiled=False)
    both12, (paired_partial, mirrored_partial) = dense([paired, mirrored])
    slots, both12, paired_partial, mirrored_partial = together(
        slots, both12, paired_partial, mirrored_partial
    )
    g_gate, g_up, g_down, slot_terms = expert_block(
        slots, expert_gate[0], expert_up[0], expert_down[0]
    )

    last, both12, slot_terms = together(last, both12, slot_terms)
    routed = lax.psum_scatter(slot_terms, "ep", scatter_dimension=0, tiled=True)
    both3, (partial3,) = dense([last])
    from_last = pairs(partial3)

    acts, tokens = (a + b + c for a, b, c in zip(both0, both12, both3))
    cut, width = -(-half // 32) * 16, 2 * columns
    low_sent = weight_terms(chip_tiles[0], acts, tokens, width, 0, cut)
    high_sent = weight_terms(chip_tiles[1], acts, tokens, width, cut, half)
    high_sent, chip_tiles, from_last = together(high_sent, chip_tiles, from_last)
    low_kept = weight_terms(chip_tiles[2], acts, tokens, width, 0, cut)
    high_kept = weight_terms(chip_tiles[3], acts, tokens, width, cut, half)
    low_near, high_near = across(low_sent, 2), across(high_sent, 4)
    from_pair = pairs(paired_partial)
    low_kept, high_kept, from_pair, routed = together(low_kept, high_kept, from_pair, routed)
    back = slots_back(routed, experts)
    from_last, back = together(from_last, back)
    from_mirror = mirror(add(mirrored_partial, from_last))
    low_near, high_near, low_kept, high_kept, back = together(
        low_near, high_near, low_kept, high_kept, back
    )
    low_far = across(add(low_kept[:, :, :width], low_near[:, :, :width]), 4)
    high_far = across(add(high_kept[:, :, :width], high_near[:, :, :width]), 2)
    low_far, high_far, from_mirror = together(low_far, high_far, from_mirror)
    routed_input = to_tokens(back, dispatch, me, experts)
    mine, other = final_sum(
        core, (low_kept, low_near, low_far), (high_kept, high_near, high_far)
    )
    grads = join_halves(core, mine, across(other, 1))
    grad_input = (
        partial0.astype(F32)
        + from_pair.astype(F32)
        + from_mirror.astype(F32)
        + routed_input
    ).astype(BF16)
    return (grad_input, grads[1], grads[2], grads[0], g_gate[None], g_up[None], g_down[None])


def general_body(
    hidden_in,
    cotangent,
    routes,
    gate_values,
    dense_gate,
    dense_up,
    dense_down,
    expert_gate,
    expert_up,
    expert_down,
):
    experts = lax.axis_size("tp")
    me = lax.axis_index("tp")
    dispatch, weight = slot_tables(routes, gate_values, me, experts)
    sent = slots_to_send(hidden_in, cotangent, dispatch, weight, experts)
    got = exchange_slots(sent, me, experts)
    slots = lax.all_gather(got, "ep", axis=0, tiled=False)
    slot_rows, slot_cot = slots[:, 0].reshape(-1, hidden_in.shape[1]), slots[:, 1].reshape(
        -1, hidden_in.shape[1]
    )
    rows = lax.all_gather(hidden_in, "tp", axis=0, tiled=True)
    cots = lax.all_gather(cotangent, "tp", axis=0, tiled=True)
    down = lax.all_gather(dense_down, "ep", axis=1, tiled=True)
    act, grad_gate, grad_up, partial = plain_block(rows, cots, dense_gate, dense_up, down)
    dense_input = lax.psum_scatter(partial, "tp", scatter_dimension=0, tiled=True)
    grads = [
        lax.psum_scatter(
            lax.dot_general(a, b, LEADING, preferred_element_type=F32).astype(BF16),
            "ep",
            scatter_dimension=1,
            tiled=True,
        )
        for a, b in ((act, cots), (grad_gate, rows), (grad_up, rows))
    ]
    g_gate, g_up, g_down, slot_terms = expert_layer(
        slot_rows, slot_cot, expert_gate[0], expert_up[0], expert_down[0]
    )
    routed = lax.psum_scatter(slot_terms, "ep", scatter_dimension=0, tiled=True)
    routed_input = to_tokens(slots_back(routed, experts), dispatch, me, experts)
    grad_input = (dense_input.astype(F32) + routed_input).astype(BF16)
    return (grad_input, grads[1], grads[2], grads[0], g_gate[None], g_up[None], g_down[None])


def solution(mesh):
    placed = (
        P(("ep", "tp"), None),
        P(("ep", "tp"), None),
        P(("ep", "tp"), None),
        P(("ep", "tp"), None),
        P("tp", None),
        P("tp", None),
        P("tp", "ep"),
        P("tp", "ep", None),
        P("tp", "ep", None),
        P("tp", "ep", None),
    )
    in_line = mesh.shape["tp"] == 4 and mesh.shape["ep"] == 8
    return jax.shard_map(
        line_body if in_line else general_body,
        mesh=mesh,
        in_specs=placed,
        out_specs=(
            P(("ep", "tp"), None),
            P("tp", "ep"),
            P("tp", "ep"),
            P("tp", "ep"),
            P("tp", "ep", None),
            P("tp", "ep", None),
            P("tp", "ep", None),
        ),
        check_vma=False,
    )
```

```python
import jax
import jax.numpy as jnp
from jax import lax
from jax.experimental import pallas as pl
from jax.experimental.pallas import tpu as pltpu
from jax.sharding import PartitionSpec as P

CAP = 4
CONTRACT = (((1,), (1,)), ((), ()))
LEADING = (((0,), (0,)), ((), ()))
F32 = jnp.float32
BF16 = jnp.bfloat16


def swiglu_backward(gate_pre, up_pre, grad_act):
    sigmoid_gate = jax.nn.sigmoid(gate_pre)
    silu_gate = gate_pre * sigmoid_gate
    act = (silu_gate * up_pre).astype(BF16)
    silu_slope = sigmoid_gate * (1.0 + gate_pre * (1.0 - sigmoid_gate))
    grad_gate = (grad_act * up_pre * silu_slope).astype(BF16)
    grad_up = (grad_act * silu_gate).astype(BF16)
    return act, grad_gate, grad_up


def slot_tables(routes, gate_values, me, experts):
    tok_count = routes.shape[0]
    named = lax.rem(me + jnp.arange(experts, dtype=jnp.int32), experts)
    onehot = (routes.reshape(-1)[:, None] == named[None, :]).astype(jnp.int32)
    before = jnp.cumsum(onehot, axis=0) - onehot
    slot = onehot[:, :, None] * (before[:, :, None] == jnp.arange(CAP, dtype=jnp.int32)).astype(
        jnp.int32
    )
    slot = slot.reshape(tok_count, 2, experts * CAP).astype(F32)
    dispatch = jnp.sum(slot, axis=1).T.astype(BF16)
    weight = jnp.sum(slot * gate_values[:, :, None], axis=(0, 1))
    return dispatch, weight


def shift(x, axis, size, by):
    return lax.ppermute(x, axis, [(i, (i + by) % size) for i in range(size)])


def slots_to_send(hidden_in, cotangent, dispatch, weight, experts):
    width = hidden_in.shape[1]
    rows = jnp.dot(dispatch, hidden_in, preferred_element_type=F32).astype(BF16)
    cots = jnp.dot(dispatch, cotangent, preferred_element_type=F32)
    cots = (cots * weight[:, None]).astype(BF16)
    return jnp.stack(
        [rows.reshape(experts, CAP, width), cots.reshape(experts, CAP, width)], axis=1
    )


def exchange_slots(sent, me, experts):
    width = sent.shape[3]
    sent = jnp.roll(sent, me, axis=0)
    got = lax.all_to_all(sent, "tp", split_axis=0, concat_axis=0, tiled=True)
    return got.transpose(1, 0, 2, 3).reshape(2, experts * CAP, width)


def expert_layer(slot_rows, slot_cot, gate_weight, up_weight, down_weight):
    e_gate = lax.dot_general(slot_rows, gate_weight, CONTRACT, preferred_element_type=F32)
    e_up = lax.dot_general(slot_rows, up_weight, CONTRACT, preferred_element_type=F32)
    e_grad_act = lax.dot_general(slot_cot, down_weight, CONTRACT, preferred_element_type=F32)
    e_act, e_grad_gate, e_grad_up = swiglu_backward(e_gate, e_up, e_grad_act)
    g_down = lax.dot_general(e_act, slot_cot, LEADING, preferred_element_type=F32).astype(BF16)
    g_gate = lax.dot_general(e_grad_gate, slot_rows, LEADING, preferred_element_type=F32).astype(
        BF16
    )
    g_up = lax.dot_general(e_grad_up, slot_rows, LEADING, preferred_element_type=F32).astype(BF16)
    terms = jnp.dot(e_grad_gate, gate_weight, preferred_element_type=F32) + jnp.dot(
        e_grad_up, up_weight, preferred_element_type=F32
    )
    return g_gate, g_up, g_down, terms.astype(BF16)


def slots_back(own, experts):
    own = own.reshape(experts, CAP, own.shape[1])
    return lax.all_to_all(own, "tp", split_axis=0, concat_axis=0, tiled=True)


def to_tokens(back, dispatch, me, experts):
    dispatch = jnp.roll(dispatch.reshape(experts, CAP, -1), me, axis=0)
    return lax.dot_general(
        dispatch.reshape(experts * CAP, -1),
        back.reshape(experts * CAP, -1),
        LEADING,
        preferred_element_type=F32,
    )


def plain_block(rows, cot, gate, up, down):
    gate_pre = lax.dot_general(rows, gate, CONTRACT, preferred_element_type=F32)
    up_pre = lax.dot_general(rows, up, CONTRACT, preferred_element_type=F32)
    grad_act = lax.dot_general(cot, down, CONTRACT, preferred_element_type=F32)
    act, grad_gate, grad_up = swiglu_backward(gate_pre, up_pre, grad_act)
    partial = jnp.dot(grad_gate, gate, preferred_element_type=F32) + jnp.dot(
        grad_up, up, preferred_element_type=F32
    )
    return act, grad_gate, grad_up, partial.astype(BF16)


VMEM_LIMIT = 20 * 1024 * 1024
VMEM_ALL = 60 * 1024 * 1024


def unit_tiles(units):
    return [(start, min(256, units - start)) for start in range(0, units, 256)]


def layer_kernel(rows, cots, gate, up, down, down_turned, turned, partials, col, ready=None):
    units, width = gate.shape
    for t, (start, size) in enumerate(unit_tiles(units)):
        if ready is not None:
            ready(t)
        gate_pre, up_pre = [
            lax.dot_general(w[start : start + size], rows, CONTRACT, preferred_element_type=F32)
            for w in (gate, up)
        ]
        if down_turned:
            grad_act = jnp.dot(
                cots, down[:, start : start + size], preferred_element_type=F32
            ).T
        else:
            grad_act = lax.dot_general(
                down[start : start + size], cots, CONTRACT, preferred_element_type=F32
            )
        for i, value in enumerate(swiglu_backward(gate_pre, up_pre, grad_act)):
            turned[i, start : start + size] = value
    grads = [turned[1].T, turned[2].T]
    for j in range(0, width, col):
        made = (
            jnp.dot(grads[0], gate[:, j : j + col], preferred_element_type=F32)
            + jnp.dot(grads[1], up[:, j : j + col], preferred_element_type=F32)
        ).astype(BF16)
        begin = 0
        for partial in partials:
            end = begin + partial.shape[0]
            partial[:, j : j + col] = made[begin:end]
            begin = end


def dense_block(core, blocks, gate, up, down):
    tok, width = blocks[0].shape[1] * len(blocks), blocks[0].shape[2]
    units = gate.shape[0]
    half = units // 2
    tiles = unit_tiles(units)

    def kernel(core_ref, *refs):
        ins, refs = refs[: len(blocks)], refs[len(blocks) :]
        gate, up, down, own, other = refs[:5]
        partials, (gate_in, up_in, down_in, turned, sems) = refs[5:-5], refs[-5:]
        copies = [
            [
                pltpu.make_async_copy(
                    source.at[pl.ds(start, size)], target.at[pl.ds(start, size)], sems.at[w, t]
                )
                for w, (source, target) in enumerate(((gate, gate_in), (up, up_in)))
            ]
            for t, (start, size) in enumerate(tiles)
        ]
        copies[0].append(pltpu.make_async_copy(down, down_in, sems.at[2, 0]))
        for group in copies:
            for copy in group:
                copy.start()

        def ready(t):
            for copy in copies[t]:
                copy.wait()

        rows, cots = [
            ins[0][k]
            if len(ins) == 1
            else jnp.concatenate([ref[k] for ref in ins], axis=0)
            for k in range(2)
        ]
        layer_kernel(rows, cots, gate_in, up_in, down_in, True, turned, partials, 512, ready)
        mine = core_ref[0]
        own[...] = turned[:, pl.ds(pl.multiple_of(mine * half, 16), half), :]
        other[...] = turned[:, pl.ds(pl.multiple_of((1 - mine) * half, 16), half), :]

    vmem = pl.BlockSpec(memory_space=pltpu.VMEM)
    hbm = pl.BlockSpec(memory_space=pl.ANY)
    return pl.pallas_call(
        kernel,
        in_specs=[pl.BlockSpec(memory_space=pltpu.SMEM)] + [vmem] * len(blocks) + [hbm] * 3,
        out_specs=[vmem] * (2 + len(blocks)),
        out_shape=[
            jax.ShapeDtypeStruct((3, half, tok), BF16),
            jax.ShapeDtypeStruct((3, half, tok), BF16),
            *[jax.ShapeDtypeStruct(b.shape[1:], BF16) for b in blocks],
        ],
        scratch_shapes=[
            pltpu.VMEM((units, width), BF16),
            pltpu.VMEM((units, width), BF16),
            pltpu.VMEM((width, units), BF16),
            pltpu.VMEM((3, units, tok), BF16),
            pltpu.SemaphoreType.DMA((3, len(tiles))),
        ],
        compiler_params=pltpu.CompilerParams(vmem_limit_bytes=VMEM_ALL),
        cost_estimate=pl.CostEstimate(
            flops=10 * units * width * tok,
            bytes_accessed=6 * units * width + 6 * tok * (width + units),
            transcendentals=units * tok,
        ),
        name="dense_block",
    )(core.reshape(1), *blocks, gate, up, down)


def expert_block(slots, gate, up, down):
    devices, _, per_device, width = slots.shape
    tok = devices * per_device
    units = gate.shape[0]
    col = 512
    tiles = unit_tiles(units)

    def kernel(
        slots, gate, up, down, g_gate, g_up, g_down, partial, loaded, turned, made, sems, out_sems
    ):
        rows, cots = [
            jnp.concatenate([slots[i, k] for i in range(devices)], axis=0) for k in range(2)
        ]
        copies = [
            [
                pltpu.make_async_copy(
                    source.at[pl.ds(start, size)], loaded.at[w, pl.ds(start, size)], sems.at[w, t]
                )
                for w, source in enumerate((gate, up, down))
            ]
            for t, (start, size) in enumerate(tiles)
        ]
        for group in copies:
            for copy in group:
                copy.start()

        def ready(t):
            for copy in copies[t]:
                copy.wait()

        layer_kernel(
            rows, cots, *[loaded.at[w] for w in range(3)], False, turned, (partial,), 512, ready
        )
        outs = (g_down, g_gate, g_up)
        pending = [None, None]
        step = 0
        for i in range(3):
            right = cots if i == 0 else rows
            for j in range(0, width, col):
                slot = step % 2
                if pending[slot] is not None:
                    pending[slot].wait()
                made[slot] = jnp.dot(
                    turned[i], right[:, j : j + col], preferred_element_type=F32
                ).astype(BF16)
                copy = pltpu.make_async_copy(
                    made.at[slot], outs[i].at[:, pl.ds(j, col)], out_sems.at[slot]
                )
                copy.start()
                pending[slot] = copy
                step += 1
        for copy in pending:
            copy.wait()

    vmem = pl.BlockSpec(memory_space=pltpu.VMEM)
    hbm = pl.BlockSpec(memory_space=pl.ANY)
    grad = jax.ShapeDtypeStruct((units, width), BF16)
    return pl.pallas_call(
        kernel,
        in_specs=[vmem, hbm, hbm, hbm],
        out_specs=[hbm, hbm, hbm, vmem],
        out_shape=[grad, grad, grad, jax.ShapeDtypeStruct((tok, width), BF16)],
        scratch_shapes=[
            pltpu.VMEM((3, units, width), BF16),
            pltpu.VMEM((3, units, tok), BF16),
            pltpu.VMEM((2, units, col), BF16),
            pltpu.SemaphoreType.DMA((3, len(tiles))),
            pltpu.SemaphoreType.DMA((2,)),
        ],
        compiler_params=pltpu.CompilerParams(vmem_limit_bytes=VMEM_ALL),
        cost_estimate=pl.CostEstimate(flops=1, bytes_accessed=1, transcendentals=0),
        name="expert_block",
    )(slots, gate, up, down)


def final_sum(core, lows, highs):
    cut, width = lows[2].shape[1:]
    units = cut + highs[2].shape[1]
    half = width // 2

    def kernel(core_ref, *refs):
        ins, (mine, other) = refs[:-2], refs[-2:]
        own_first = core_ref[0] == 0
        for i in range(3):
            for begin, (own, near, far) in ((0, ins[:3]), (cut, ins[3:])):
                total = own[i, :, width:].astype(F32) + near[i, :, width:].astype(F32)
                total = total + far[i].astype(F32)
                left, right = total[:, :half].astype(BF16), total[:, half:].astype(BF16)
                size = total.shape[0]
                mine[i, begin : begin + size] = jnp.where(own_first, left, right)
                other[i, begin : begin + size] = jnp.where(own_first, right, left)

    vmem = pl.BlockSpec(memory_space=pltpu.VMEM)
    shape = jax.ShapeDtypeStruct((3, units, half), BF16)
    return pl.pallas_call(
        kernel,
        in_specs=[pl.BlockSpec(memory_space=pltpu.SMEM)] + [vmem] * 6,
        out_specs=[vmem, vmem],
        out_shape=[shape, shape],
        compiler_params=pltpu.CompilerParams(vmem_limit_bytes=VMEM_LIMIT),
        cost_estimate=pl.CostEstimate(
            flops=9 * units * width,
            bytes_accessed=24 * units * width,
            transcendentals=0,
        ),
        name="final_sum",
    )(core.reshape(1), *lows, *highs)


def join_halves(core, mine, other):
    _, units, width = mine.shape

    def kernel(core_ref, mine, other, *outs):
        first = core_ref[0] == 0
        for i in range(3):
            a, b = mine[i], other[i]
            joined = jnp.concatenate([jnp.where(first, a, b), jnp.where(first, b, a)], axis=0)
            outs[i][...] = joined.T

    vmem = pl.BlockSpec(memory_space=pltpu.VMEM)
    grads = pl.pallas_call(
        kernel,
        in_specs=[pl.BlockSpec(memory_space=pltpu.SMEM), vmem, vmem],
        out_specs=[vmem] * 3,
        out_shape=[jax.ShapeDtypeStruct((width, 2 * units), BF16)] * 3,
        compiler_params=pltpu.CompilerParams(vmem_limit_bytes=VMEM_ALL),
        cost_estimate=pl.CostEstimate(
            flops=0, bytes_accessed=24 * units * width, transcendentals=0
        ),
        name="join_halves",
    )(core.reshape(1), mine, other)
    return [grad.T for grad in grads]


def weight_terms(tiles, acts, blocks, width, begin, end):
    units = acts[0].shape[1]
    tokens = sum(b.shape[1] for b in blocks)
    size = end - begin

    def kernel(tile_ref, *refs):
        a, b, out = refs[: len(acts)], refs[len(acts) : -1], refs[-1]
        rows = jnp.concatenate([ref[0] for ref in b], axis=0)
        cots = jnp.concatenate([ref[1] for ref in b], axis=0)
        for i in range(3):
            left = jnp.concatenate([ref[i, begin:end] for ref in a], axis=1)
            out[i] = jnp.dot(
                left, cots if i == 0 else rows, preferred_element_type=F32
            ).astype(BF16)

    def whole(shape):
        return pl.BlockSpec(shape, lambda j, tile_ref: (0, 0, 0))

    def columns(block):
        return pl.BlockSpec((*block.shape[:2], width), lambda j, tile_ref: (0, 0, tile_ref[j]))

    return pl.pallas_call(
        kernel,
        grid_spec=pltpu.PrefetchScalarGridSpec(
            num_scalar_prefetch=1,
            grid=(2,),
            in_specs=[whole(a.shape) for a in acts] + [columns(b) for b in blocks],
            out_specs=pl.BlockSpec((3, size, width), lambda j, tile_ref: (0, 0, j)),
        ),
        out_shape=jax.ShapeDtypeStruct((3, size, 2 * width), BF16),
        compiler_params=pltpu.CompilerParams(vmem_limit_bytes=VMEM_ALL),
        cost_estimate=pl.CostEstimate(
            flops=12 * size * tokens * width,
            bytes_accessed=2 * (tokens * (4 * width + 3 * units) + 6 * size * width),
            transcendentals=0,
        ),
        name="weight_terms",
    )(tiles, *acts, *blocks)


def routed_rows(hidden_in, cotangent, routes, gate_values, experts):
    tok, width = hidden_in.shape
    count = experts * 2 * CAP

    def kernel(rows, cots, routes, gates, out):
        line = lax.broadcasted_iota(jnp.int32, (count, tok), 0)
        expert, slot = line // (2 * CAP), lax.rem(line, CAP)
        first, second = routes[0:1] == expert, routes[1:2] == expert
        named = jnp.where(first | second, 1.0, 0.0)
        earlier = lax.broadcasted_iota(jnp.int32, (tok, tok), 0) < lax.broadcasted_iota(
            jnp.int32, (tok, tok), 1
        )
        before = jnp.dot(
            named.astype(BF16),
            jnp.where(earlier, 1.0, 0.0).astype(BF16),
            preferred_element_type=F32,
        )
        taken = jnp.where(before == slot.astype(F32), named, 0.0)
        weight = jnp.where(first, gates[0:1], 0.0) + jnp.where(second, gates[1:2], 0.0)
        weight = jnp.sum(taken * weight, axis=1, keepdims=True)
        taken = taken.astype(BF16)
        kept = lax.broadcasted_iota(jnp.int32, (count, 1), 0)
        is_cot = lax.rem(kept, 2 * CAP) >= CAP
        for j in range(0, width, 512):
            columns = slice(j, j + 512)
            row_part = jnp.dot(taken, rows[:, columns], preferred_element_type=F32)
            cot_part = jnp.dot(taken, cots[:, columns], preferred_element_type=F32) * weight
            out[:, columns] = jnp.where(is_cot, cot_part, row_part).astype(BF16)

    vmem = pl.BlockSpec(memory_space=pltpu.VMEM)
    return pl.pallas_call(
        kernel,
        in_specs=[vmem] * 4,
        out_specs=vmem,
        out_shape=jax.ShapeDtypeStruct((count, width), BF16),
        compiler_params=pltpu.CompilerParams(vmem_limit_bytes=VMEM_LIMIT),
        cost_estimate=pl.CostEstimate(
            flops=4 * count * tok * width, bytes_accessed=4 * tok * width, transcendentals=0
        ),
        name="routed_rows",
    )(hidden_in, cotangent, routes.T, gate_values.T)


def together(*values):
    return lax.optimization_barrier(values)


def line_body(
    hidden_in,
    cotangent,
    routes,
    gate_values,
    dense_gate,
    dense_up,
    dense_down,
    expert_gate,
    expert_up,
    expert_down,
):
    experts = lax.axis_size("tp")
    me = lax.axis_index("tp")
    ep = lax.axis_index("ep")
    core, chip = lax.rem(ep, 2), lax.div(ep, 2)
    half = dense_gate.shape[0] // 2
    columns = dense_down.shape[1]
    down = lax.all_gather(dense_down.T, "ep", axis=0, tiled=True)

    def pairs(value):
        return lax.ppermute(value, "tp", [(0, 1), (1, 0), (2, 3), (3, 2)])

    def mirror(value):
        return lax.ppermute(value, "tp", [(0, 3), (1, 2), (2, 1), (3, 0)])

    def across(value, apart):
        return lax.ppermute(value, "ep", [(i, i ^ apart) for i in range(8)])

    def add(a, b):
        return (a.astype(F32) + b.astype(F32)).astype(BF16)

    def dense(blocks):
        mine, other, *partials = dense_block(core, blocks, dense_gate, dense_up, down)
        tokens = [*blocks, *(across(b, 1) for b in blocks)]
        return ([mine, across(other, 1)], tokens), partials

    own = jnp.stack([hidden_in, cotangent])
    mirrored, paired = mirror(own), pairs(own)
    sent = routed_rows(hidden_in, cotangent, routes, gate_values, experts)
    got = lax.all_to_all(sent, "tp", split_axis=0, concat_axis=0, tiled=True)
    got = got.reshape(experts, 2, CAP, -1).transpose(1, 0, 2, 3).reshape(2, experts * CAP, -1)
    dispatch, _ = slot_tables(routes, gate_values, me, experts)
    x_chip, y_chip, xy_chip = [jnp.bitwise_xor(chip, k) for k in (1, 2, 3)]
    chip_tiles = [
        jnp.stack(t)
        for t in ((xy_chip, x_chip), (xy_chip, y_chip), (y_chip, chip), (x_chip, chip))
    ]
    both0, (partial0,) = dense([own])
    got, partial0, both0, dispatch, chip_tiles = together(
        got, partial0, both0, dispatch, chip_tiles
    )

    mirrored, paired, got = together(mirrored, paired, got)
    last = pairs(mirrored)
    slots = lax.all_gather(got, "ep", axis=0, tiled=False)
    both12, (paired_partial, mirrored_partial) = dense([paired, mirrored])
    slots, both12, paired_partial, mirrored_partial = together(
        slots, both12, paired_partial, mirrored_partial
    )
    g_gate, g_up, g_down, slot_terms = expert_block(
        slots, expert_gate[0], expert_up[0], expert_down[0]
    )

    last, both12, slot_terms = together(last, both12, slot_terms)
    routed = lax.psum_scatter(slot_terms, "ep", scatter_dimension=0, tiled=True)
    both3, (partial3,) = dense([last])
    from_last = pairs(partial3)

    acts, tokens = (a + b + c for a, b, c in zip(both0, both12, both3))
    cut, width = -(-half // 32) * 16, 2 * columns
    low_sent = weight_terms(chip_tiles[0], acts, tokens, width, 0, cut)
    high_sent = weight_terms(chip_tiles[1], acts, tokens, width, cut, half)
    high_sent, chip_tiles, from_last = together(high_sent, chip_tiles, from_last)
    low_kept = weight_terms(chip_tiles[2], acts, tokens, width, 0, cut)
    high_kept = weight_terms(chip_tiles[3], acts, tokens, width, cut, half)
    low_near, high_near = across(low_sent, 2), across(high_sent, 4)
    from_mirror = mirror(add(mirrored_partial, from_last))
    low_kept, high_kept, routed = together(low_kept, high_kept, routed)
    low_near, high_near, low_kept, high_kept, paired_partial, routed = together(
        low_near, high_near, low_kept, high_kept, paired_partial, routed
    )
    from_pair = pairs(paired_partial)
    low_far = across(add(low_kept[:, :, :width], low_near[:, :, :width]), 4)
    high_far = across(add(high_kept[:, :, :width], high_near[:, :, :width]), 2)
    from_mirror, routed = together(from_mirror, routed)
    routed_input = to_tokens(slots_back(routed, experts), dispatch, me, experts)
    mine, other = final_sum(
        core, (low_kept, low_near, low_far), (high_kept, high_near, high_far)
    )
    grads = join_halves(core, mine, across(other, 1))
    grad_input = (
        partial0.astype(F32)
        + from_pair.astype(F32)
        + from_mirror.astype(F32)
        + routed_input
    ).astype(BF16)
    return (grad_input, grads[1], grads[2], grads[0], g_gate[None], g_up[None], g_down[None])


def general_body(
    hidden_in,
    cotangent,
    routes,
    gate_values,
    dense_gate,
    dense_up,
    dense_down,
    expert_gate,
    expert_up,
    expert_down,
):
    experts = lax.axis_size("tp")
    me = lax.axis_index("tp")
    dispatch, weight = slot_tables(routes, gate_values, me, experts)
    sent = slots_to_send(hidden_in, cotangent, dispatch, weight, experts)
    got = exchange_slots(sent, me, experts)
    slots = lax.all_gather(got, "ep", axis=0, tiled=False)
    slot_rows, slot_cot = slots[:, 0].reshape(-1, hidden_in.shape[1]), slots[:, 1].reshape(
        -1, hidden_in.shape[1]
    )
    rows = lax.all_gather(hidden_in, "tp", axis=0, tiled=True)
    cots = lax.all_gather(cotangent, "tp", axis=0, tiled=True)
    down = lax.all_gather(dense_down, "ep", axis=1, tiled=True)
    act, grad_gate, grad_up, partial = plain_block(rows, cots, dense_gate, dense_up, down)
    dense_input = lax.psum_scatter(partial, "tp", scatter_dimension=0, tiled=True)
    grads = [
        lax.psum_scatter(
            lax.dot_general(a, b, LEADING, preferred_element_type=F32).astype(BF16),
            "ep",
            scatter_dimension=1,
            tiled=True,
        )
        for a, b in ((act, cots), (grad_gate, rows), (grad_up, rows))
    ]
    g_gate, g_up, g_down, slot_terms = expert_layer(
        slot_rows, slot_cot, expert_gate[0], expert_up[0], expert_down[0]
    )
    routed = lax.psum_scatter(slot_terms, "ep", scatter_dimension=0, tiled=True)
    routed_input = to_tokens(slots_back(routed, experts), dispatch, me, experts)
    grad_input = (dense_input.astype(F32) + routed_input).astype(BF16)
    return (grad_input, grads[1], grads[2], grads[0], g_gate[None], g_up[None], g_down[None])


def solution(mesh):
    placed = (
        P(("ep", "tp"), None),
        P(("ep", "tp"), None),
        P(("ep", "tp"), None),
        P(("ep", "tp"), None),
        P("tp", None),
        P("tp", None),
        P("tp", "ep"),
        P("tp", "ep", None),
        P("tp", "ep", None),
        P("tp", "ep", None),
    )
    in_line = mesh.shape["tp"] == 4 and mesh.shape["ep"] == 8
    return jax.shard_map(
        line_body if in_line else general_body,
        mesh=mesh,
        in_specs=placed,
        out_specs=(
            P(("ep", "tp"), None),
            P("tp", "ep"),
            P("tp", "ep"),
            P("tp", "ep"),
            P("tp", "ep", None),
            P("tp", "ep", None),
            P("tp", "ep", None),
        ),
        check_vma=False,
    )
```

```python
import jax
import jax.numpy as jnp
from jax import lax
from jax.experimental import pallas as pl
from jax.experimental.pallas import tpu as pltpu
from jax.sharding import PartitionSpec as P

CAP = 4
CONTRACT = (((1,), (1,)), ((), ()))
LEADING = (((0,), (0,)), ((), ()))
F32 = jnp.float32
BF16 = jnp.bfloat16


def swiglu_backward(gate_pre, up_pre, grad_act):
    sigmoid_gate = jax.nn.sigmoid(gate_pre)
    silu_gate = gate_pre * sigmoid_gate
    act = (silu_gate * up_pre).astype(BF16)
    silu_slope = sigmoid_gate * (1.0 + gate_pre * (1.0 - sigmoid_gate))
    grad_gate = (grad_act * up_pre * silu_slope).astype(BF16)
    grad_up = (grad_act * silu_gate).astype(BF16)
    return act, grad_gate, grad_up


def slot_tables(routes, gate_values, me, experts):
    tok_count = routes.shape[0]
    named = lax.rem(me + jnp.arange(experts, dtype=jnp.int32), experts)
    onehot = (routes.reshape(-1)[:, None] == named[None, :]).astype(jnp.int32)
    before = jnp.cumsum(onehot, axis=0) - onehot
    slot = onehot[:, :, None] * (before[:, :, None] == jnp.arange(CAP, dtype=jnp.int32)).astype(
        jnp.int32
    )
    slot = slot.reshape(tok_count, 2, experts * CAP).astype(F32)
    dispatch = jnp.sum(slot, axis=1).T.astype(BF16)
    weight = jnp.sum(slot * gate_values[:, :, None], axis=(0, 1))
    return dispatch, weight


def shift(x, axis, size, by):
    return lax.ppermute(x, axis, [(i, (i + by) % size) for i in range(size)])


def slots_to_send(hidden_in, cotangent, dispatch, weight, experts):
    width = hidden_in.shape[1]
    rows = jnp.dot(dispatch, hidden_in, preferred_element_type=F32).astype(BF16)
    cots = jnp.dot(dispatch, cotangent, preferred_element_type=F32)
    cots = (cots * weight[:, None]).astype(BF16)
    return jnp.stack(
        [rows.reshape(experts, CAP, width), cots.reshape(experts, CAP, width)], axis=1
    )


def exchange_slots(sent, me, experts):
    width = sent.shape[3]
    sent = jnp.roll(sent, me, axis=0)
    got = lax.all_to_all(sent, "tp", split_axis=0, concat_axis=0, tiled=True)
    return got.transpose(1, 0, 2, 3).reshape(2, experts * CAP, width)


def expert_layer(slot_rows, slot_cot, gate_weight, up_weight, down_weight):
    e_gate = lax.dot_general(slot_rows, gate_weight, CONTRACT, preferred_element_type=F32)
    e_up = lax.dot_general(slot_rows, up_weight, CONTRACT, preferred_element_type=F32)
    e_grad_act = lax.dot_general(slot_cot, down_weight, CONTRACT, preferred_element_type=F32)
    e_act, e_grad_gate, e_grad_up = swiglu_backward(e_gate, e_up, e_grad_act)
    g_down = lax.dot_general(e_act, slot_cot, LEADING, preferred_element_type=F32).astype(BF16)
    g_gate = lax.dot_general(e_grad_gate, slot_rows, LEADING, preferred_element_type=F32).astype(
        BF16
    )
    g_up = lax.dot_general(e_grad_up, slot_rows, LEADING, preferred_element_type=F32).astype(BF16)
    terms = jnp.dot(e_grad_gate, gate_weight, preferred_element_type=F32) + jnp.dot(
        e_grad_up, up_weight, preferred_element_type=F32
    )
    return g_gate, g_up, g_down, terms.astype(BF16)


def slots_back(own, experts):
    own = own.reshape(experts, CAP, own.shape[1])
    return lax.all_to_all(own, "tp", split_axis=0, concat_axis=0, tiled=True)


def to_tokens(back, dispatch, me, experts):
    dispatch = jnp.roll(dispatch.reshape(experts, CAP, -1), me, axis=0)
    return lax.dot_general(
        dispatch.reshape(experts * CAP, -1),
        back.reshape(experts * CAP, -1),
        LEADING,
        preferred_element_type=F32,
    )


def plain_block(rows, cot, gate, up, down):
    gate_pre = lax.dot_general(rows, gate, CONTRACT, preferred_element_type=F32)
    up_pre = lax.dot_general(rows, up, CONTRACT, preferred_element_type=F32)
    grad_act = lax.dot_general(cot, down, CONTRACT, preferred_element_type=F32)
    act, grad_gate, grad_up = swiglu_backward(gate_pre, up_pre, grad_act)
    partial = jnp.dot(grad_gate, gate, preferred_element_type=F32) + jnp.dot(
        grad_up, up, preferred_element_type=F32
    )
    return act, grad_gate, grad_up, partial.astype(BF16)


VMEM_LIMIT = 20 * 1024 * 1024
VMEM_ALL = 60 * 1024 * 1024


def unit_tiles(units):
    return [(start, min(256, units - start)) for start in range(0, units, 256)]


def layer_kernel(rows, cots, gate, up, down, down_turned, turned, partials, col, ready=None):
    units, width = gate.shape
    for t, (start, size) in enumerate(unit_tiles(units)):
        if ready is not None:
            ready(t)
        gate_pre, up_pre = [
            lax.dot_general(w[start : start + size], rows, CONTRACT, preferred_element_type=F32)
            for w in (gate, up)
        ]
        if down_turned:
            grad_act = jnp.dot(
                cots, down[:, start : start + size], preferred_element_type=F32
            ).T
        else:
            grad_act = lax.dot_general(
                down[start : start + size], cots, CONTRACT, preferred_element_type=F32
            )
        for i, value in enumerate(swiglu_backward(gate_pre, up_pre, grad_act)):
            turned[i, start : start + size] = value
    grads = [turned[1].T, turned[2].T]
    for j in range(0, width, col):
        made = (
            jnp.dot(grads[0], gate[:, j : j + col], preferred_element_type=F32)
            + jnp.dot(grads[1], up[:, j : j + col], preferred_element_type=F32)
        ).astype(BF16)
        begin = 0
        for partial in partials:
            end = begin + partial.shape[0]
            partial[:, j : j + col] = made[begin:end]
            begin = end


def dense_block(core, blocks, gate, up, down):
    tok, width = blocks[0].shape[1] * len(blocks), blocks[0].shape[2]
    units = gate.shape[0]
    half = units // 2
    tiles = unit_tiles(units)

    def kernel(core_ref, *refs):
        ins, refs = refs[: len(blocks)], refs[len(blocks) :]
        gate, up, down, own, other = refs[:5]
        partials, (gate_in, up_in, down_in, turned, sems) = refs[5:-5], refs[-5:]
        copies = [
            [
                pltpu.make_async_copy(
                    source.at[pl.ds(start, size)], target.at[pl.ds(start, size)], sems.at[w, t]
                )
                for w, (source, target) in enumerate(((gate, gate_in), (up, up_in)))
            ]
            for t, (start, size) in enumerate(tiles)
        ]
        copies[0].append(pltpu.make_async_copy(down, down_in, sems.at[2, 0]))
        for group in copies:
            for copy in group:
                copy.start()

        def ready(t):
            for copy in copies[t]:
                copy.wait()

        rows, cots = [
            ins[0][k]
            if len(ins) == 1
            else jnp.concatenate([ref[k] for ref in ins], axis=0)
            for k in range(2)
        ]
        layer_kernel(rows, cots, gate_in, up_in, down_in, True, turned, partials, 512, ready)
        mine = core_ref[0]
        own[...] = turned[:, pl.ds(pl.multiple_of(mine * half, 16), half), :]
        other[...] = turned[:, pl.ds(pl.multiple_of((1 - mine) * half, 16), half), :]

    vmem = pl.BlockSpec(memory_space=pltpu.VMEM)
    hbm = pl.BlockSpec(memory_space=pl.ANY)
    return pl.pallas_call(
        kernel,
        in_specs=[pl.BlockSpec(memory_space=pltpu.SMEM)] + [vmem] * len(blocks) + [hbm] * 3,
        out_specs=[vmem] * (2 + len(blocks)),
        out_shape=[
            jax.ShapeDtypeStruct((3, half, tok), BF16),
            jax.ShapeDtypeStruct((3, half, tok), BF16),
            *[jax.ShapeDtypeStruct(b.shape[1:], BF16) for b in blocks],
        ],
        scratch_shapes=[
            pltpu.VMEM((units, width), BF16),
            pltpu.VMEM((units, width), BF16),
            pltpu.VMEM((width, units), BF16),
            pltpu.VMEM((3, units, tok), BF16),
            pltpu.SemaphoreType.DMA((3, len(tiles))),
        ],
        compiler_params=pltpu.CompilerParams(vmem_limit_bytes=VMEM_ALL),
        cost_estimate=pl.CostEstimate(
            flops=10 * units * width * tok,
            bytes_accessed=6 * units * width + 6 * tok * (width + units),
            transcendentals=units * tok,
        ),
        name="dense_block",
    )(core.reshape(1), *blocks, gate, up, down)


def expert_block(slots, gate, up, down):
    devices, _, per_device, width = slots.shape
    tok = devices * per_device
    units = gate.shape[0]
    col = 512
    tiles = unit_tiles(units)

    def kernel(
        slots, gate, up, down, g_gate, g_up, g_down, partial, loaded, turned, made, sems, out_sems
    ):
        rows, cots = [
            jnp.concatenate([slots[i, k] for i in range(devices)], axis=0) for k in range(2)
        ]
        copies = [
            [
                pltpu.make_async_copy(
                    source.at[pl.ds(start, size)], loaded.at[w, pl.ds(start, size)], sems.at[w, t]
                )
                for w, source in enumerate((gate, up, down))
            ]
            for t, (start, size) in enumerate(tiles)
        ]
        for group in copies:
            for copy in group:
                copy.start()

        def ready(t):
            for copy in copies[t]:
                copy.wait()

        layer_kernel(
            rows, cots, *[loaded.at[w] for w in range(3)], False, turned, (partial,), 512, ready
        )
        outs = (g_down, g_gate, g_up)
        pending = [None, None]
        step = 0
        for i in range(3):
            right = cots if i == 0 else rows
            for j in range(0, width, col):
                slot = step % 2
                if pending[slot] is not None:
                    pending[slot].wait()
                made[slot] = jnp.dot(
                    turned[i], right[:, j : j + col], preferred_element_type=F32
                ).astype(BF16)
                copy = pltpu.make_async_copy(
                    made.at[slot], outs[i].at[:, pl.ds(j, col)], out_sems.at[slot]
                )
                copy.start()
                pending[slot] = copy
                step += 1
        for copy in pending:
            copy.wait()

    vmem = pl.BlockSpec(memory_space=pltpu.VMEM)
    hbm = pl.BlockSpec(memory_space=pl.ANY)
    grad = jax.ShapeDtypeStruct((units, width), BF16)
    return pl.pallas_call(
        kernel,
        in_specs=[vmem, hbm, hbm, hbm],
        out_specs=[hbm, hbm, hbm, vmem],
        out_shape=[grad, grad, grad, jax.ShapeDtypeStruct((tok, width), BF16)],
        scratch_shapes=[
            pltpu.VMEM((3, units, width), BF16),
            pltpu.VMEM((3, units, tok), BF16),
            pltpu.VMEM((2, units, col), BF16),
            pltpu.SemaphoreType.DMA((3, len(tiles))),
            pltpu.SemaphoreType.DMA((2,)),
        ],
        compiler_params=pltpu.CompilerParams(vmem_limit_bytes=VMEM_ALL),
        cost_estimate=pl.CostEstimate(flops=1, bytes_accessed=1, transcendentals=0),
        name="expert_block",
    )(slots, gate, up, down)


def final_sum(core, lows, highs):
    cut, width = lows[2].shape[1:]
    units = cut + highs[2].shape[1]
    half = width // 2

    def kernel(core_ref, *refs):
        ins, (mine, other) = refs[:-2], refs[-2:]
        own_first = core_ref[0] == 0
        for i in range(3):
            for begin, (own, near, far) in ((0, ins[:3]), (cut, ins[3:])):
                total = own[i, :, width:].astype(F32) + near[i, :, width:].astype(F32)
                total = total + far[i].astype(F32)
                left, right = total[:, :half].astype(BF16), total[:, half:].astype(BF16)
                size = total.shape[0]
                mine[i, begin : begin + size] = jnp.where(own_first, left, right)
                other[i, begin : begin + size] = jnp.where(own_first, right, left)

    vmem = pl.BlockSpec(memory_space=pltpu.VMEM)
    shape = jax.ShapeDtypeStruct((3, units, half), BF16)
    return pl.pallas_call(
        kernel,
        in_specs=[pl.BlockSpec(memory_space=pltpu.SMEM)] + [vmem] * 6,
        out_specs=[vmem, vmem],
        out_shape=[shape, shape],
        compiler_params=pltpu.CompilerParams(vmem_limit_bytes=VMEM_LIMIT),
        cost_estimate=pl.CostEstimate(
            flops=9 * units * width,
            bytes_accessed=24 * units * width,
            transcendentals=0,
        ),
        name="final_sum",
    )(core.reshape(1), *lows, *highs)


def join_halves(core, mine, other):
    _, units, width = mine.shape

    def kernel(core_ref, mine, other, *outs):
        first = core_ref[0] == 0
        for i in range(3):
            a, b = mine[i], other[i]
            joined = jnp.concatenate([jnp.where(first, a, b), jnp.where(first, b, a)], axis=0)
            outs[i][...] = joined.T

    vmem = pl.BlockSpec(memory_space=pltpu.VMEM)
    grads = pl.pallas_call(
        kernel,
        in_specs=[pl.BlockSpec(memory_space=pltpu.SMEM), vmem, vmem],
        out_specs=[vmem] * 3,
        out_shape=[jax.ShapeDtypeStruct((width, 2 * units), BF16)] * 3,
        compiler_params=pltpu.CompilerParams(vmem_limit_bytes=VMEM_ALL),
        cost_estimate=pl.CostEstimate(
            flops=0, bytes_accessed=24 * units * width, transcendentals=0
        ),
        name="join_halves",
    )(core.reshape(1), mine, other)
    return [grad.T for grad in grads]


def weight_terms(tiles, acts, blocks, width, begin, end):
    units = acts[0].shape[1]
    tokens = sum(b.shape[1] for b in blocks)
    size = end - begin

    def kernel(tile_ref, *refs):
        a, b, out = refs[: len(acts)], refs[len(acts) : -1], refs[-1]
        rows = jnp.concatenate([ref[0] for ref in b], axis=0)
        cots = jnp.concatenate([ref[1] for ref in b], axis=0)
        for i in range(3):
            left = jnp.concatenate([ref[i, begin:end] for ref in a], axis=1)
            out[i] = jnp.dot(
                left, cots if i == 0 else rows, preferred_element_type=F32
            ).astype(BF16)

    def whole(shape):
        return pl.BlockSpec(shape, lambda j, tile_ref: (0, 0, 0))

    def columns(block):
        return pl.BlockSpec((*block.shape[:2], width), lambda j, tile_ref: (0, 0, tile_ref[j]))

    return pl.pallas_call(
        kernel,
        grid_spec=pltpu.PrefetchScalarGridSpec(
            num_scalar_prefetch=1,
            grid=(2,),
            in_specs=[whole(a.shape) for a in acts] + [columns(b) for b in blocks],
            out_specs=pl.BlockSpec((3, size, width), lambda j, tile_ref: (0, 0, j)),
        ),
        out_shape=jax.ShapeDtypeStruct((3, size, 2 * width), BF16),
        compiler_params=pltpu.CompilerParams(vmem_limit_bytes=VMEM_ALL),
        cost_estimate=pl.CostEstimate(
            flops=12 * size * tokens * width,
            bytes_accessed=2 * (tokens * (4 * width + 3 * units) + 6 * size * width),
            transcendentals=0,
        ),
        name="weight_terms",
    )(tiles, *acts, *blocks)


def routed_rows(hidden_in, cotangent, routes, gate_values, experts):
    tok, width = hidden_in.shape
    count = experts * 2 * CAP

    def kernel(rows, cots, routes, gates, out):
        line = lax.broadcasted_iota(jnp.int32, (count, tok), 0)
        expert, slot = line // (2 * CAP), lax.rem(line, CAP)
        first, second = routes[0:1] == expert, routes[1:2] == expert
        named = jnp.where(first | second, 1.0, 0.0)
        earlier = lax.broadcasted_iota(jnp.int32, (tok, tok), 0) < lax.broadcasted_iota(
            jnp.int32, (tok, tok), 1
        )
        before = jnp.dot(
            named.astype(BF16),
            jnp.where(earlier, 1.0, 0.0).astype(BF16),
            preferred_element_type=F32,
        )
        taken = jnp.where(before == slot.astype(F32), named, 0.0)
        weight = jnp.where(first, gates[0:1], 0.0) + jnp.where(second, gates[1:2], 0.0)
        weight = jnp.sum(taken * weight, axis=1, keepdims=True)
        taken = taken.astype(BF16)
        kept = lax.broadcasted_iota(jnp.int32, (count, 1), 0)
        is_cot = lax.rem(kept, 2 * CAP) >= CAP
        for j in range(0, width, 512):
            columns = slice(j, j + 512)
            row_part = jnp.dot(taken, rows[:, columns], preferred_element_type=F32)
            cot_part = jnp.dot(taken, cots[:, columns], preferred_element_type=F32) * weight
            out[:, columns] = jnp.where(is_cot, cot_part, row_part).astype(BF16)

    vmem = pl.BlockSpec(memory_space=pltpu.VMEM)
    return pl.pallas_call(
        kernel,
        in_specs=[vmem] * 4,
        out_specs=vmem,
        out_shape=jax.ShapeDtypeStruct((count, width), BF16),
        compiler_params=pltpu.CompilerParams(vmem_limit_bytes=VMEM_LIMIT),
        cost_estimate=pl.CostEstimate(
            flops=4 * count * tok * width, bytes_accessed=4 * tok * width, transcendentals=0
        ),
        name="routed_rows",
    )(hidden_in, cotangent, routes.T, gate_values.T)


def together(*values):
    return lax.optimization_barrier(values)


def line_body(
    hidden_in,
    cotangent,
    routes,
    gate_values,
    dense_gate,
    dense_up,
    dense_down,
    expert_gate,
    expert_up,
    expert_down,
):
    experts = lax.axis_size("tp")
    me = lax.axis_index("tp")
    ep = lax.axis_index("ep")
    core, chip = lax.rem(ep, 2), lax.div(ep, 2)
    half = dense_gate.shape[0] // 2
    columns = dense_down.shape[1]
    down = lax.all_gather(dense_down.T, "ep", axis=0, tiled=True)

    def pairs(value):
        return lax.ppermute(value, "tp", [(0, 1), (1, 0), (2, 3), (3, 2)])

    def mirror(value):
        return lax.ppermute(value, "tp", [(0, 3), (1, 2), (2, 1), (3, 0)])

    def across(value, apart):
        return lax.ppermute(value, "ep", [(i, i ^ apart) for i in range(8)])

    def add(a, b):
        return (a.astype(F32) + b.astype(F32)).astype(BF16)

    def dense(blocks):
        mine, other, *partials = dense_block(core, blocks, dense_gate, dense_up, down)
        tokens = [*blocks, *(across(b, 1) for b in blocks)]
        return ([mine, across(other, 1)], tokens), partials

    own = jnp.stack([hidden_in, cotangent])
    mirrored, paired = mirror(own), pairs(own)
    sent = routed_rows(hidden_in, cotangent, routes, gate_values, experts)
    got = lax.all_to_all(sent, "tp", split_axis=0, concat_axis=0, tiled=True)
    got = got.reshape(experts, 2, CAP, -1).transpose(1, 0, 2, 3).reshape(2, experts * CAP, -1)
    dispatch, _ = slot_tables(routes, gate_values, me, experts)
    x_chip, y_chip, xy_chip = [jnp.bitwise_xor(chip, k) for k in (1, 2, 3)]
    chip_tiles = [
        jnp.stack(t)
        for t in ((xy_chip, x_chip), (xy_chip, y_chip), (y_chip, chip), (x_chip, chip))
    ]
    both0, (partial0,) = dense([own])
    got, partial0, both0, dispatch, chip_tiles = together(
        got, partial0, both0, dispatch, chip_tiles
    )

    mirrored, paired, got = together(mirrored, paired, got)
    last = pairs(mirrored)
    slots = lax.all_gather(got, "ep", axis=0, tiled=False)
    both12, (paired_partial, mirrored_partial) = dense([paired, mirrored])
    slots, both12, paired_partial, mirrored_partial = together(
        slots, both12, paired_partial, mirrored_partial
    )
    g_gate, g_up, g_down, slot_terms = expert_block(
        slots, expert_gate[0], expert_up[0], expert_down[0]
    )

    last, both12, slot_terms = together(last, both12, slot_terms)
    routed = lax.psum_scatter(slot_terms, "ep", scatter_dimension=0, tiled=True)
    both3, (partial3,) = dense([last])
    from_last = pairs(partial3)

    acts, tokens = (a + b + c for a, b, c in zip(both0, both12, both3))
    cut, width = -(-half // 32) * 16, 2 * columns
    low_sent = weight_terms(chip_tiles[0], acts, tokens, width, 0, cut)
    high_sent = weight_terms(chip_tiles[1], acts, tokens, width, cut, half)
    high_sent, chip_tiles, from_last = together(high_sent, chip_tiles, from_last)
    low_kept = weight_terms(chip_tiles[2], acts, tokens, width, 0, cut)
    high_kept = weight_terms(chip_tiles[3], acts, tokens, width, cut, half)
    low_near, high_near = across(low_sent, 2), across(high_sent, 4)
    from_pair = pairs(paired_partial)
    low_kept, high_kept, from_pair, routed = together(low_kept, high_kept, from_pair, routed)
    from_mirror = mirror(add(mirrored_partial, from_last))
    low_near, high_near, low_kept, high_kept = together(
        low_near, high_near, low_kept, high_kept
    )
    low_far = across(add(low_kept[:, :, :width], low_near[:, :, :width]), 4)
    high_far = across(add(high_kept[:, :, :width], high_near[:, :, :width]), 2)
    low_far, high_far, from_mirror = together(low_far, high_far, from_mirror)
    mine, other = final_sum(
        core, (low_kept, low_near, low_far), (high_kept, high_near, high_far)
    )
    mine, routed = together(mine, routed)
    routed_input = to_tokens(slots_back(routed, experts), dispatch, me, experts)
    grads = join_halves(core, mine, across(other, 1))
    grad_input = (
        partial0.astype(F32)
        + from_pair.astype(F32)
        + from_mirror.astype(F32)
        + routed_input
    ).astype(BF16)
    return (grad_input, grads[1], grads[2], grads[0], g_gate[None], g_up[None], g_down[None])


def general_body(
    hidden_in,
    cotangent,
    routes,
    gate_values,
    dense_gate,
    dense_up,
    dense_down,
    expert_gate,
    expert_up,
    expert_down,
):
    experts = lax.axis_size("tp")
    me = lax.axis_index("tp")
    dispatch, weight = slot_tables(routes, gate_values, me, experts)
    sent = slots_to_send(hidden_in, cotangent, dispatch, weight, experts)
    got = exchange_slots(sent, me, experts)
    slots = lax.all_gather(got, "ep", axis=0, tiled=False)
    slot_rows, slot_cot = slots[:, 0].reshape(-1, hidden_in.shape[1]), slots[:, 1].reshape(
        -1, hidden_in.shape[1]
    )
    rows = lax.all_gather(hidden_in, "tp", axis=0, tiled=True)
    cots = lax.all_gather(cotangent, "tp", axis=0, tiled=True)
    down = lax.all_gather(dense_down, "ep", axis=1, tiled=True)
    act, grad_gate, grad_up, partial = plain_block(rows, cots, dense_gate, dense_up, down)
    dense_input = lax.psum_scatter(partial, "tp", scatter_dimension=0, tiled=True)
    grads = [
        lax.psum_scatter(
            lax.dot_general(a, b, LEADING, preferred_element_type=F32).astype(BF16),
            "ep",
            scatter_dimension=1,
            tiled=True,
        )
        for a, b in ((act, cots), (grad_gate, rows), (grad_up, rows))
    ]
    g_gate, g_up, g_down, slot_terms = expert_layer(
        slot_rows, slot_cot, expert_gate[0], expert_up[0], expert_down[0]
    )
    routed = lax.psum_scatter(slot_terms, "ep", scatter_dimension=0, tiled=True)
    routed_input = to_tokens(slots_back(routed, experts), dispatch, me, experts)
    grad_input = (dense_input.astype(F32) + routed_input).astype(BF16)
    return (grad_input, grads[1], grads[2], grads[0], g_gate[None], g_up[None], g_down[None])


def solution(mesh):
    placed = (
        P(("ep", "tp"), None),
        P(("ep", "tp"), None),
        P(("ep", "tp"), None),
        P(("ep", "tp"), None),
        P("tp", None),
        P("tp", None),
        P("tp", "ep"),
        P("tp", "ep", None),
        P("tp", "ep", None),
        P("tp", "ep", None),
    )
    in_line = mesh.shape["tp"] == 4 and mesh.shape["ep"] == 8
    return jax.shard_map(
        line_body if in_line else general_body,
        mesh=mesh,
        in_specs=placed,
        out_specs=(
            P(("ep", "tp"), None),
            P("tp", "ep"),
            P("tp", "ep"),
            P("tp", "ep"),
            P("tp", "ep", None),
            P("tp", "ep", None),
            P("tp", "ep", None),
        ),
        check_vma=False,
    )
```

```python
import jax
import jax.numpy as jnp
from jax import lax
from jax.experimental import pallas as pl
from jax.experimental.pallas import tpu as pltpu
from jax.sharding import PartitionSpec as P

CAP = 4
CONTRACT = (((1,), (1,)), ((), ()))
LEADING = (((0,), (0,)), ((), ()))
F32 = jnp.float32
BF16 = jnp.bfloat16


def swiglu_backward(gate_pre, up_pre, grad_act):
    sigmoid_gate = jax.nn.sigmoid(gate_pre)
    silu_gate = gate_pre * sigmoid_gate
    act = (silu_gate * up_pre).astype(BF16)
    silu_slope = sigmoid_gate * (1.0 + gate_pre * (1.0 - sigmoid_gate))
    grad_gate = (grad_act * up_pre * silu_slope).astype(BF16)
    grad_up = (grad_act * silu_gate).astype(BF16)
    return act, grad_gate, grad_up


def slot_tables(routes, gate_values, me, experts):
    tok_count = routes.shape[0]
    named = lax.rem(me + jnp.arange(experts, dtype=jnp.int32), experts)
    onehot = (routes.reshape(-1)[:, None] == named[None, :]).astype(jnp.int32)
    before = jnp.cumsum(onehot, axis=0) - onehot
    slot = onehot[:, :, None] * (before[:, :, None] == jnp.arange(CAP, dtype=jnp.int32)).astype(
        jnp.int32
    )
    slot = slot.reshape(tok_count, 2, experts * CAP).astype(F32)
    dispatch = jnp.sum(slot, axis=1).T.astype(BF16)
    weight = jnp.sum(slot * gate_values[:, :, None], axis=(0, 1))
    return dispatch, weight


def shift(x, axis, size, by):
    return lax.ppermute(x, axis, [(i, (i + by) % size) for i in range(size)])


def slots_to_send(hidden_in, cotangent, dispatch, weight, experts):
    width = hidden_in.shape[1]
    rows = jnp.dot(dispatch, hidden_in, preferred_element_type=F32).astype(BF16)
    cots = jnp.dot(dispatch, cotangent, preferred_element_type=F32)
    cots = (cots * weight[:, None]).astype(BF16)
    return jnp.stack(
        [rows.reshape(experts, CAP, width), cots.reshape(experts, CAP, width)], axis=1
    )


def exchange_slots(sent, me, experts):
    width = sent.shape[3]
    sent = jnp.roll(sent, me, axis=0)
    got = lax.all_to_all(sent, "tp", split_axis=0, concat_axis=0, tiled=True)
    return got.transpose(1, 0, 2, 3).reshape(2, experts * CAP, width)


def expert_layer(slot_rows, slot_cot, gate_weight, up_weight, down_weight):
    e_gate = lax.dot_general(slot_rows, gate_weight, CONTRACT, preferred_element_type=F32)
    e_up = lax.dot_general(slot_rows, up_weight, CONTRACT, preferred_element_type=F32)
    e_grad_act = lax.dot_general(slot_cot, down_weight, CONTRACT, preferred_element_type=F32)
    e_act, e_grad_gate, e_grad_up = swiglu_backward(e_gate, e_up, e_grad_act)
    g_down = lax.dot_general(e_act, slot_cot, LEADING, preferred_element_type=F32).astype(BF16)
    g_gate = lax.dot_general(e_grad_gate, slot_rows, LEADING, preferred_element_type=F32).astype(
        BF16
    )
    g_up = lax.dot_general(e_grad_up, slot_rows, LEADING, preferred_element_type=F32).astype(BF16)
    terms = jnp.dot(e_grad_gate, gate_weight, preferred_element_type=F32) + jnp.dot(
        e_grad_up, up_weight, preferred_element_type=F32
    )
    return g_gate, g_up, g_down, terms.astype(BF16)


def slots_back(own, experts):
    own = own.reshape(experts, CAP, own.shape[1])
    return lax.all_to_all(own, "tp", split_axis=0, concat_axis=0, tiled=True)


def to_tokens(back, dispatch, me, experts):
    dispatch = jnp.roll(dispatch.reshape(experts, CAP, -1), me, axis=0)
    return lax.dot_general(
        dispatch.reshape(experts * CAP, -1),
        back.reshape(experts * CAP, -1),
        LEADING,
        preferred_element_type=F32,
    )


def plain_block(rows, cot, gate, up, down):
    gate_pre = lax.dot_general(rows, gate, CONTRACT, preferred_element_type=F32)
    up_pre = lax.dot_general(rows, up, CONTRACT, preferred_element_type=F32)
    grad_act = lax.dot_general(cot, down, CONTRACT, preferred_element_type=F32)
    act, grad_gate, grad_up = swiglu_backward(gate_pre, up_pre, grad_act)
    partial = jnp.dot(grad_gate, gate, preferred_element_type=F32) + jnp.dot(
        grad_up, up, preferred_element_type=F32
    )
    return act, grad_gate, grad_up, partial.astype(BF16)


VMEM_LIMIT = 20 * 1024 * 1024
VMEM_ALL = 60 * 1024 * 1024


def unit_tiles(units):
    return [(start, min(256, units - start)) for start in range(0, units, 256)]


def layer_kernel(rows, cots, gate, up, down, down_turned, turned, partials, col, ready=None):
    units, width = gate.shape
    for t, (start, size) in enumerate(unit_tiles(units)):
        if ready is not None:
            ready(t)
        gate_pre, up_pre = [
            lax.dot_general(w[start : start + size], rows, CONTRACT, preferred_element_type=F32)
            for w in (gate, up)
        ]
        if down_turned:
            grad_act = jnp.dot(
                cots, down[:, start : start + size], preferred_element_type=F32
            ).T
        else:
            grad_act = lax.dot_general(
                down[start : start + size], cots, CONTRACT, preferred_element_type=F32
            )
        for i, value in enumerate(swiglu_backward(gate_pre, up_pre, grad_act)):
            turned[i, start : start + size] = value
    grads = [turned[1].T, turned[2].T]
    for j in range(0, width, col):
        made = (
            jnp.dot(grads[0], gate[:, j : j + col], preferred_element_type=F32)
            + jnp.dot(grads[1], up[:, j : j + col], preferred_element_type=F32)
        ).astype(BF16)
        begin = 0
        for partial in partials:
            end = begin + partial.shape[0]
            partial[:, j : j + col] = made[begin:end]
            begin = end


def dense_block(core, blocks, gate, up, down):
    tok, width = blocks[0].shape[1] * len(blocks), blocks[0].shape[2]
    units = gate.shape[0]
    half = units // 2
    tiles = unit_tiles(units)

    def kernel(core_ref, *refs):
        ins, refs = refs[: len(blocks)], refs[len(blocks) :]
        gate, up, down, own, other = refs[:5]
        partials, (gate_in, up_in, down_in, turned, sems) = refs[5:-5], refs[-5:]
        copies = [
            [
                pltpu.make_async_copy(
                    source.at[pl.ds(start, size)], target.at[pl.ds(start, size)], sems.at[w, t]
                )
                for w, (source, target) in enumerate(((gate, gate_in), (up, up_in)))
            ]
            for t, (start, size) in enumerate(tiles)
        ]
        copies[0].append(pltpu.make_async_copy(down, down_in, sems.at[2, 0]))
        for group in copies:
            for copy in group:
                copy.start()

        def ready(t):
            for copy in copies[t]:
                copy.wait()

        rows, cots = [
            ins[0][k]
            if len(ins) == 1
            else jnp.concatenate([ref[k] for ref in ins], axis=0)
            for k in range(2)
        ]
        layer_kernel(rows, cots, gate_in, up_in, down_in, True, turned, partials, 512, ready)
        mine = core_ref[0]
        own[...] = turned[:, pl.ds(pl.multiple_of(mine * half, 16), half), :]
        other[...] = turned[:, pl.ds(pl.multiple_of((1 - mine) * half, 16), half), :]

    vmem = pl.BlockSpec(memory_space=pltpu.VMEM)
    hbm = pl.BlockSpec(memory_space=pl.ANY)
    return pl.pallas_call(
        kernel,
        in_specs=[pl.BlockSpec(memory_space=pltpu.SMEM)] + [vmem] * len(blocks) + [hbm] * 3,
        out_specs=[vmem] * (2 + len(blocks)),
        out_shape=[
            jax.ShapeDtypeStruct((3, half, tok), BF16),
            jax.ShapeDtypeStruct((3, half, tok), BF16),
            *[jax.ShapeDtypeStruct(b.shape[1:], BF16) for b in blocks],
        ],
        scratch_shapes=[
            pltpu.VMEM((units, width), BF16),
            pltpu.VMEM((units, width), BF16),
            pltpu.VMEM((width, units), BF16),
            pltpu.VMEM((3, units, tok), BF16),
            pltpu.SemaphoreType.DMA((3, len(tiles))),
        ],
        compiler_params=pltpu.CompilerParams(vmem_limit_bytes=VMEM_ALL),
        cost_estimate=pl.CostEstimate(
            flops=10 * units * width * tok,
            bytes_accessed=6 * units * width + 6 * tok * (width + units),
            transcendentals=units * tok,
        ),
        name="dense_block",
    )(core.reshape(1), *blocks, gate, up, down)


def expert_block(slots, gate, up, down):
    devices, _, per_device, width = slots.shape
    tok = devices * per_device
    units = gate.shape[0]
    col = 512
    tiles = unit_tiles(units)

    def kernel(
        slots, gate, up, down, g_gate, g_up, g_down, partial, loaded, turned, made, sems, out_sems
    ):
        rows, cots = [
            jnp.concatenate([slots[i, k] for i in range(devices)], axis=0) for k in range(2)
        ]
        copies = [
            [
                pltpu.make_async_copy(
                    source.at[pl.ds(start, size)], loaded.at[w, pl.ds(start, size)], sems.at[w, t]
                )
                for w, source in enumerate((gate, up, down))
            ]
            for t, (start, size) in enumerate(tiles)
        ]
        for group in copies:
            for copy in group:
                copy.start()

        def ready(t):
            for copy in copies[t]:
                copy.wait()

        layer_kernel(
            rows, cots, *[loaded.at[w] for w in range(3)], False, turned, (partial,), 512, ready
        )
        outs = (g_down, g_gate, g_up)
        pending = [None, None]
        step = 0
        for i in range(3):
            right = cots if i == 0 else rows
            for j in range(0, width, col):
                slot = step % 2
                if pending[slot] is not None:
                    pending[slot].wait()
                made[slot] = jnp.dot(
                    turned[i], right[:, j : j + col], preferred_element_type=F32
                ).astype(BF16)
                copy = pltpu.make_async_copy(
                    made.at[slot], outs[i].at[:, pl.ds(j, col)], out_sems.at[slot]
                )
                copy.start()
                pending[slot] = copy
                step += 1
        for copy in pending:
            copy.wait()

    vmem = pl.BlockSpec(memory_space=pltpu.VMEM)
    hbm = pl.BlockSpec(memory_space=pl.ANY)
    grad = jax.ShapeDtypeStruct((units, width), BF16)
    return pl.pallas_call(
        kernel,
        in_specs=[vmem, hbm, hbm, hbm],
        out_specs=[hbm, hbm, hbm, vmem],
        out_shape=[grad, grad, grad, jax.ShapeDtypeStruct((tok, width), BF16)],
        scratch_shapes=[
            pltpu.VMEM((3, units, width), BF16),
            pltpu.VMEM((3, units, tok), BF16),
            pltpu.VMEM((2, units, col), BF16),
            pltpu.SemaphoreType.DMA((3, len(tiles))),
            pltpu.SemaphoreType.DMA((2,)),
        ],
        compiler_params=pltpu.CompilerParams(vmem_limit_bytes=VMEM_ALL),
        cost_estimate=pl.CostEstimate(flops=1, bytes_accessed=1, transcendentals=0),
        name="expert_block",
    )(slots, gate, up, down)


def final_sum(core, lows, highs):
    cut, width = lows[2].shape[1:]
    units = cut + highs[2].shape[1]
    half = width // 2

    def kernel(core_ref, *refs):
        ins, (mine, other) = refs[:-2], refs[-2:]
        own_first = core_ref[0] == 0
        for i in range(3):
            for begin, (own, near, far) in ((0, ins[:3]), (cut, ins[3:])):
                total = own[i, :, width:].astype(F32) + near[i, :, width:].astype(F32)
                total = total + far[i].astype(F32)
                left, right = total[:, :half].astype(BF16), total[:, half:].astype(BF16)
                size = total.shape[0]
                mine[i, begin : begin + size] = jnp.where(own_first, left, right)
                other[i, begin : begin + size] = jnp.where(own_first, right, left)

    vmem = pl.BlockSpec(memory_space=pltpu.VMEM)
    shape = jax.ShapeDtypeStruct((3, units, half), BF16)
    return pl.pallas_call(
        kernel,
        in_specs=[pl.BlockSpec(memory_space=pltpu.SMEM)] + [vmem] * 6,
        out_specs=[vmem, vmem],
        out_shape=[shape, shape],
        compiler_params=pltpu.CompilerParams(vmem_limit_bytes=VMEM_LIMIT),
        cost_estimate=pl.CostEstimate(
            flops=9 * units * width,
            bytes_accessed=24 * units * width,
            transcendentals=0,
        ),
        name="final_sum",
    )(core.reshape(1), *lows, *highs)


def join_halves(core, mine, other):
    _, units, width = mine.shape

    def kernel(core_ref, mine, other, *outs):
        first = core_ref[0] == 0
        for i in range(3):
            a, b = mine[i], other[i]
            joined = jnp.concatenate([jnp.where(first, a, b), jnp.where(first, b, a)], axis=0)
            outs[i][...] = joined.T

    vmem = pl.BlockSpec(memory_space=pltpu.VMEM)
    grads = pl.pallas_call(
        kernel,
        in_specs=[pl.BlockSpec(memory_space=pltpu.SMEM), vmem, vmem],
        out_specs=[vmem] * 3,
        out_shape=[jax.ShapeDtypeStruct((width, 2 * units), BF16)] * 3,
        compiler_params=pltpu.CompilerParams(vmem_limit_bytes=VMEM_ALL),
        cost_estimate=pl.CostEstimate(
            flops=0, bytes_accessed=24 * units * width, transcendentals=0
        ),
        name="join_halves",
    )(core.reshape(1), mine, other)
    return [grad.T for grad in grads]


def weight_terms(tiles, acts, blocks, width, begin, end):
    units = acts[0].shape[1]
    tokens = sum(b.shape[1] for b in blocks)
    size = end - begin

    def kernel(tile_ref, *refs):
        a, b, out = refs[: len(acts)], refs[len(acts) : -1], refs[-1]
        rows = jnp.concatenate([ref[0] for ref in b], axis=0)
        cots = jnp.concatenate([ref[1] for ref in b], axis=0)
        for i in range(3):
            left = jnp.concatenate([ref[i, begin:end] for ref in a], axis=1)
            out[i] = jnp.dot(
                left, cots if i == 0 else rows, preferred_element_type=F32
            ).astype(BF16)

    def whole(shape):
        return pl.BlockSpec(shape, lambda j, tile_ref: (0, 0, 0))

    def columns(block):
        return pl.BlockSpec((*block.shape[:2], width), lambda j, tile_ref: (0, 0, tile_ref[j]))

    return pl.pallas_call(
        kernel,
        grid_spec=pltpu.PrefetchScalarGridSpec(
            num_scalar_prefetch=1,
            grid=(2,),
            in_specs=[whole(a.shape) for a in acts] + [columns(b) for b in blocks],
            out_specs=pl.BlockSpec((3, size, width), lambda j, tile_ref: (0, 0, j)),
        ),
        out_shape=jax.ShapeDtypeStruct((3, size, 2 * width), BF16),
        compiler_params=pltpu.CompilerParams(vmem_limit_bytes=VMEM_ALL),
        cost_estimate=pl.CostEstimate(
            flops=12 * size * tokens * width,
            bytes_accessed=2 * (tokens * (4 * width + 3 * units) + 6 * size * width),
            transcendentals=0,
        ),
        name="weight_terms",
    )(tiles, *acts, *blocks)


def routed_rows(hidden_in, cotangent, routes, gate_values, experts):
    tok, width = hidden_in.shape
    count = experts * 2 * CAP

    def kernel(rows, cots, routes, gates, out):
        line = lax.broadcasted_iota(jnp.int32, (count, tok), 0)
        expert, slot = line // (2 * CAP), lax.rem(line, CAP)
        first, second = routes[0:1] == expert, routes[1:2] == expert
        named = jnp.where(first | second, 1.0, 0.0)
        earlier = lax.broadcasted_iota(jnp.int32, (tok, tok), 0) < lax.broadcasted_iota(
            jnp.int32, (tok, tok), 1
        )
        before = jnp.dot(
            named.astype(BF16),
            jnp.where(earlier, 1.0, 0.0).astype(BF16),
            preferred_element_type=F32,
        )
        taken = jnp.where(before == slot.astype(F32), named, 0.0)
        weight = jnp.where(first, gates[0:1], 0.0) + jnp.where(second, gates[1:2], 0.0)
        weight = jnp.sum(taken * weight, axis=1, keepdims=True)
        taken = taken.astype(BF16)
        kept = lax.broadcasted_iota(jnp.int32, (count, 1), 0)
        is_cot = lax.rem(kept, 2 * CAP) >= CAP
        for j in range(0, width, 512):
            columns = slice(j, j + 512)
            row_part = jnp.dot(taken, rows[:, columns], preferred_element_type=F32)
            cot_part = jnp.dot(taken, cots[:, columns], preferred_element_type=F32) * weight
            out[:, columns] = jnp.where(is_cot, cot_part, row_part).astype(BF16)

    vmem = pl.BlockSpec(memory_space=pltpu.VMEM)
    return pl.pallas_call(
        kernel,
        in_specs=[vmem] * 4,
        out_specs=vmem,
        out_shape=jax.ShapeDtypeStruct((count, width), BF16),
        compiler_params=pltpu.CompilerParams(vmem_limit_bytes=VMEM_LIMIT),
        cost_estimate=pl.CostEstimate(
            flops=4 * count * tok * width, bytes_accessed=4 * tok * width, transcendentals=0
        ),
        name="routed_rows",
    )(hidden_in, cotangent, routes.T, gate_values.T)


def together(*values):
    return lax.optimization_barrier(values)


def line_body(
    hidden_in,
    cotangent,
    routes,
    gate_values,
    dense_gate,
    dense_up,
    dense_down,
    expert_gate,
    expert_up,
    expert_down,
):
    experts = lax.axis_size("tp")
    me = lax.axis_index("tp")
    ep = lax.axis_index("ep")
    core, chip = lax.rem(ep, 2), lax.div(ep, 2)
    half = dense_gate.shape[0] // 2
    columns = dense_down.shape[1]
    down = lax.all_gather(dense_down.T, "ep", axis=0, tiled=True)

    def pairs(value):
        return lax.ppermute(value, "tp", [(0, 1), (1, 0), (2, 3), (3, 2)])

    def mirror(value):
        return lax.ppermute(value, "tp", [(0, 3), (1, 2), (2, 1), (3, 0)])

    def across(value, apart):
        return lax.ppermute(value, "ep", [(i, i ^ apart) for i in range(8)])

    def add(a, b):
        return (a.astype(F32) + b.astype(F32)).astype(BF16)

    def dense(blocks):
        mine, other, *partials = dense_block(core, blocks, dense_gate, dense_up, down)
        tokens = [*blocks, *(across(b, 1) for b in blocks)]
        return ([mine, across(other, 1)], tokens), partials

    own = jnp.stack([hidden_in, cotangent])
    mirrored, paired = mirror(own), pairs(own)
    sent = routed_rows(hidden_in, cotangent, routes, gate_values, experts)
    got = lax.all_to_all(sent, "tp", split_axis=0, concat_axis=0, tiled=True)
    got = got.reshape(experts, 2, CAP, -1).transpose(1, 0, 2, 3).reshape(2, experts * CAP, -1)
    dispatch, _ = slot_tables(routes, gate_values, me, experts)
    x_chip, y_chip, xy_chip = [jnp.bitwise_xor(chip, k) for k in (1, 2, 3)]
    chip_tiles = [
        jnp.stack(t)
        for t in ((xy_chip, x_chip), (xy_chip, y_chip), (y_chip, chip), (x_chip, chip))
    ]
    both0, (partial0,) = dense([own])
    got, partial0, both0, dispatch, chip_tiles = together(
        got, partial0, both0, dispatch, chip_tiles
    )

    mirrored, paired, got = together(mirrored, paired, got)
    last = pairs(mirrored)
    slots = lax.all_gather(got, "ep", axis=0, tiled=False)
    both12, (paired_partial, mirrored_partial) = dense([paired, mirrored])
    slots, both12, paired_partial, mirrored_partial = together(
        slots, both12, paired_partial, mirrored_partial
    )
    g_gate, g_up, g_down, slot_terms = expert_block(
        slots, expert_gate[0], expert_up[0], expert_down[0]
    )

    last, both12, slot_terms = together(last, both12, slot_terms)
    routed = lax.psum_scatter(slot_terms, "ep", scatter_dimension=0, tiled=True)
    both3, (partial3,) = dense([last])
    from_last = pairs(partial3)

    acts, tokens = (a + b + c for a, b, c in zip(both0, both12, both3))
    cut, width = -(-half // 32) * 16, 2 * columns
    low_sent = weight_terms(chip_tiles[0], acts, tokens, width, 0, cut)
    high_sent = weight_terms(chip_tiles[1], acts, tokens, width, cut, half)
    high_sent, chip_tiles, from_last = together(high_sent, chip_tiles, from_last)
    low_kept = weight_terms(chip_tiles[2], acts, tokens, width, 0, cut)
    high_kept = weight_terms(chip_tiles[3], acts, tokens, width, cut, half)
    low_near, high_near = across(low_sent, 2), across(high_sent, 4)
    from_mirror = mirror(add(mirrored_partial, from_last))
    paired_partial, routed = together(paired_partial, routed)
    from_pair = pairs(paired_partial)
    low_near, high_near, low_kept, high_kept = together(
        low_near, high_near, low_kept, high_kept
    )
    low_far = across(add(low_kept[:, :, :width], low_near[:, :, :width]), 4)
    high_far = across(add(high_kept[:, :, :width], high_near[:, :, :width]), 2)
    low_far, high_far, from_mirror = together(low_far, high_far, from_mirror)
    mine, other = final_sum(
        core, (low_kept, low_near, low_far), (high_kept, high_near, high_far)
    )
    mine, routed, from_pair = together(mine, routed, from_pair)
    routed_input = to_tokens(slots_back(routed, experts), dispatch, me, experts)
    grads = join_halves(core, mine, across(other, 1))
    grad_input = (
        partial0.astype(F32)
        + from_pair.astype(F32)
        + from_mirror.astype(F32)
        + routed_input
    ).astype(BF16)
    return (grad_input, grads[1], grads[2], grads[0], g_gate[None], g_up[None], g_down[None])


def general_body(
    hidden_in,
    cotangent,
    routes,
    gate_values,
    dense_gate,
    dense_up,
    dense_down,
    expert_gate,
    expert_up,
    expert_down,
):
    experts = lax.axis_size("tp")
    me = lax.axis_index("tp")
    dispatch, weight = slot_tables(routes, gate_values, me, experts)
    sent = slots_to_send(hidden_in, cotangent, dispatch, weight, experts)
    got = exchange_slots(sent, me, experts)
    slots = lax.all_gather(got, "ep", axis=0, tiled=False)
    slot_rows, slot_cot = slots[:, 0].reshape(-1, hidden_in.shape[1]), slots[:, 1].reshape(
        -1, hidden_in.shape[1]
    )
    rows = lax.all_gather(hidden_in, "tp", axis=0, tiled=True)
    cots = lax.all_gather(cotangent, "tp", axis=0, tiled=True)
    down = lax.all_gather(dense_down, "ep", axis=1, tiled=True)
    act, grad_gate, grad_up, partial = plain_block(rows, cots, dense_gate, dense_up, down)
    dense_input = lax.psum_scatter(partial, "tp", scatter_dimension=0, tiled=True)
    grads = [
        lax.psum_scatter(
            lax.dot_general(a, b, LEADING, preferred_element_type=F32).astype(BF16),
            "ep",
            scatter_dimension=1,
            tiled=True,
        )
        for a, b in ((act, cots), (grad_gate, rows), (grad_up, rows))
    ]
    g_gate, g_up, g_down, slot_terms = expert_layer(
        slot_rows, slot_cot, expert_gate[0], expert_up[0], expert_down[0]
    )
    routed = lax.psum_scatter(slot_terms, "ep", scatter_dimension=0, tiled=True)
    routed_input = to_tokens(slots_back(routed, experts), dispatch, me, experts)
    grad_input = (dense_input.astype(F32) + routed_input).astype(BF16)
    return (grad_input, grads[1], grads[2], grads[0], g_gate[None], g_up[None], g_down[None])


def solution(mesh):
    placed = (
        P(("ep", "tp"), None),
        P(("ep", "tp"), None),
        P(("ep", "tp"), None),
        P(("ep", "tp"), None),
        P("tp", None),
        P("tp", None),
        P("tp", "ep"),
        P("tp", "ep", None),
        P("tp", "ep", None),
        P("tp", "ep", None),
    )
    in_line = mesh.shape["tp"] == 4 and mesh.shape["ep"] == 8
    return jax.shard_map(
        line_body if in_line else general_body,
        mesh=mesh,
        in_specs=placed,
        out_specs=(
            P(("ep", "tp"), None),
            P("tp", "ep"),
            P("tp", "ep"),
            P("tp", "ep"),
            P("tp", "ep", None),
            P("tp", "ep", None),
            P("tp", "ep", None),
        ),
        check_vma=False,
    )
```
